32 devices in a mesh: dp: 8 (over z, x), row: 2 (over y), col: 2 (over core).
Axes of the slice: x: 2, y: 2, z: 4, core: 2. Of those that a mesh axis runs over, the one named last changes fastest.
Arguments:
- hidden: bfloat16 [2048, 1024], P('dp', ('row', 'col')), may hold values from -6 to 6
- segment_ids: int32 [8, 256], P('dp'), may hold values from 0 to 3, never falling along the last dimension, each value on 1 to 128 neighbouring positions
- norm1_gain: bfloat16 [1024], P('row'), may hold values from 0.5 to 1.5
- w_gate: bfloat16 [1024, 1536], P('row', 'col'), may hold values from -0.1875 to 0.1875
- w_xin: bfloat16 [1024, 1536], P('row', 'col'), may hold values from -0.1875 to 0.1875
- w_dt: bfloat16 [1024, 24], P('row', 'col'), may hold values from -0.1875 to 0.1875
- w_bc: bfloat16 [1024, 256], P('row'), may hold values from -0.1875 to 0.1875
- w_query: bfloat16 [1024, 512], P('row', 'col'), may hold values from -0.1875 to 0.1875
- w_kv: bfloat16 [1024, 2, 128], P('row', 'col'), may hold values from -0.1875 to 0.1875
- convx_weight: bfloat16 [1536, 4], P(('col', 'row')), may hold values from -3 to 3
- convx_bias: bfloat16 [1536], P(('col', 'row')), may hold values from -3 to 3
- convbc_weight: bfloat16 [256, 4], replicated, may hold values from -3 to 3
- convbc_bias: bfloat16 [256], replicated, may hold values from -3 to 3
- dt_bias: bfloat16 [24], P(('col', 'row')), may hold values from -3 to 0.5
- a_log: bfloat16 [24], P(('col', 'row')), may hold values from -4.5 to 0
- d_skip: bfloat16 [24], P(('col', 'row')), may hold values from 0.5 to 1.5
- w_mixout: bfloat16 [1536, 1024], P('col', 'row'), may hold values from -0.009765625 to 0.009765625
- w_attnout: bfloat16 [512, 1024], P('col', 'row'), may hold values from -2 to 2
- norm2_gain: bfloat16 [1024], P('row'), may hold values from 0.5 to 1.5
- w_gateup: bfloat16 [1024, 2, 2048], P('row', None, 'col'), may hold values from -0.1875 to 0.1875
- w_down: bfloat16 [2048, 1024], P('col', 'row'), may hold values from -0.125 to 0.125
- cotangent: bfloat16 [2048, 1024], P('dp', ('row', 'col')), may hold values from -6 to 6
Outputs:
- output: bfloat16 [2048, 1024], P('dp', ('row', 'col'))
- grad_hidden: float32 [2048, 1024], P('dp', ('row', 'col'))
- grad_norm1_gain: float32 [1024], P('row')
- grad_w_gate: float32 [1024, 1536], P(('row', 'dp'), 'col')
- grad_w_xin: float32 [1024, 1536], P(('row', 'dp'), 'col')
- grad_w_dt: float32 [1024, 24], P(('row', 'dp'), 'col')
- grad_w_bc: float32 [1024, 256], P(('row', 'dp'))
- grad_w_query: float32 [1024, 512], P(('row', 'dp'), 'col')
- grad_w_kv: float32 [1024, 2, 128], P(('row', 'dp'), 'col')
- grad_convx_weight: float32 [1536, 4], P(('col', 'row'))
- grad_convx_bias: float32 [1536], P(('col', 'row'))
- grad_convbc_weight: float32 [256, 4], replicated
- grad_convbc_bias: float32 [256], replicated
- grad_dt_bias: float32 [24], P(('col', 'row'))
- grad_a_log: float32 [24], P(('col', 'row'))
- grad_d_skip: float32 [24], P(('col', 'row'))
- grad_w_mixout: float32 [1536, 1024], P(('col', 'dp'), 'row')
- grad_w_attnout: float32 [512, 1024], P(('col', 'dp'), 'row')
- grad_norm2_gain: float32 [1024], P('row')
- grad_w_gateup: float32 [1024, 2, 2048], P(('row', 'dp'), None, 'col')
- grad_w_down: float32 [2048, 1024], P(('col', 'dp'), 'row')
The draws below stay inside these ranges and needn't reach their ends.
Inputs may be any that keep to these rules, and one draw needn't show every extreme that they name: `segment_ids`: segment ids never fall along a sequence.
All inputs are finite; a program needn't handle non-finite values.
Results may differ from the reference program's by a relative error of at most 0.0093.
Values may be sent and summed in bfloat16 or wider, within the bound.
No kernel may reach another device: no remote copies, remote signals or barrier semaphores. Data moves between devices by JAX's collectives and lax.ppermute only.
A program may use at most 128 MiB of HBM per device.

```python
import math
import jax
import jax.numpy as jnp
import numpy as np
from jax import lax

D = 1024
HM = 24
P_SIZE = 64
NSTATE = 128
HQ = 8
KVH = 2
HD = 64
FF = 2048
KCONV = 4
DOCS = 4
TOK_DEV = 256
DSSM = 1536
NSEQ = 8
TOKENS = 2048


def block_scale(rng, shape, cuts, low, largest):
    level = 1.0
    for dim, blocks in cuts:
        steps = jax.random.uniform(jax.random.fold_in(jax.random.fold_in(rng, 6), dim), (blocks,), jnp.float32, low / len(cuts), largest / len(cuts))
        level = level * jnp.repeat(jnp.exp(steps), shape[dim] // blocks).reshape((-1,) + (1,) * (len(shape) - 1 - dim))
    return level


def profile(count, total, reach, lean):
    loads = [(1 << 20) // math.isqrt(rank ** lean) + 1 for rank in range(2, count + 1)]
    surplus, counts = total - reach - (count - 1), [1] * (count - 1)
    while surplus > 0:
        movable = [i for i in range(count - 1) if counts[i] < reach]
        mass, budget = sum([loads[i] for i in movable]), surplus
        for i in movable:
            more = min(reach - counts[i], max(1, budget * loads[i] // mass), surplus)
            counts[i] = counts[i] + more
            surplus = surplus - more
    return np.array([reach] + counts)


def uneven(rng, amount, total, most, skew):
    if amount == 2:
        one = jax.random.randint(rng, (), max(1, total - most), min(most, total - 1) + 1)
        return jnp.stack([one, total - one])
    tallies = jnp.asarray(profile(amount, total, most, skew), jnp.int32)
    couples = (amount - 1) // 2
    donor, taker = tallies[1:1 + 2 * couples:2], tallies[2:2 + 2 * couples:2]
    slack = jnp.minimum(donor - 1, most - taker)
    moved = jax.random.randint(jax.random.fold_in(rng, 1), (couples,), 0, 1 << 20) % (slack + 1)
    tallies = tallies.at[1:1 + 2 * couples:2].set(donor - moved).at[2:2 + 2 * couples:2].set(taker + moved)
    return tallies[jax.random.permutation(jax.random.fold_in(rng, 2), amount)]


def centred(key, extent, spread, most, shards=(), held_as=jnp.bfloat16):
    entries = jax.random.normal(key, extent, jnp.float32) * spread
    if len(shards) > 0:
        entries = block_scale(key, extent, shards, -0.22, 0.18) * entries
    return jnp.clip(entries, min=-most, max=most).astype(held_as)


def setup_inputs(seed: int = 0) -> dict:
    seeds = jax.random.split(jax.random.key(seed), 23)
    hidden = centred(seeds[0], (TOKENS, D), 1.0, 6.0, ((0, 8), (1, 4)))
    segment_ids = jax.vmap(lambda own: jnp.searchsorted(jnp.cumsum(uneven(own, DOCS, TOK_DEV, TOK_DEV // 2, 2)), jnp.arange(TOK_DEV), side="right"))(jax.random.split(seeds[1], NSEQ)).reshape((NSEQ, TOK_DEV)).astype(jnp.int32)
    norm1_gain = jnp.clip(1.0 + 0.1 * jax.random.normal(seeds[2], (D,), jnp.float32), 0.5, 1.5).astype(jnp.bfloat16)
    w_gate = centred(seeds[3], (D, DSSM), D ** -0.5, 0.1875, ((0, 2), (1, 2)))
    w_xin = centred(seeds[4], (D, DSSM), D ** -0.5, 0.1875, ((0, 2), (1, 2)))
    w_dt = centred(seeds[5], (D, HM), D ** -0.5, 0.1875, ((0, 2), (1, 2)))
    w_bc = centred(seeds[6], (D, 2 * NSTATE), D ** -0.5, 0.1875, ((0, 2),))
    w_query = centred(seeds[7], (D, HQ * HD), D ** -0.5, 0.1875, ((0, 2), (1, 2)))
    w_kv = centred(seeds[8], (D, KVH, 2 * HD), D ** -0.5, 0.1875, ((0, 2), (1, 2)))
    convx_weight = centred(seeds[9], (DSSM, KCONV), KCONV ** -0.5, 3.0, ((0, 4),))
    convx_bias = centred(seeds[10], (DSSM,), 0.5, 3.0, ((0, 4),))
    convbc_weight = centred(seeds[11], (2 * NSTATE, KCONV), KCONV ** -0.5, 3.0)
    convbc_bias = centred(seeds[12], (2 * NSTATE,), 0.5, 3.0)
    dt_bias = jnp.clip(-3.0 + 3.5 * jax.random.uniform(seeds[13], (HM,), jnp.float32) ** block_scale(seeds[13], (HM,), ((0, 4),), -0.2, 0.2), -3.0, 0.5).astype(jnp.bfloat16)
    a_log = jnp.clip(-4.5 + 4.5 * jax.random.uniform(seeds[14], (HM,), jnp.float32) ** block_scale(seeds[14], (HM,), ((0, 4),), -0.2, 0.2), -4.5, 0.0).astype(jnp.bfloat16)
    d_skip = jnp.clip(0.5 + 1.0 * jax.random.uniform(seeds[15], (HM,), jnp.float32) ** block_scale(seeds[15], (HM,), ((0, 4),), -0.2, 0.2), 0.5, 1.5).astype(jnp.bfloat16)
    w_mixout = centred(seeds[16], (DSSM, D), (HM * P_SIZE * 256) ** -0.5, 0.009765625, ((0, 2), (1, 2)))
    w_attnout = centred(seeds[17], (HQ * HD, D), (HQ * HD // 64) ** -0.5, 2.0, ((0, 2), (1, 2)))
    norm2_gain = jnp.clip(1.0 + 0.1 * jax.random.normal(seeds[18], (D,), jnp.float32), 0.5, 1.5).astype(jnp.bfloat16)
    w_gateup = centred(seeds[19], (D, 2, FF), D ** -0.5, 0.1875, ((0, 2), (2, 2)))
    w_down = centred(seeds[20], (FF, D), FF ** -0.5, 0.125, ((0, 2), (1, 2)))
    cotangent = centred(seeds[21], (TOKENS, D), 1.0, 6.0, ((0, 8), (1, 4)))
    return dict(hidden=hidden, segment_ids=segment_ids, norm1_gain=norm1_gain, w_gate=w_gate, w_xin=w_xin, w_dt=w_dt, w_bc=w_bc, w_query=w_query, w_kv=w_kv, convx_weight=convx_weight, convx_bias=convx_bias, convbc_weight=convbc_weight, convbc_bias=convbc_bias, dt_bias=dt_bias, a_log=a_log, d_skip=d_skip, w_mixout=w_mixout, w_attnout=w_attnout, norm2_gain=norm2_gain, w_gateup=w_gateup, w_down=w_down, cotangent=cotangent)


NORM_EPS = 1e-05
PRECISE = lax.Precision.HIGHEST

@jax.custom_vjp
def low(v):
    return lax.optimization_barrier(v.astype(jnp.bfloat16)).astype(jnp.float32)

@jax.custom_vjp
def low_back(v):
    return v

def low_keep(v):
    return (low(v), None)

def low_pass(kept, grad):
    return (grad,)

def back_keep(v):
    return (v, None)

def back_low(kept, grad):
    return (low(grad),)
low.defvjp(low_keep, low_pass)
low_back.defvjp(back_keep, back_low)

def matmul_high(left, right):
    return jnp.dot(left, right, precision=PRECISE)

def rms_norm(values, gain_vec):
    factor = lax.rsqrt(lax.optimization_barrier(jnp.mean(values * values, axis=-1, keepdims=True)) + NORM_EPS)
    return values * factor * gain_vec

def causal_conv(channels, kernel, conv_bias, segments):
    length = channels.shape[0]
    kernel_taps = kernel.shape[1]
    summed = channels * kernel[:, kernel_taps - 1] + conv_bias
    for offset in range(1, kernel_taps):
        shifted = jnp.pad(channels, ((offset, 0), (0, 0)))[:length]
        earlier = jnp.pad(segments, (offset, 0), constant_values=-1)[:length]
        same_doc = (earlier == segments)[:, None]
        summed = summed + jnp.where(same_doc, shifted, 0.0) * kernel[:, kernel_taps - 1 - offset]
    return summed

def mixers(gate_z, x_input, dt_raw, query, kv_pair, bc_conv, convx_weight, convx_bias, dt_bias, a_log, d_skip, segments):
    length = x_input.shape[0]
    head_count = dt_raw.shape[1]
    head_size = x_input.shape[1] // head_count
    state_size = bc_conv.shape[1] // 2
    x_conv = jax.nn.silu(causal_conv(x_input, convx_weight, convx_bias, segments))
    step_size = jax.nn.softplus(dt_raw + dt_bias)
    cumulative = jnp.cumsum(step_size * -jnp.exp(a_log), axis=0)
    positions = jnp.arange(length)
    allowed = (positions[:, None] >= positions[None, :]) & (segments[:, None] == segments[None, :])
    state_inner = jnp.dot(bc_conv[:, state_size:], bc_conv[:, :state_size].T, precision=PRECISE)
    decays = jnp.exp(jnp.where(allowed[:, :, None], cumulative[:, None, :] - cumulative[None, :, :], -1e+30))
    x_heads = x_conv.reshape(length, head_count, head_size)
    ssm_sum = jnp.einsum('ijh,jhp->ihp', state_inner[:, :, None] * decays, x_heads * step_size[:, :, None], precision=PRECISE)
    ssm_sum = ssm_sum + d_skip[None, :, None] * x_heads
    ssm_out = ssm_sum.reshape(length, head_count * head_size) * jax.nn.silu(gate_z)
    kv_heads = kv_pair.shape[1]
    key_size = kv_pair.shape[2] // 2
    query_heads = query.shape[1] // key_size
    queries = query.reshape(length, query_heads, key_size)
    key_rows = jnp.repeat(kv_pair[:, :, :key_size], query_heads // kv_heads, axis=1)
    value_rows = jnp.repeat(kv_pair[:, :, key_size:], query_heads // kv_heads, axis=1)
    scores = jnp.einsum('ihd,jhd->hij', queries, key_rows, precision=PRECISE) / math.sqrt(key_size)
    scores = jnp.where(allowed[None], scores, -1e+30)
    weights_attn = jax.nn.softmax(scores, axis=-1)
    attended = jnp.einsum('hij,jhd->ihd', weights_attn, value_rows, precision=PRECISE)
    return (ssm_out, attended.reshape(length, query_heads * key_size))

def whole_layer(hidden, norm1_gain, w_gate, w_xin, w_dt, w_bc, w_query, w_kv, convx_weight, convx_bias, convbc_weight, convbc_bias, dt_bias, a_log, d_skip, w_mixout, w_attnout, norm2_gain, w_gateup, w_down, segment_ids):

    def one_sequence(sequence):
        resid, segments = sequence
        normed1 = low(rms_norm(resid, norm1_gain))
        gate_z = low_back(matmul_high(normed1, w_gate))
        x_input = low_back(matmul_high(normed1, w_xin))
        dt_raw = low_back(matmul_high(normed1, w_dt))
        query = low_back(matmul_high(normed1, w_query))
        bc_raw = low_back(matmul_high(normed1, w_bc))
        kv_pair = low_back(jnp.einsum('td,dkc->tkc', normed1, w_kv, precision=PRECISE))
        bc_conv = jax.nn.silu(causal_conv(bc_raw, convbc_weight, convbc_bias, segments))
        ssm_out, attended = mixers(gate_z, x_input, dt_raw, query, kv_pair, bc_conv, convx_weight, convx_bias, dt_bias, a_log, d_skip, segments)
        mixture = low_back(matmul_high(low(ssm_out), w_mixout) + matmul_high(low(attended), w_attnout))
        resid2 = resid + mixture
        normed2 = low(rms_norm(resid2, norm2_gain))
        gate_part = low_back(matmul_high(normed2, w_gateup[:, 0, :]))
        up_part = low_back(matmul_high(normed2, w_gateup[:, 1, :]))
        activation = low(jax.nn.silu(gate_part) * up_part)
        return resid2 + low_back(matmul_high(activation, w_down))
    stacked = hidden.reshape(NSEQ, TOK_DEV, D)
    result = lax.map(jax.checkpoint(one_sequence), (stacked, segment_ids))
    return result.reshape(TOKENS, D)

def reference(hidden, segment_ids, norm1_gain, w_gate, w_xin, w_dt, w_bc, w_query, w_kv, convx_weight, convx_bias, convbc_weight, convbc_bias, dt_bias, a_log, d_skip, w_mixout, w_attnout, norm2_gain, w_gateup, w_down, cotangent):

    def forward(*values):
        return whole_layer(*values, segment_ids)
    primals = (hidden, norm1_gain, w_gate, w_xin, w_dt, w_bc, w_query, w_kv, convx_weight, convx_bias, convbc_weight, convbc_bias, dt_bias, a_log, d_skip, w_mixout, w_attnout, norm2_gain, w_gateup, w_down)
    primals = jax.tree.map(lambda value: value.astype(jnp.float32), primals)
    output, pullback = jax.vjp(forward, *primals)
    g_hidden, g_norm1, g_gate, g_xin, g_dt, g_bc, g_query, g_kv, g_convx_w, g_convx_b, g_convbc_w, g_convbc_b, g_dt_bias, g_a_log, g_d_skip, g_mixout, g_attnout, g_norm2, g_gateup, g_down = pullback(cotangent.astype(jnp.float32))
    return (output.astype(jnp.bfloat16), g_hidden, g_norm1, g_gate, g_xin, g_dt, g_bc, g_query, g_kv, g_convx_w, g_convx_b, g_convbc_w, g_convbc_b, g_dt_bias, g_a_log, g_d_skip, g_mixout, g_attnout, g_norm2, g_gateup, g_down)
```

```python
import math

import jax
import jax.numpy as jnp
from jax import lax
from jax.sharding import PartitionSpec as P

NORM_EPS = 1e-05
PRECISE = lax.Precision.HIGHEST


def causal_conv(channels, kernel, conv_bias, segments):
    length = channels.shape[0]
    kernel_taps = kernel.shape[1]
    summed = channels * kernel[:, kernel_taps - 1] + conv_bias
    for offset in range(1, kernel_taps):
        shifted = jnp.pad(channels, ((offset, 0), (0, 0)))[:length]
        earlier = jnp.pad(segments, (offset, 0), constant_values=-1)[:length]
        same_doc = (earlier == segments)[:, None]
        summed = summed + jnp.where(same_doc, shifted, 0.0) * kernel[:, kernel_taps - 1 - offset]
    return summed


def mixers(
    gate_z,
    x_input,
    dt_raw,
    query,
    kv_pair,
    bc_conv,
    convx_weight,
    convx_bias,
    dt_bias,
    a_log,
    d_skip,
    segments,
):
    length = x_input.shape[0]
    head_count = dt_raw.shape[1]
    head_size = x_input.shape[1] // head_count
    state_size = bc_conv.shape[1] // 2
    x_conv = jax.nn.silu(causal_conv(x_input, convx_weight, convx_bias, segments))
    step_size = jax.nn.softplus(dt_raw + dt_bias)
    cumulative = jnp.cumsum(step_size * -jnp.exp(a_log), axis=0)
    positions = jnp.arange(length)
    allowed = (positions[:, None] >= positions[None, :]) & (segments[:, None] == segments[None, :])
    state_inner = jnp.dot(bc_conv[:, state_size:], bc_conv[:, :state_size].T, precision=PRECISE)
    decays = jnp.exp(
        jnp.where(allowed[:, :, None], cumulative[:, None, :] - cumulative[None, :, :], -1e30)
    )
    x_heads = x_conv.reshape(length, head_count, head_size)
    ssm_sum = jnp.einsum(
        "ijh,jhp->ihp",
        state_inner[:, :, None] * decays,
        x_heads * step_size[:, :, None],
        precision=PRECISE,
    )
    ssm_sum = ssm_sum + d_skip[None, :, None] * x_heads
    ssm_out = ssm_sum.reshape(length, head_count * head_size) * jax.nn.silu(gate_z)
    kv_heads = kv_pair.shape[1]
    key_size = kv_pair.shape[2] // 2
    query_heads = query.shape[1] // key_size
    queries = query.reshape(length, query_heads, key_size)
    key_rows = jnp.repeat(kv_pair[:, :, :key_size], query_heads // kv_heads, axis=1)
    value_rows = jnp.repeat(kv_pair[:, :, key_size:], query_heads // kv_heads, axis=1)
    scores = jnp.einsum("ihd,jhd->hij", queries, key_rows, precision=PRECISE) / math.sqrt(key_size)
    scores = jnp.where(allowed[None], scores, -1e30)
    weights_attn = jax.nn.softmax(scores, axis=-1)
    attended = jnp.einsum("hij,jhd->ihd", weights_attn, value_rows, precision=PRECISE)
    return (ssm_out, attended.reshape(length, query_heads * key_size))


def swap(values, axis, step=1):
    count = lax.axis_size(axis)
    return lax.ppermute(values, axis, [(i, i ^ step) for i in range(count)])


def dot(left, right):
    return jnp.dot(left, right, preferred_element_type=jnp.float32)


def dot_bt(left, right):
    return lax.dot_general(
        left, right, (((1,), (1,)), ((), ())), preferred_element_type=jnp.float32
    )


def in_order(index, own, other, axis):
    first = index == 0
    return jnp.concatenate([jnp.where(first, own, other), jnp.where(first, other, own)], axis)


def pick_blocks(values, places, size, axis):
    return jnp.concatenate(
        [lax.dynamic_slice_in_dim(values, p * size, size, axis) for p in places], axis
    )


def spread(weight, spot, axis, near_first):
    size = weight.shape[axis] // 4
    mine = lax.dynamic_slice_in_dim(weight, spot * size, size, axis)
    first = swap(mine, "row")
    steps = (1, 2) if near_first else (2, 1)
    second = swap(first, "dp", steps[0])
    pair = swap(jnp.concatenate([first, second], axis), "dp", steps[1])
    low = lax.slice_in_dim(pair, 0, size, axis=axis)
    high = lax.slice_in_dim(pair, size, 2 * size, axis=axis)
    if near_first:
        return jnp.concatenate([first, second, low, high], axis)
    return jnp.concatenate([first, low, second, high], axis)


def halving_order(count):
    order = [0]
    step = count // 2
    while step >= 1:
        order = order + [o | step for o in order]
        step //= 2
    return order


def shuffled(left, sizes):
    count = lax.axis_size("dp")
    me = lax.axis_index("dp")
    parts = []
    for o in halving_order(count):
        for turned in left:
            size = turned.shape[0] // count
            parts.append(lax.dynamic_slice_in_dim(turned, (me ^ o) * size, size, 0))
    return jnp.concatenate(parts, 0)


def dp_scatter(rows, right):
    half = rows.shape[0] // 2
    sent = dot(rows[half:], right).astype(jnp.bfloat16)
    came = swap(sent, "dp", 1)
    total = dot(rows[:half], right) + came.astype(jnp.float32)
    step = 2
    while step < lax.axis_size("dp"):
        half = half // 2
        came = swap(total[half:].astype(jnp.bfloat16), "dp", step)
        total = total[:half] + came.astype(jnp.float32)
        step *= 2
    return total


def shards(
    hidden,
    segment_ids,
    norm1_gain,
    w_gate,
    w_xin,
    w_dt,
    w_bc,
    w_query,
    w_kv,
    convx_weight,
    convx_bias,
    convbc_weight,
    convbc_bias,
    dt_bias,
    a_log,
    d_skip,
    w_mixout,
    w_attnout,
    norm2_gain,
    w_gateup,
    w_down,
    cotangent,
):
    f32 = jnp.float32
    bf16 = jnp.bfloat16
    segments = segment_ids[0]
    row = lax.axis_index("row")
    col = lax.axis_index("col")
    spot = lax.axis_index("dp") & 3
    tokens, quarter = hidden.shape
    halfw = 2 * quarter
    full_width = 4 * quarter
    piece = halfw // 4
    ch = w_xin.shape[1]
    nq = w_query.shape[1]
    nkv = w_kv.shape[2]
    nbc = w_bc.shape[1]
    heads = w_dt.shape[1]
    ff = w_down.shape[0]

    both = jnp.concatenate([hidden, cotangent], 0)
    over_row = swap(both, "row")
    over_col = swap(jnp.concatenate([both, over_row], 0), "col")
    own_half = in_order(col, both, over_col[: 2 * tokens], 1)
    far_half = in_order(col, over_row, over_col[2 * tokens :], 1)
    far_half = pick_blocks(far_half, [spot ^ j for j in range(4)], piece, 1)
    hid = jnp.concatenate([own_half[:tokens], far_half[:tokens]], 1).astype(f32)
    grad_out = jnp.concatenate([own_half[tokens:], far_half[tokens:]], 1)

    small = jnp.concatenate(
        [
            convx_weight.T.reshape(-1),
            convx_bias,
            dt_bias,
            a_log,
            d_skip,
            norm2_gain,
        ]
    )
    small_far = swap(small, "row")
    taps = convx_weight.shape[1]
    cq = convx_bias.shape[0]
    hq = dt_bias.shape[0]

    def joined(start, size):
        return in_order(row, small[start : start + size], small_far[start : start + size], 0)

    at = taps * cq
    cx_w = jnp.stack([joined(k * cq, cq) for k in range(taps)], 1).astype(f32)
    cx_b = joined(at, cq).astype(f32)
    dtb = joined(at + cq, hq).astype(f32)
    alog = joined(at + cq + hq, hq).astype(f32)
    dsk = joined(at + cq + 2 * hq, hq).astype(f32)
    gain2_far = pick_blocks(small_far[at + cq + 3 * hq :], [spot ^ j for j in range(4)], piece, 0)
    gain_one = norm1_gain.astype(f32)
    gain_two = jnp.concatenate([norm2_gain, gain2_far]).astype(f32)

    w_tall = jnp.concatenate([w_mixout, w_attnout, w_down], 0)
    w_gu = w_gateup.reshape(halfw, 2 * ff)
    w_tall_far = spread(w_tall, spot, 1, True)
    w_gu_far = spread(w_gu, spot, 0, False)

    factor1 = lax.rsqrt(jnp.mean(hid * hid, axis=1) + NORM_EPS)
    hid_own = hid[:, :halfw]
    normed1 = (hid_own * factor1[:, None] * gain_one).astype(bf16)
    w_kv2 = w_kv.reshape(halfw, nkv)
    w_dtp = jnp.pad(w_dt, ((0, 0), (0, 128 - heads)))
    w_one = jnp.concatenate([w_xin, w_bc, w_dtp], 1)
    w_two = jnp.concatenate([w_gate, w_query, w_kv2], 1)
    part_one = dot(normed1, w_one)
    part_two = dot(normed1, w_two)
    sum_one = part_one + swap(part_one.astype(bf16), "row").astype(f32)
    sum_two = part_two + swap(part_two.astype(bf16), "row").astype(f32)
    x_input = sum_one[:, :ch]
    bc_raw = sum_one[:, ch : ch + nbc]
    dt_raw = sum_one[:, ch + nbc : ch + nbc + heads]
    gate_z = sum_two[:, :ch]
    query = sum_two[:, ch : ch + nq]
    kv_pair = sum_two[:, ch + nq :].reshape(tokens, 1, nkv)

    def shared_conv(bc_values, conv_kernel, conv_shift):
        return jax.nn.silu(causal_conv(bc_values, conv_kernel, conv_shift, segments))

    bc_conv, conv_back = jax.vjp(
        shared_conv, bc_raw, convbc_weight.astype(f32), convbc_bias.astype(f32)
    )

    def local_mix(*values):
        return mixers(*values, segments)

    (ssm_out, attended), mix_back = jax.vjp(
        local_mix, gate_z, x_input, dt_raw, query, kv_pair, bc_conv, cx_w, cx_b, dtb, alog, dsk
    )
    ssm_low = ssm_out.astype(bf16)
    att_low = attended.astype(bf16)
    mixed_low = jnp.concatenate([ssm_low, att_low], 1)
    inner = ch + nq
    mix_part = jnp.concatenate(
        [dot(mixed_low, w_tall[:inner]), dot(mixed_low, w_tall_far[:inner])], 1
    )
    resid2 = hid + (mix_part + swap(mix_part, "col"))
    factor2 = lax.rsqrt(jnp.mean(resid2 * resid2, axis=1) + NORM_EPS)
    normed2 = (resid2 * factor2[:, None] * gain_two).astype(bf16)
    gate_up = dot(normed2[:, :halfw], w_gu) + dot(normed2[:, halfw:], w_gu_far)
    grad_act = dot_bt(grad_out[:, :halfw], w_tall[inner:]) + dot_bt(
        grad_out[:, halfw:], w_tall_far[inner:]
    )
    gate_part = gate_up[:, :ff]
    up_part = gate_up[:, ff:]
    sigmoid_gate = jax.nn.sigmoid(gate_part)
    silu_gate = gate_part * sigmoid_gate
    activation = (silu_gate * up_part).astype(bf16)
    grad_gate = grad_act * up_part * (sigmoid_gate * (1.0 + gate_part * (1.0 - sigmoid_gate)))
    grad_up = grad_act * silu_gate
    grad_gu = jnp.concatenate([grad_gate.astype(bf16), grad_up.astype(bf16)], 1)
    n2_part = jnp.concatenate([dot_bt(grad_gu, w_gu), dot_bt(grad_gu, w_gu_far)], 1)
    grad_n2 = n2_part + swap(n2_part, "col")

    down_part = dot(activation, w_tall[inner:])
    start = col * quarter
    other = (1 - col) * quarter
    down_came = swap(lax.dynamic_slice_in_dim(down_part, other, quarter, 1), "col")
    output = (
        lax.dynamic_slice_in_dim(resid2, start, quarter, 1)
        + (lax.dynamic_slice_in_dim(down_part, start, quarter, 1) + down_came)
    ).astype(bf16)

    gained = grad_n2 * gain_two
    inner_sum = jnp.sum(gained * resid2, axis=1)
    v_norm2 = jnp.sum(grad_n2[:, :halfw] * resid2[:, :halfw] * factor2[:, None], axis=0)
    grad_resid2 = (
        grad_out.astype(f32)
        + factor2[:, None] * gained
        - resid2 * (factor2 * factor2 * factor2 * inner_sum / full_width)[:, None]
    )
    grad_mixed = grad_resid2.astype(bf16)
    dym = dot_bt(grad_mixed[:, :halfw], w_tall[:inner]) + dot_bt(
        grad_mixed[:, halfw:], w_tall_far[:inner]
    )
    g_z, g_x, g_dt, g_q, g_kv, g_bcc, g_cxw, g_cxb, g_dtb, g_alog, g_dsk = mix_back(
        (dym[:, :ch], dym[:, ch:])
    )
    g_bc, g_cbw, g_cbb = conv_back(g_bcc)
    g_bc = g_bc + swap(g_bc, "col")
    g_bc = g_bc.astype(bf16)
    g_dtp = jnp.pad(g_dt.astype(bf16), ((0, 0), (0, 128 - heads)))
    g_one = jnp.concatenate([g_x.astype(bf16), g_bc, g_dtp], 1)
    g_two = jnp.concatenate(
        [g_z.astype(bf16), g_q.astype(bf16), g_kv.reshape(tokens, nkv).astype(bf16)], 1
    )
    n1_part = (
        dot_bt(g_x.astype(bf16), w_xin) + dot_bt(g_dtp, w_dtp) + dot_bt(g_two, w_two)
    )
    grad_n1 = (n1_part + swap(n1_part, "col")) + dot_bt(g_bc, w_bc)
    gained1 = grad_n1 * gain_one
    sum1 = jnp.sum(gained1 * hid_own, axis=1)
    sum1 = sum1 + swap(sum1, "row")
    v_norm1 = jnp.sum(grad_n1 * hid_own * factor1[:, None], axis=0)
    grad_full = (
        grad_resid2[:, :halfw]
        + factor1[:, None] * gained1
        - hid_own * (factor1 * factor1 * factor1 * sum1 / full_width)[:, None]
    )
    grad_hidden = lax.dynamic_slice_in_dim(grad_full, start, quarter, 1)

    r_down = dp_scatter(shuffled([activation.T], None), grad_out[:, :halfw])
    r_gu = dp_scatter(shuffled([normed2[:, :halfw].T], None), grad_gu)
    r_tall = dp_scatter(shuffled([ssm_low.T, att_low.T], None), grad_mixed[:, :halfw])
    left1 = shuffled([normed1.T], None)
    r_two = dp_scatter(left1, g_two)
    r_one = dp_scatter(left1, g_one)

    def mine(values):
        size = values.shape[0] // 2
        return lax.dynamic_slice_in_dim(values, row * size, size, 0)

    shared = jnp.concatenate([g_cbw.T.reshape(-1), g_cbb])
    shared = shared + swap(shared, "col")
    shared_far = swap(shared, "row")
    shared = jnp.where(row == 0, shared, shared_far)
    vector = jnp.concatenate(
        [
            v_norm1,
            v_norm2,
            mine(g_cxw.T.reshape(taps, 2, cq).transpose(1, 0, 2).reshape(-1)),
            mine(g_cxb),
            mine(g_dtb),
            mine(g_alog),
            mine(g_dsk),
            shared,
        ]
    )
    vector = lax.optimization_barrier(vector)
    step = 1
    while step < lax.axis_size("dp"):
        vector = vector + swap(vector, "dp", step)
        step *= 2
    sizes = [halfw, halfw, taps * cq, cq, hq, hq, hq, taps * nbc, nbc]
    cuts = []
    at = 0
    for size in sizes:
        cuts.append(vector[at : at + size])
        at += size
    o_norm1, o_norm2, o_cxw, o_cxb, o_dtb, o_alog, o_dsk, o_cbw, o_cbb = cuts
    k_rows = r_one.shape[0]
    m_rows = ch // lax.axis_size("dp")
    return (
        output,
        grad_hidden,
        o_norm1,
        r_two[:, :ch],
        r_one[:, :ch],
        r_one[:, ch + nbc : ch + nbc + heads],
        r_one[:, ch : ch + nbc],
        r_two[:, ch : ch + nq],
        r_two[:, ch + nq :].reshape(k_rows, 1, nkv),
        o_cxw.reshape(taps, cq).T,
        o_cxb,
        o_cbw.reshape(taps, nbc).T,
        o_cbb,
        o_dtb,
        o_alog,
        o_dsk,
        r_tall[:m_rows],
        r_tall[m_rows:],
        o_norm2,
        r_gu.reshape(k_rows, 2, ff),
        r_down,
    )


def solution(mesh):
    placed = (
        P("dp", ("row", "col")),
        P("dp", None),
        P("row"),
        P("row", "col"),
        P("row", "col"),
        P("row", "col"),
        P("row", None),
        P("row", "col"),
        P("row", "col", None),
        P(("col", "row"), None),
        P(("col", "row")),
        P(),
        P(),
        P(("col", "row")),
        P(("col", "row")),
        P(("col", "row")),
        P("col", "row"),
        P("col", "row"),
        P("row"),
        P("row", None, "col"),
        P("col", "row"),
        P("dp", ("row", "col")),
    )
    return jax.shard_map(
        shards,
        mesh=mesh,
        in_specs=placed,
        out_specs=(
            P("dp", ("row", "col")),
            P("dp", ("row", "col")),
            P("row"),
            P(("row", "dp"), "col"),
            P(("row", "dp"), "col"),
            P(("row", "dp"), "col"),
            P(("row", "dp"), None),
            P(("row", "dp"), "col"),
            P(("row", "dp"), "col", None),
            P(("col", "row"), None),
            P(("col", "row")),
            P(),
            P(),
            P(("col", "row")),
            P(("col", "row")),
            P(("col", "row")),
            P(("col", "dp"), "row"),
            P(("col", "dp"), "row"),
            P("row"),
            P(("row", "dp"), None, "col"),
            P(("col", "dp"), "row"),
        ),
        check_vma=False,
    )
```

```python
import jax
import jax.numpy as jnp
import numpy as np
from jax import lax
from jax.experimental import pallas as pl
from jax.experimental.pallas import tpu as pltpu
from jax.sharding import PartitionSpec as P

NORM_EPS = 1e-05
F32 = jnp.float32
BF16 = jnp.bfloat16
HEAD = 64
LANES = 128
TAPS = 4
FAR = -1e30


def swap(values, axis, step=1):
    count = lax.axis_size(axis)
    return lax.ppermute(values, axis, [(i, i ^ step) for i in range(count)])


def dot(left, right):
    return jnp.dot(left, right, preferred_element_type=F32)


def dot_bt(left, right):
    return lax.dot_general(left, right, (((1,), (1,)), ((), ())), preferred_element_type=F32)


def dot_at(left, right):
    return lax.dot_general(left, right, (((0,), (0,)), ((), ())), preferred_element_type=F32)


def fine(left, right, dims=((1,), (0,))):
    return lax.dot_general(
        left, right, (dims, ((), ())), precision=lax.Precision.HIGHEST, preferred_element_type=F32
    )


def call(kernel, outs, *args, scratch=(), smem=()):
    specs = [
        pl.BlockSpec(memory_space=pltpu.SMEM if i in smem else pltpu.VMEM)
        for i in range(len(args))
    ]
    return pl.pallas_call(
        kernel,
        out_shape=[jax.ShapeDtypeStruct(s, d) for s, d in outs],
        in_specs=specs,
        out_specs=[pl.BlockSpec(memory_space=pltpu.VMEM)] * len(outs),
        scratch_shapes=[pltpu.VMEM(s, d) for s, d in scratch],
        compiler_params=pltpu.CompilerParams(vmem_limit_bytes=56 << 20),
    )(*args)


def iota(shape, dim):
    return lax.broadcasted_iota(jnp.int32, shape, dim)


def column(row_vector):
    ones = jnp.full((row_vector.shape[0], LANES), 1.0 / row_vector.shape[0], F32)
    return fine(row_vector, ones, ((0,), (0,)))


def token_sums(values):
    return fine(jnp.ones((8, values.shape[1]), F32), values, ((1,), (1,)))


def open_kernel(place, mine, came, own_out, sums_out):
    tokens = mine.shape[0] // 2
    width = mine.shape[1]
    first = place[0] == 0
    a = mine[...]
    b = came[...]
    own_out[:, :width] = jnp.where(first, a, b)
    own_out[:, width:] = jnp.where(first, b, a)
    ha = a[:tokens].astype(F32)
    hb = b[:tokens].astype(F32)
    sums_out[...] = token_sums(ha * ha + hb * hb)


def project_kernel(full_width, own, sums, sums_far, gain, wx, wb, wd, wg, wq, wk, n1_out, p_out, low_out):
    tokens = n1_out.shape[0]
    mean = column(sums[...] + sums_far[...])[:, :1] / full_width
    factor = lax.rsqrt(mean + NORM_EPS)
    n1 = (own[:tokens].astype(F32) * factor * gain[...]).astype(BF16)
    n1_out[...] = n1
    at = 0
    for w in (wx, wb, wd, wg, wq, wk):
        size = w.shape[1]
        part = dot(n1, w[...])
        p_out[:, at : at + size] = part
        low_out[:, at : at + size] = part.astype(BF16)
        at += size


def masks(seg_row, seg_col, turned):
    tokens = seg_row.shape[1]
    i = iota((tokens, tokens), 1 if turned else 0)
    j = iota((tokens, tokens), 0 if turned else 1)
    same = seg_col[:, :1] == seg_row[...]
    return jnp.where((i >= j) & same, 0.0, FAR)


def valids(seg_col):
    seg = seg_col[...]
    t = iota(seg.shape, 0)
    return [
        jnp.where((t >= k) & (pltpu.roll(seg, k, 0) == seg), 1.0, 0.0) for k in range(1, TAPS)
    ]


def conv(block, taps, bias, valid):
    total = block * taps[TAPS - 1 : TAPS] + bias
    for k in range(1, TAPS):
        total = total + (pltpu.roll(block, k, 0) * valid[k - 1]) * taps[TAPS - 1 - k : TAPS - k]
    return total


def conv_turn(grad, block, taps, valid):
    tokens = grad.shape[0]
    back = grad * taps[TAPS - 1 : TAPS]
    rows = [None] * TAPS
    rows[TAPS - 1] = jnp.sum(grad * block, axis=0, keepdims=True)
    for k in range(1, TAPS):
        kept = grad * valid[k - 1]
        back = back + pltpu.roll(kept, tokens - k, 0) * taps[TAPS - 1 - k : TAPS - k]
        rows[TAPS - 1 - k] = jnp.sum(kept * pltpu.roll(block, k, 0), axis=0, keepdims=True)
    rows.append(jnp.sum(grad, axis=0, keepdims=True))
    rows.append(jnp.zeros((8 - len(rows), grad.shape[1]), F32))
    return back, jnp.concatenate(rows, 0)


def silu_turn(value):
    sig = jax.nn.sigmoid(value)
    return value * sig, sig * (1.0 + value * (1.0 - sig))


def steps(dt_raw, head_par):
    shifted = dt_raw + head_par[0:1]
    return jnp.maximum(shifted, 0.0) + jnp.log1p(jnp.exp(-jnp.abs(shifted)))


def mix_kernel(
    ch, nq, seg_row, seg_col, own, came, x_par, bc_par, head_par,
    mixed_out, sums_out, pre_out, y_out,
):
    tokens = own.shape[0]
    nbc = bc_par.shape[1]
    state = nbc // 2
    sums_out[...] = own[...] + came[...].astype(F32)
    lane = iota((tokens, LANES), 1)
    low = lane < HEAD
    mask = masks(seg_row, seg_col, False)
    valid = valids(seg_col)
    for b in range(nbc // LANES):
        at = ch + b * LANES
        part = slice(b * LANES, (b + 1) * LANES)
        pre_out[:, at : at + LANES] = conv(
            sums_out[:, at : at + LANES], bc_par[0:TAPS, part], bc_par[TAPS : TAPS + 1, part], valid
        )
    bcc = pre_out[:, ch : ch + nbc]
    bcc = bcc * jax.nn.sigmoid(bcc)
    inner = fine(bcc[:, state:], bcc[:, :state], ((1,), (1,)))
    dt = steps(sums_out[:, ch + nbc : ch + nbc + LANES], head_par)
    tri = jnp.where(iota((tokens, tokens), 0) >= iota((tokens, tokens), 1), 1.0, 0.0)
    cum = fine(tri, dt * -jnp.exp(head_par[1:2]))
    cum_row = cum.T
    base = ch + nbc + LANES
    for p in range(ch // LANES):
        part = slice(p * LANES, (p + 1) * LANES)
        pre = conv(sums_out[:, part], x_par[0:TAPS, part], x_par[TAPS : TAPS + 1, part], valid)
        pre_out[:, part] = pre
        xc = pre * jax.nn.sigmoid(pre)
        h = 2 * p
        xdt = (xc * jnp.where(low, dt[:, h : h + 1], dt[:, h + 1 : h + 2])).astype(BF16)
        ys = []
        for e in (h, h + 1):
            decay = jnp.exp((cum[:, e : e + 1] - cum_row[e : e + 1]) + mask)
            ys.append(dot((inner * decay).astype(BF16), xdt))
        y = jnp.where(low, ys[0], ys[1])
        y_out[:, part] = y
        y = y + x_par[TAPS + 1 : TAPS + 2, part] * xc
        z = sums_out[:, base + p * LANES : base + (p + 1) * LANES]
        mixed_out[:, part] = (y * (z * jax.nn.sigmoid(z))).astype(BF16)
    at = base + ch
    kv = sums_out[:, at + nq : at + nq + LANES].astype(BF16)
    kv_turn = pltpu.roll(sums_out[:, at + nq : at + nq + LANES], HEAD, 1).astype(BF16)
    keys = jnp.where(low, kv, kv_turn)
    vals = jnp.where(low, kv_turn, kv)
    for p in range(nq // LANES):
        query = sums_out[:, at + p * LANES : at + (p + 1) * LANES] * (HEAD ** -0.5)
        outs = []
        for side in (low, ~low):
            score = dot_bt(jnp.where(side, query, 0.0).astype(BF16), keys) + mask
            score = jnp.exp(score - jnp.max(score, axis=1, keepdims=True))
            total = jnp.sum(score, axis=1, keepdims=True)
            outs.append(dot(score.astype(BF16), vals) / total)
        mixed_out[:, ch + p * LANES : ch + (p + 1) * LANES] = jnp.where(
            low, outs[0], outs[1]
        ).astype(BF16)


def unmix_kernel(
    ch, nq, seg_row, seg_col, sums, pre, ys, dym, x_par, bc_par, head_par,
    gx_out, gtwo_out, gdt_out, gbc_out, small_out, prod_a, prod_b, turned,
):
    tokens = sums.shape[0]
    nbc = bc_par.shape[1]
    state = nbc // 2
    lane = iota((tokens, LANES), 1)
    low = lane < HEAD
    mask = masks(seg_row, seg_col, True)
    valid = valids(seg_col)
    bc_pre = pre[:, ch : ch + nbc]
    bcc, bcc_turn = silu_turn(bc_pre)
    b_in = bcc[:, :state]
    c_in = bcc[:, state:]
    inner = fine(b_in, c_in, ((1,), (1,)))
    dt_raw = sums[:, ch + nbc : ch + nbc + LANES]
    dt = steps(dt_raw, head_par)
    rate = jnp.exp(head_par[1:2])
    tri = jnp.where(iota((tokens, tokens), 0) >= iota((tokens, tokens), 1), 1.0, 0.0)
    cum = fine(tri, dt * -rate)
    cum_row = cum.T
    base = ch + nbc + LANES
    small_out[...] = jnp.zeros_like(small_out)
    turned[...] = jnp.zeros_like(turned)
    for p in range(ch // LANES):
        part = slice(p * LANES, (p + 1) * LANES)
        xc, xc_turn = silu_turn(pre[:, part])
        skip = x_par[TAPS + 1 : TAPS + 2, part]
        z = sums[:, base + p * LANES : base + (p + 1) * LANES]
        gate, gate_turn = silu_turn(z)
        dy_in = dym[:, part]
        y = ys[:, part]
        gtwo_out[:, part] = (dy_in * (y + skip * xc) * gate_turn).astype(BF16)
        dy = dy_in * gate
        h = 2 * p
        dt_pair = jnp.where(low, dt[:, h : h + 1], dt[:, h + 1 : h + 2])
        xdt = xc * dt_pair
        dy_low = dy.astype(BF16)
        x_low = xdt.astype(BF16)
        sides = []
        for e, side in ((h, low), (h + 1, ~low)):
            decay = jnp.exp((cum_row[e : e + 1] - cum[:, e : e + 1]) + mask)
            turned[...] += dot_bt(jnp.where(side, xdt, 0.0).astype(BF16), dy_low) * decay
            sides.append(dot((inner * decay).astype(BF16), dy_low))
        dxdt = jnp.where(low, sides[0], sides[1])
        prod_a[:, part] = dy_low.astype(F32) * y - x_low.astype(F32) * dxdt
        prod_b[:, part] = dxdt * xc
        small_out[8 + TAPS + 1 : 8 + TAPS + 2, part] = jnp.sum(dy * xc, axis=0, keepdims=True)
        dpre = (skip * dy + dxdt * dt_pair) * xc_turn
        back, rows = conv_turn(dpre, sums[:, part], x_par[0:TAPS, part], valid)
        gx_out[:, part] = back.astype(BF16)
        small_out[0:8, part] = rows
    pick = jnp.where(iota((ch, LANES), 0) // HEAD == iota((ch, LANES), 1), 1.0, 0.0)
    dcum = fine(prod_a[...], pick)
    ddt = fine(prod_b[...], pick)
    after = fine(tri, dcum, ((0,), (0,)))
    ddt = ddt - rate * after
    ddt = ddt * jax.nn.sigmoid(dt_raw + head_par[0:1])
    gdt_out[...] = ddt.astype(BF16)
    small_out[8 + TAPS : 8 + TAPS + 1, 0:LANES] = jnp.sum(ddt, axis=0, keepdims=True)
    small_out[8 + TAPS : 8 + TAPS + 1, LANES : 2 * LANES] = jnp.sum(
        after * (-dt * rate), axis=0, keepdims=True
    )
    skip_sum = jnp.broadcast_to(small_out[8 + TAPS + 1 : 8 + TAPS + 2, :], (8, ch))
    small_out[8 + TAPS : 8 + TAPS + 1, 2 * LANES : 3 * LANES] = fine(skip_sum, pick)[0:1]
    dinner = turned[...]
    d_b = fine(dinner, c_in) * bcc_turn[:, :state]
    d_c = fine(dinner, b_in, ((0,), (0,))) * bcc_turn[:, state:]
    for b, grad in enumerate((d_b, d_c)):
        at = ch + b * LANES
        part = slice(b * LANES, (b + 1) * LANES)
        back, rows = conv_turn(grad, sums[:, at : at + LANES], bc_par[0:TAPS, part], valid)
        gbc_out[0:tokens, part] = back
        gbc_out[tokens : tokens + 8, part] = rows
    at = base + ch
    kv = sums[:, at + nq : at + nq + LANES]
    kv_turn = pltpu.roll(kv, HEAD, 1)
    keys = jnp.where(low, kv, kv_turn).astype(BF16)
    vals = jnp.where(low, kv_turn, kv).astype(BF16)
    dk = jnp.zeros((tokens, LANES), F32)
    dv = jnp.zeros((tokens, LANES), F32)
    for p in range(nq // LANES):
        query = sums[:, at + p * LANES : at + (p + 1) * LANES] * (HEAD ** -0.5)
        grad = dym[:, ch + p * LANES : ch + (p + 1) * LANES]
        dqs = []
        for side in (low, ~low):
            q_low = jnp.where(side, query, 0.0).astype(BF16)
            g_low = jnp.where(side, grad, 0.0).astype(BF16)
            score = dot_bt(keys, q_low) + mask
            score = jnp.exp(score - jnp.max(score, axis=0, keepdims=True))
            prob = score * (1.0 / jnp.sum(score, axis=0, keepdims=True))
            dprob = dot_bt(vals, g_low)
            dv = dv + dot(prob.astype(BF16), g_low)
            inner_sum = jnp.sum(prob * dprob, axis=0, keepdims=True)
            dscore = (prob * (dprob - inner_sum)).astype(BF16)
            dk = dk + dot(dscore, q_low)
            dqs.append(dot_at(dscore, keys))
        gtwo_out[:, ch + p * LANES : ch + (p + 1) * LANES] = (
            jnp.where(low, dqs[0], dqs[1]) * (HEAD ** -0.5)
        ).astype(BF16)
    dk = dk + pltpu.roll(dk, HEAD, 1)
    dv = dv + pltpu.roll(dv, HEAD, 1)
    gtwo_out[:, ch + nq : ch + nq + LANES] = jnp.where(low, dk, dv).astype(BF16)


def tall_far(first, second, pair, start, size):
    return jnp.concatenate(
        [r[start : start + size] for r in (first, second, pair)], axis=1
    )


def out_kernel(mixed, tall, first, second, pair, part_out):
    inner = mixed.shape[1]
    half = tall.shape[1]
    value = mixed[...]
    part_out[:, :half] = dot(value, tall[0:inner])
    part_out[:, half:] = dot(value, tall_far(first, second, pair, 0, inner))


def norm_factor(value):
    return lax.rsqrt(jnp.mean(value * value, axis=1, keepdims=True) + NORM_EPS)


def feed_kernel(
    inner, place, own, far, part, came, gain, gu, gu_first, gu_second, gu_pair,
    tall, first, second, pair,
    h2_out, n2_out, act_out, ggu_out, n2p_out, down_out, far_out,
):
    tokens = part.shape[0]
    half = own.shape[1]
    piece = half // 4
    spot = place[1]
    for j in range(4):
        at = pl.multiple_of((spot ^ j) * piece, piece)
        far_out[:, j * piece : (j + 1) * piece] = far[:, pl.ds(at, piece)]
    h2_out[:, :half] = own[0:tokens].astype(F32) + (part[:, :half] + came[:, :half])
    h2_out[:, half:] = far_out[0:tokens].astype(F32) + (part[:, half:] + came[:, half:])
    h2 = h2_out[...]
    n2 = (h2 * norm_factor(h2) * gain[...]).astype(BF16)
    n2_out[...] = n2[:, :half]
    gu_far = jnp.concatenate(
        [gu_first[...], gu_pair[0:piece], gu_second[...], gu_pair[piece:]], axis=0
    )
    ff = tall.shape[0] - inner
    gate_up = dot(n2[:, :half], gu[...]) + dot(n2[:, half:], gu_far)
    grad_act = dot_bt(own[tokens:], tall[inner:]) + dot_bt(
        far_out[tokens:], tall_far(first, second, pair, inner, ff)
    )
    gate = gate_up[:, :ff]
    up = gate_up[:, ff:]
    silu, silu_grad = silu_turn(gate)
    act = (silu * up).astype(BF16)
    act_out[...] = act
    ggu_out[:, :ff] = (grad_act * up * silu_grad).astype(BF16)
    ggu_out[:, ff:] = (grad_act * silu).astype(BF16)
    ggu = ggu_out[...]
    n2p_out[:, :half] = dot_bt(ggu, gu[...])
    n2p_out[:, half:] = dot_bt(ggu, gu_far)
    down_out[...] = dot(act, tall[inner:])


def permuted(left, source):
    width = left.shape[1]
    hot = jnp.where(iota((width, source.shape[1]), 0) == source, 1.0, 0.0).astype(BF16)
    return dot(left, hot).astype(BF16)


def feed_grad_kernel(n2, act, ggu, own, order, order2, send_out, keep_out):
    tokens = n2.shape[0]
    half = n2.shape[1] // 2
    wide = ggu.shape[1]
    left = permuted(n2[...], order[...])
    keep_out[:, :wide] = dot_at(left[:, :half], ggu[...])
    send_out[:, :wide] = dot_at(left[:, half:], ggu[...]).astype(BF16)
    left = permuted(act[...], order2[...])
    right = own[tokens:]
    width = right.shape[1]
    for s in (0, 1):
        at = wide + s * width
        cut = 2 * s * half
        keep_out[:, at : at + width] = dot_at(left[:, cut : cut + half], right)
        send_out[:, at : at + width] = dot_at(left[:, cut + half : cut + 2 * half], right).astype(BF16)


def turn_kernel(
    full_width, own, far, h2, part, came, gain, mixed, tall, first, second, pair, order,
    dym_out, resid_out, gain_out, send_out, keep_out,
):
    tokens = h2.shape[0]
    half = own.shape[1]
    inner = mixed.shape[1]
    value = h2[...]
    factor = norm_factor(value)
    dn2 = part[...] + came[...]
    gained = dn2 * gain[...]
    inner_sum = jnp.sum(gained * value, axis=1, keepdims=True)
    gain_out[...] = jnp.broadcast_to(
        jnp.sum(dn2[:, :half] * value[:, :half] * factor, axis=0, keepdims=True), gain_out.shape
    )
    slope = factor * factor * factor * inner_sum / full_width
    change = factor * gained - value * slope
    dh_own = own[tokens:].astype(F32) + change[:, :half]
    dh_far = far[tokens:].astype(F32) + change[:, half:]
    resid_out[...] = dh_own
    low_own = dh_own.astype(BF16)
    dym_out[...] = dot_bt(low_own, tall[0:inner]) + dot_bt(
        dh_far.astype(BF16), tall_far(first, second, pair, 0, inner)
    )
    left = permuted(mixed[...], order[...])
    rows = half // 2
    for s in (0, 1):
        at = s * half
        cut = 2 * s * rows
        keep_out[:, at : at + half] = dot_at(left[:, cut : cut + rows], low_own)
        send_out[:, at : at + half] = dot_at(
            left[:, cut + rows : cut + 2 * rows], low_own
        ).astype(BF16)


def grad_two_kernel(n1, g_two, gx, gdt, wx, wd, wg, wq, wk, order, send_out, keep_out, n1p_out):
    rows = n1.shape[1] // 2
    left = permuted(n1[...], order[...])
    send_out[...] = dot_at(left[:, rows:], g_two[...]).astype(BF16)
    keep_out[...] = dot_at(left[:, :rows], g_two[...])
    ch = wg.shape[1]
    nq = wq.shape[1]
    total = dot_bt(gx[...], wx[...]) + dot_bt(gdt[...], wd[...])
    total = total + dot_bt(g_two[:, :ch], wg[...]) + dot_bt(g_two[:, ch : ch + nq], wq[...])
    n1p_out[...] = total + dot_bt(g_two[:, ch + nq :], wk[...])


def grad_one_kernel(n1, gx, gdt, gbc, gbc_came, wb, order, send_out, keep_out, n1b_out):
    tokens = n1.shape[0]
    rows = n1.shape[1] // 2
    ch = gx.shape[1]
    nbc = gbc.shape[1]
    left = permuted(n1[...], order[...])
    both = (gbc[0:tokens] + gbc_came[0:tokens]).astype(BF16)
    at = 0
    for right in (gx[...], both, gdt[...]):
        size = right.shape[1]
        send_out[:, at : at + size] = dot_at(left[:, rows:], right).astype(BF16)
        keep_out[:, at : at + size] = dot_at(left[:, :rows], right)
        at += size
    n1b_out[...] = dot_bt(both, wb[...])


def close_kernel(own, part, came, n1b, gain, gbc, gbc_came, dn1_out, gain_out, rows_out):
    tokens = part.shape[0]
    hid = own[0:tokens].astype(F32)
    dn1 = (part[...] + came[...]) + n1b[...]
    dn1_out[...] = dn1
    rows_out[0:8, :] = token_sums(dn1 * gain[...] * hid)
    rows_out[8:16, :] = gbc[tokens:] + gbc_came[tokens:]


def end_kernel(
    full_width, place, own, sums, sums_far, resid, dn1, gain, rows, rows_far, small, gain2,
    hidden_out, vector_out,
):
    tokens = dn1.shape[0]
    half = dn1.shape[1]
    quarter = hidden_out.shape[1]
    hid = own[0:tokens].astype(F32)
    mean = column(sums[...] + sums_far[...])[:, :1] / full_width
    factor = lax.rsqrt(mean + NORM_EPS)
    inner_sum = column(rows[0:8] + rows_far[0:8])[:, :1]
    value = dn1[...]
    change = resid[...] + factor * (value * gain[...]) - hid * (
        factor * factor * factor * inner_sum / full_width
    )
    first = place[0] == 0
    hidden_out[...] = jnp.where(first, change[:, :quarter], change[:, quarter:])
    count = small.shape[0]
    vector_out[...] = jnp.zeros_like(vector_out)
    vector_out[0:count] = small[...]
    vector_out[count : count + 8, 0 : rows.shape[1]] = jnp.where(
        place[2] == 0, rows[8:16], rows_far[8:16]
    )
    vector_out[count + 8 : count + 9, 0:half] = jnp.sum(value * hid * factor, axis=0, keepdims=True)
    vector_out[count + 9 : count + 10, 0:half] = gain2[0:1]


def halving_order(count):
    order = [0]
    step = count // 2
    while step >= 1:
        order = order + [o | step for o in order]
        step //= 2
    return order


def dp_rest(keep, came, step=2):
    total = keep + came.astype(F32)
    while step < lax.axis_size("dp"):
        half = total.shape[0] // 2
        came = swap(total[half:].astype(BF16), "dp", step)
        total = total[:half] + came.astype(F32)
        step *= 2
    return total


def shards(
    hidden,
    segment_ids,
    norm1_gain,
    w_gate,
    w_xin,
    w_dt,
    w_bc,
    w_query,
    w_kv,
    convx_weight,
    convx_bias,
    convbc_weight,
    convbc_bias,
    dt_bias,
    a_log,
    d_skip,
    w_mixout,
    w_attnout,
    norm2_gain,
    w_gateup,
    w_down,
    cotangent,
):
    row = lax.axis_index("row")
    col = lax.axis_index("col")
    me = lax.axis_index("dp")
    count = lax.axis_size("dp")
    spot = me & 3
    place = jnp.stack([col, spot, row]).astype(jnp.int32)
    tokens, quarter = hidden.shape
    half = 2 * quarter
    full_width = 4 * quarter
    piece = half // 4
    ch = w_xin.shape[1]
    nq = w_query.shape[1]
    nkv = w_kv.shape[2]
    nbc = w_bc.shape[1]
    heads = w_dt.shape[1]
    ff = w_down.shape[0]
    cq = convx_bias.shape[0]
    hq = dt_bias.shape[0]

    both = jnp.concatenate([hidden, cotangent], 0)
    own, sums = call(
        open_kernel,
        [((2 * tokens, half), BF16), ((8, tokens), F32)],
        place,
        both,
        swap(both, "col"),
        smem=(0,),
    )
    sums_far = swap(sums, "row")

    small = jnp.concatenate(
        [convx_weight.T.reshape(-1), convx_bias, dt_bias, a_log, d_skip, norm2_gain]
    )
    small_far = swap(small, "row")
    far = swap(own, "row")

    tall = jnp.concatenate([w_mixout, w_attnout, w_down], 0)
    gu = w_gateup.reshape(half, 2 * ff)
    tall_mine = lax.dynamic_slice_in_dim(tall, spot * piece, piece, 1)
    gu_mine = lax.dynamic_slice_in_dim(gu, spot * piece, piece, 0)
    t_first = swap(tall_mine, "row")
    g_first = swap(gu_mine, "row")
    t_second = swap(t_first, "dp", 1)
    g_second = swap(g_first, "dp", 2)
    t_pair = swap(jnp.concatenate([t_first, t_second], 1), "dp", 2)
    g_pair = swap(jnp.concatenate([g_first, g_second], 0), "dp", 1)

    def joined(start, size):
        a = small[start : start + size]
        b = small_far[start : start + size]
        first = row == 0
        return jnp.concatenate([jnp.where(first, a, b), jnp.where(first, b, a)], 0).astype(F32)

    at = TAPS * cq
    x_par = jnp.stack(
        [joined(k * cq, cq) for k in range(TAPS + 1)]
        + [jnp.repeat(joined(at + cq + 2 * hq, hq), HEAD)]
        + [jnp.zeros((ch,), F32)] * 2
    )
    bc_par = jnp.concatenate(
        [convbc_weight.T, convbc_bias[None], jnp.zeros((3, nbc), BF16)], 0
    ).astype(F32)
    head_par = jnp.stack(
        [jnp.pad(joined(at + cq + k * hq, hq), (0, LANES - heads)) for k in (0, 1)]
        + [jnp.zeros((LANES,), F32)] * 6
    )
    gain2_far = jnp.concatenate(
        [
            lax.dynamic_slice_in_dim(small_far, at + cq + 3 * hq + (spot ^ j) * piece, piece, 0)
            for j in range(4)
        ]
    )
    gain_one = norm1_gain.astype(F32)[None]
    gain_two = jnp.concatenate([norm2_gain, gain2_far]).astype(F32)[None]
    seg_row = segment_ids.astype(F32)
    seg_col = jnp.broadcast_to(segment_ids[0].astype(F32)[:, None], (tokens, LANES))
    wk = w_kv.reshape(half, nkv)
    wd = jnp.pad(w_dt, ((0, 0), (0, LANES - heads)))

    blocks = np.array(halving_order(count))
    order_block = jnp.asarray(np.repeat(blocks, half // count), jnp.int32) ^ me
    within = jnp.asarray(np.tile(np.arange(half // count), count), jnp.int32)
    size = half // count
    order = (order_block * size + within)[None]
    both_within = jnp.concatenate([within, within + size])
    both_block = jnp.concatenate([order_block, order_block])
    order_down = (both_block * (ff // count) + both_within)[None]
    m_rows = ch // count
    a_rows = nq // count
    order_mix = jnp.where(
        both_within < m_rows,
        both_block * m_rows + both_within,
        ch + both_block * a_rows + both_within - m_rows,
    )[None]

    cols = ch + nbc + LANES + ch + nq + nkv
    n1, part, part_low = call(
        lambda *refs: project_kernel(full_width, *refs),
        [((tokens, half), BF16), ((tokens, cols), F32), ((tokens, cols), BF16)],
        own, sums, sums_far, gain_one, w_xin, w_bc, wd, w_gate, w_query, wk,
    )
    mixed, raw, pre, ys = call(
        lambda *refs: mix_kernel(ch, nq, *refs),
        [
            ((tokens, ch + nq), BF16),
            ((tokens, cols), F32),
            ((tokens, ch + nbc), F32),
            ((tokens, ch), F32),
        ],
        seg_row, seg_col, part, swap(part_low, "row"), x_par, bc_par, head_par,
    )
    mix_part = call(
        out_kernel, [((tokens, full_width), F32)], mixed, tall, t_first, t_second, t_pair
    )[0]
    h2, n2, act, ggu, n2_part, down, far_order = call(
        lambda *refs: feed_kernel(ch + nq, *refs),
        [
            ((tokens, full_width), F32),
            ((tokens, half), BF16),
            ((tokens, ff), BF16),
            ((tokens, 2 * ff), BF16),
            ((tokens, full_width), F32),
            ((tokens, half), F32),
            ((2 * tokens, half), BF16),
        ],
        place, own, far, mix_part, swap(mix_part, "col"), gain_two,
        gu, g_first, g_second, g_pair, tall, t_first, t_second, t_pair,
        smem=(0,),
    )
    n2_came = swap(n2_part, "col")
    send_feed, keep_feed = call(
        feed_grad_kernel,
        [((half // 2, 2 * ff + 2 * half), BF16), ((half // 2, 2 * ff + 2 * half), F32)],
        n2, act, ggu, own, order, order_down,
    )
    came_feed = swap(send_feed, "dp", 1)
    down_came = swap(lax.dynamic_slice_in_dim(down, (1 - col) * quarter, quarter, 1), "col")

    dym, resid, gain2_sum, send_mix, keep_mix = call(
        lambda *refs: turn_kernel(full_width, *refs),
        [
            ((tokens, ch + nq), F32),
            ((tokens, half), F32),
            ((8, half), F32),
            ((half // 2, 2 * half), BF16),
            ((half // 2, 2 * half), F32),
        ],
        own, far_order, h2, n2_part, n2_came, gain_two, mixed, tall, t_first, t_second, t_pair,
        order_mix,
    )
    came_mix = swap(send_mix, "dp", 1)
    gx, g_two, gdt, gbc, small_sum = call(
        lambda *refs: unmix_kernel(ch, nq, *refs),
        [
            ((tokens, ch), BF16),
            ((tokens, ch + nq + nkv), BF16),
            ((tokens, LANES), BF16),
            ((tokens + 8, nbc), F32),
            ((16, ch), F32),
        ],
        seg_row, seg_col, raw, pre, ys, dym, x_par, bc_par, head_par,
        scratch=[((tokens, ch), F32), ((tokens, ch), F32), ((tokens, tokens), F32)],
    )
    gbc_came = swap(gbc, "col")
    send_two, keep_two, n1_part = call(
        grad_two_kernel,
        [
            ((half // 2, ch + nq + nkv), BF16),
            ((half // 2, ch + nq + nkv), F32),
            ((tokens, half), F32),
        ],
        n1, g_two, gx, gdt, w_xin, wd, w_gate, w_query, wk, order,
    )
    came_two = swap(send_two, "dp", 1)
    n1_came = swap(n1_part, "col")
    send_one, keep_one, n1_bc = call(
        grad_one_kernel,
        [
            ((half // 2, ch + nbc + LANES), BF16),
            ((half // 2, ch + nbc + LANES), F32),
            ((tokens, half), F32),
        ],
        n1, gx, gdt, gbc, gbc_came, w_bc, order,
    )
    came_one = swap(send_one, "dp", 1)
    dn1, _, rows = call(
        close_kernel,
        [((tokens, half), F32), ((8, half), F32), ((16, tokens), F32)],
        own, n1_part, n1_came, n1_bc, gain_one, gbc, gbc_came,
    )
    grad_hidden, vector = call(
        lambda *refs: end_kernel(full_width, *refs),
        [((tokens, quarter), F32), ((32, ch), F32)],
        place, own, sums, sums_far, resid, dn1, gain_one, rows, swap(rows, "row"), small_sum, gain2_sum,
        smem=(0,),
    )
    step = 1
    while step < count:
        vector = vector + swap(vector, "dp", step)
        step *= 2

    start = col * quarter
    output = (
        lax.dynamic_slice_in_dim(h2, start, quarter, 1)
        + (lax.dynamic_slice_in_dim(down, start, quarter, 1) + down_came)
    ).astype(BF16)

    r_feed = dp_rest(keep_feed, came_feed)
    r_mix = dp_rest(keep_mix, came_mix)
    r_two = dp_rest(keep_two, came_two)
    r_one = dp_rest(keep_one, came_one)
    r_down = jnp.concatenate([r_feed[:, 2 * ff : 2 * ff + half], r_feed[:, 2 * ff + half :]], 0)
    r_tall = jnp.concatenate([r_mix[:, :half], r_mix[:, half:]], 0)

    def mine(values, width):
        return lax.dynamic_slice_in_dim(values, row * width, width, values.ndim - 1)

    return (
        output,
        grad_hidden,
        vector[24, :half],
        r_two[:, :ch],
        r_one[:, :ch],
        r_one[:, ch + nbc : ch + nbc + heads],
        r_one[:, ch : ch + nbc],
        r_two[:, ch : ch + nq],
        r_two[:, ch + nq :].reshape(size, 1, nkv),
        mine(vector[0:TAPS], cq).T,
        mine(vector[TAPS], cq),
        vector[16 : 16 + TAPS, :nbc].T,
        vector[16 + TAPS, :nbc],
        mine(vector[12, :heads], hq),
        mine(vector[12, LANES : LANES + heads], hq),
        mine(vector[12, 2 * LANES : 2 * LANES + heads], hq),
        r_tall[:m_rows],
        r_tall[m_rows:],
        vector[25, :half],
        r_feed[:, : 2 * ff].reshape(size, 2, ff),
        r_down,
    )


def solution(mesh):
    placed = (
        P("dp", ("row", "col")),
        P("dp", None),
        P("row"),
        P("row", "col"),
        P("row", "col"),
        P("row", "col"),
        P("row", None),
        P("row", "col"),
        P("row", "col", None),
        P(("col", "row"), None),
        P(("col", "row")),
        P(),
        P(),
        P(("col", "row")),
        P(("col", "row")),
        P(("col", "row")),
        P("col", "row"),
        P("col", "row"),
        P("row"),
        P("row", None, "col"),
        P("col", "row"),
        P("dp", ("row", "col")),
    )
    return jax.shard_map(
        shards,
        mesh=mesh,
        in_specs=placed,
        out_specs=(
            P("dp", ("row", "col")),
            P("dp", ("row", "col")),
            P("row"),
            P(("row", "dp"), "col"),
            P(("row", "dp"), "col"),
            P(("row", "dp"), "col"),
            P(("row", "dp"), None),
            P(("row", "dp"), "col"),
            P(("row", "dp"), "col", None),
            P(("col", "row"), None),
            P(("col", "row")),
            P(),
            P(),
            P(("col", "row")),
            P(("col", "row")),
            P(("col", "row")),
            P(("col", "dp"), "row"),
            P(("col", "dp"), "row"),
            P("row"),
            P(("row", "dp"), None, "col"),
            P(("col", "dp"), "row"),
        ),
        check_vma=False,
    )
```

```python
import jax
import jax.numpy as jnp
import numpy as np
from jax import lax
from jax.experimental import pallas as pl
from jax.experimental.pallas import tpu as pltpu
from jax.sharding import PartitionSpec as P

NORM_EPS = 1e-05
F32 = jnp.float32
BF16 = jnp.bfloat16
HEAD = 64
LANES = 128
TAPS = 4
FAR = -1e30


def swap(values, axis, step=1):
    count = lax.axis_size(axis)
    return lax.ppermute(values, axis, [(i, i ^ step) for i in range(count)])


def dot(left, right):
    return jnp.dot(left, right, preferred_element_type=F32)


def dot_bt(left, right):
    return lax.dot_general(left, right, (((1,), (1,)), ((), ())), preferred_element_type=F32)


def dot_at(left, right):
    return lax.dot_general(left, right, (((0,), (0,)), ((), ())), preferred_element_type=F32)


def fine(left, right, dims=((1,), (0,))):
    return lax.dot_general(
        left, right, (dims, ((), ())), precision=lax.Precision.HIGHEST, preferred_element_type=F32
    )


class Chain:
    def __init__(self):
        self.token = jnp.zeros((8, LANES), F32)

    def __call__(self, kernel, outs, *args, scratch=(), smem=(), direct=False, after=()):
        plain = pl.ANY if direct else pltpu.VMEM
        specs = [
            pl.BlockSpec(memory_space=pltpu.SMEM if i in smem else plain)
            for i in range(len(args))
        ]
        extra = (self.token,) + tuple(after)
        count = len(args)
        held = count + len(extra)

        def body(*refs):
            refs[held][...] = jnp.zeros((8, LANES), F32)
            kernel(*refs[:count], *refs[held + 1 :])

        results = pl.pallas_call(
            body,
            out_shape=[jax.ShapeDtypeStruct((8, LANES), F32)]
            + [jax.ShapeDtypeStruct(s, d) for s, d in outs],
            in_specs=specs + [pl.BlockSpec(memory_space=pl.ANY)] * len(extra),
            out_specs=[pl.BlockSpec(memory_space=pltpu.VMEM)]
            + [pl.BlockSpec(memory_space=plain)] * len(outs),
            scratch_shapes=[pltpu.VMEM(s, d) if d is not None else s for s, d in scratch],
            compiler_params=pltpu.CompilerParams(vmem_limit_bytes=56 << 20),
            cost_estimate=pl.CostEstimate(flops=0, bytes_accessed=0, transcendentals=0),
        )(*args, *extra)
        self.token = results[0]
        return results[1:]


def iota(shape, dim):
    return lax.broadcasted_iota(jnp.int32, shape, dim)


def column(row_vector):
    ones = jnp.full((row_vector.shape[0], LANES), 1.0 / row_vector.shape[0], F32)
    return fine(row_vector, ones, ((0,), (0,)))


def token_sums(values):
    return fine(jnp.ones((8, values.shape[1]), F32), values, ((1,), (1,)))


def pieces_kernel(place, wm, wa, wd, gu, cot, t_out, g_out, c_out, sem):
    piece = t_out.shape[1]
    at = pl.multiple_of(place[1] * piece, piece)
    parts = []
    row = 0
    for w in (wm, wa, wd):
        size = w.shape[0]
        parts.append((w.at[:, pl.ds(at, piece)], t_out.at[row : row + size]))
        row += size
    parts.append((gu.at[pl.ds(at, piece)], g_out))
    parts.append((cot, c_out))
    copies = [pltpu.make_async_copy(s, d, sem.at[i]) for i, (s, d) in enumerate(parts)]
    for copy in copies:
        copy.start()
    for copy in copies:
        copy.wait()


def gather_quarters(place, mine, over_col, over_row, over_both, own_out, far_out, far_tmp):
    width = mine.shape[1]
    piece = width // 2
    first = place[0] == 0
    for a, b, out in ((mine, over_col, own_out), (over_row, over_both, far_tmp)):
        out[:, :width] = jnp.where(first, a[...], b[...])
        out[:, width:] = jnp.where(first, b[...], a[...])
    for j in range(4):
        at = pl.multiple_of((place[1] ^ j) * piece, piece)
        far_out[:, j * piece : (j + 1) * piece] = far_tmp[:, pl.ds(at, piece)]


def project_kernel(
    place, mine, over_col, over_row, over_both, gain, wx, wb, wd, wg, wq, wk,
    n1_out, p_out, low_out, own_out, far_out, factor_out, far_tmp,
):
    gather_quarters(place, mine, over_col, over_row, over_both, own_out, far_out, far_tmp)
    own = own_out[...].astype(F32)
    far = far_tmp[...].astype(F32)
    mean = jnp.sum(own * own + far * far, axis=1, keepdims=True) / (2 * own.shape[1])
    factor = lax.rsqrt(mean + NORM_EPS)
    factor_out[...] = jnp.broadcast_to(factor, factor_out.shape)
    n1 = (own * factor * gain[...]).astype(BF16)
    n1_out[...] = n1
    at = 0
    for w in (wx, wb, wd, wg, wq, wk):
        size = w.shape[1]
        part = dot(n1, w[...])
        p_out[:, at : at + size] = part
        low_out[:, at : at + size] = part.astype(BF16)
        at += size


def hop_kernel(t_first, t_second, g_first, g_second, t_out, g_out):
    t_piece = t_first.shape[1]
    g_piece = g_first.shape[0]
    t_out[:, :t_piece] = t_first[...]
    t_out[:, t_piece:] = t_second[...]
    g_out[:g_piece] = g_first[...]
    g_out[g_piece:] = g_second[...]


def masks(seg_row, seg_col, turned):
    tokens = seg_row.shape[1]
    i = iota((tokens, tokens), 1 if turned else 0)
    j = iota((tokens, tokens), 0 if turned else 1)
    same = seg_col[:, :1] == seg_row[...]
    return jnp.where((i >= j) & same, 0.0, FAR)


def valids(seg_col):
    seg = seg_col[...]
    t = iota(seg.shape, 0)
    return [
        jnp.where((t >= k) & (pltpu.roll(seg, k, 0) == seg), 1.0, 0.0) for k in range(1, TAPS)
    ]


def conv(block, taps, bias, valid):
    total = block * taps[TAPS - 1 : TAPS] + bias
    for k in range(1, TAPS):
        total = total + (pltpu.roll(block, k, 0) * valid[k - 1]) * taps[TAPS - 1 - k : TAPS - k]
    return total


def conv_turn(grad, block, taps, valid):
    tokens = grad.shape[0]
    back = grad * taps[TAPS - 1 : TAPS]
    rows = [None] * TAPS
    rows[TAPS - 1] = jnp.sum(grad * block, axis=0, keepdims=True)
    for k in range(1, TAPS):
        kept = grad * valid[k - 1]
        back = back + pltpu.roll(kept, tokens - k, 0) * taps[TAPS - 1 - k : TAPS - k]
        rows[TAPS - 1 - k] = jnp.sum(kept * pltpu.roll(block, k, 0), axis=0, keepdims=True)
    rows.append(jnp.sum(grad, axis=0, keepdims=True))
    rows.append(jnp.zeros((8 - len(rows), grad.shape[1]), F32))
    return back, jnp.concatenate(rows, 0)


def silu_turn(value):
    sig = jax.nn.sigmoid(value)
    return value * sig, sig * (1.0 + value * (1.0 - sig))


def steps(dt_raw, head_par):
    shifted = dt_raw + head_par[0:1]
    return jnp.maximum(shifted, 0.0) + jnp.log1p(jnp.exp(-jnp.abs(shifted)))


def mix_kernel(
    ch, nq, seg_row, seg_col, own, came, x_par, bc_par, head_par, wm, wa, first, second, pair,
    mixed_out, sums_out, pre_out, y_out, part_out,
):
    tokens = own.shape[0]
    nbc = bc_par.shape[1]
    state = nbc // 2
    sums_out[...] = own[...] + came[...].astype(F32)
    lane = iota((tokens, LANES), 1)
    low = lane < HEAD
    mask = masks(seg_row, seg_col, False)
    valid = valids(seg_col)
    for b in range(nbc // LANES):
        at = ch + b * LANES
        part = slice(b * LANES, (b + 1) * LANES)
        pre_out[:, at : at + LANES] = conv(
            sums_out[:, at : at + LANES], bc_par[0:TAPS, part], bc_par[TAPS : TAPS + 1, part], valid
        )
    bcc = pre_out[:, ch : ch + nbc]
    bcc = bcc * jax.nn.sigmoid(bcc)
    inner = fine(bcc[:, state:], bcc[:, :state], ((1,), (1,)))
    dt = steps(sums_out[:, ch + nbc : ch + nbc + LANES], head_par)
    tri = jnp.where(iota((tokens, tokens), 0) >= iota((tokens, tokens), 1), 1.0, 0.0)
    cum = fine(tri, dt * -jnp.exp(head_par[1:2]))
    cum_row = cum.T
    base = ch + nbc + LANES
    for p in range(ch // LANES):
        part = slice(p * LANES, (p + 1) * LANES)
        pre = conv(sums_out[:, part], x_par[0:TAPS, part], x_par[TAPS : TAPS + 1, part], valid)
        pre_out[:, part] = pre
        xc = pre * jax.nn.sigmoid(pre)
        h = 2 * p
        xdt = (xc * jnp.where(low, dt[:, h : h + 1], dt[:, h + 1 : h + 2])).astype(BF16)
        ys = []
        for e in (h, h + 1):
            decay = jnp.exp((cum[:, e : e + 1] - cum_row[e : e + 1]) + mask)
            ys.append(dot((inner * decay).astype(BF16), xdt))
        y = jnp.where(low, ys[0], ys[1])
        y_out[:, part] = y
        y = y + x_par[TAPS + 1 : TAPS + 2, part] * xc
        z = sums_out[:, base + p * LANES : base + (p + 1) * LANES]
        mixed_out[:, part] = (y * (z * jax.nn.sigmoid(z))).astype(BF16)
    at = base + ch
    kv = sums_out[:, at + nq : at + nq + LANES].astype(BF16)
    kv_turn = pltpu.roll(sums_out[:, at + nq : at + nq + LANES], HEAD, 1).astype(BF16)
    keys = jnp.where(low, kv, kv_turn)
    vals = jnp.where(low, kv_turn, kv)
    for p in range(nq // LANES):
        query = sums_out[:, at + p * LANES : at + (p + 1) * LANES] * (HEAD ** -0.5)
        outs = []
        for side in (low, ~low):
            score = dot_bt(jnp.where(side, query, 0.0).astype(BF16), keys) + mask
            score = jnp.exp(score - jnp.max(score, axis=1, keepdims=True))
            total = jnp.sum(score, axis=1, keepdims=True)
            outs.append(dot(score.astype(BF16), vals) / total)
        mixed_out[:, ch + p * LANES : ch + (p + 1) * LANES] = jnp.where(
            low, outs[0], outs[1]
        ).astype(BF16)
    half = wm.shape[1]
    value = mixed_out[...]
    part_out[:, :half] = dot(value[:, :ch], wm[...]) + dot(value[:, ch:], wa[...])
    part_out[:, half:] = dot(value, tall_far(first, second, pair, 0, ch + nq))


def unmix_two_kernel(ch, nq, seg_row, seg_col, sums, pre, ys, dym, x_par, gtwo_out):
    tokens = sums.shape[0]
    base = sums.shape[1] - (ch + nq + LANES)
    low = iota((tokens, LANES), 1) < HEAD
    mask = masks(seg_row, seg_col, True)
    for p in range(ch // LANES):
        part = slice(p * LANES, (p + 1) * LANES)
        value = pre[:, part]
        xc = value * jax.nn.sigmoid(value)
        _, gate_turn = silu_turn(sums[:, base + p * LANES : base + (p + 1) * LANES])
        y = ys[:, part] + x_par[TAPS + 1 : TAPS + 2, part] * xc
        gtwo_out[:, part] = (dym[:, part] * y * gate_turn).astype(BF16)
    at = base + ch
    kv = sums[:, at + nq : at + nq + LANES]
    kv_turn = pltpu.roll(kv, HEAD, 1)
    keys = jnp.where(low, kv, kv_turn).astype(BF16)
    vals = jnp.where(low, kv_turn, kv).astype(BF16)
    dk = jnp.zeros((tokens, LANES), F32)
    dv = jnp.zeros((tokens, LANES), F32)
    for p in range(nq // LANES):
        query = sums[:, at + p * LANES : at + (p + 1) * LANES] * (HEAD ** -0.5)
        grad = dym[:, ch + p * LANES : ch + (p + 1) * LANES]
        dqs = []
        for side in (low, ~low):
            q_low = jnp.where(side, query, 0.0).astype(BF16)
            g_low = jnp.where(side, grad, 0.0).astype(BF16)
            score = dot_bt(keys, q_low) + mask
            score = jnp.exp(score - jnp.max(score, axis=0, keepdims=True))
            prob = score * (1.0 / jnp.sum(score, axis=0, keepdims=True))
            dprob = dot_bt(vals, g_low)
            dv = dv + dot(prob.astype(BF16), g_low)
            inner_sum = jnp.sum(prob * dprob, axis=0, keepdims=True)
            dscore = (prob * (dprob - inner_sum)).astype(BF16)
            dk = dk + dot(dscore, q_low)
            dqs.append(dot_at(dscore, keys))
        gtwo_out[:, ch + p * LANES : ch + (p + 1) * LANES] = (
            jnp.where(low, dqs[0], dqs[1]) * (HEAD ** -0.5)
        ).astype(BF16)
    dk = dk + pltpu.roll(dk, HEAD, 1)
    dv = dv + pltpu.roll(dv, HEAD, 1)
    gtwo_out[:, ch + nq : ch + nq + LANES] = jnp.where(low, dk, dv).astype(BF16)

def unmix_one_kernel(
    ch, nq, seg_row, seg_col, sums, pre, ys, dym, x_par, bc_par, head_par,
    gx_out, gdt_out, gbc_out, small_out, prod_a, prod_b, turned,
):
    tokens = sums.shape[0]
    nbc = bc_par.shape[1]
    state = nbc // 2
    lane = iota((tokens, LANES), 1)
    low = lane < HEAD
    mask = masks(seg_row, seg_col, True)
    valid = valids(seg_col)
    bc_pre = pre[:, ch : ch + nbc]
    bcc, bcc_turn = silu_turn(bc_pre)
    b_in = bcc[:, :state]
    c_in = bcc[:, state:]
    inner = fine(b_in, c_in, ((1,), (1,)))
    dt_raw = sums[:, ch + nbc : ch + nbc + LANES]
    dt = steps(dt_raw, head_par)
    rate = jnp.exp(head_par[1:2])
    tri = jnp.where(iota((tokens, tokens), 0) >= iota((tokens, tokens), 1), 1.0, 0.0)
    cum = fine(tri, dt * -rate)
    cum_row = cum.T
    base = ch + nbc + LANES
    small_out[...] = jnp.zeros_like(small_out)
    turned[...] = jnp.zeros_like(turned)
    for p in range(ch // LANES):
        part = slice(p * LANES, (p + 1) * LANES)
        xc, xc_turn = silu_turn(pre[:, part])
        skip = x_par[TAPS + 1 : TAPS + 2, part]
        z = sums[:, base + p * LANES : base + (p + 1) * LANES]
        gate = z * jax.nn.sigmoid(z)
        dy_in = dym[:, part]
        y = ys[:, part]
        dy = dy_in * gate
        h = 2 * p
        dt_pair = jnp.where(low, dt[:, h : h + 1], dt[:, h + 1 : h + 2])
        xdt = xc * dt_pair
        dy_low = dy.astype(BF16)
        x_low = xdt.astype(BF16)
        sides = []
        for e, side in ((h, low), (h + 1, ~low)):
            decay = jnp.exp((cum_row[e : e + 1] - cum[:, e : e + 1]) + mask)
            turned[...] += dot_bt(jnp.where(side, xdt, 0.0).astype(BF16), dy_low) * decay
            sides.append(dot((inner * decay).astype(BF16), dy_low))
        dxdt = jnp.where(low, sides[0], sides[1])
        prod_a[:, part] = dy_low.astype(F32) * y - x_low.astype(F32) * dxdt
        prod_b[:, part] = dxdt * xc
        small_out[8 + TAPS + 1 : 8 + TAPS + 2, part] = jnp.sum(dy * xc, axis=0, keepdims=True)
        dpre = (skip * dy + dxdt * dt_pair) * xc_turn
        back, rows = conv_turn(dpre, sums[:, part], x_par[0:TAPS, part], valid)
        gx_out[:, part] = back.astype(BF16)
        small_out[0:8, part] = rows
    pick = jnp.where(iota((ch, LANES), 0) // HEAD == iota((ch, LANES), 1), 1.0, 0.0)
    dcum = fine(prod_a[...], pick)
    ddt = fine(prod_b[...], pick)
    after = fine(tri, dcum, ((0,), (0,)))
    ddt = ddt - rate * after
    ddt = ddt * jax.nn.sigmoid(dt_raw + head_par[0:1])
    gdt_out[...] = ddt.astype(BF16)
    small_out[8 + TAPS : 8 + TAPS + 1, 0:LANES] = jnp.sum(ddt, axis=0, keepdims=True)
    small_out[8 + TAPS : 8 + TAPS + 1, LANES : 2 * LANES] = jnp.sum(
        after * (-dt * rate), axis=0, keepdims=True
    )
    skip_sum = jnp.broadcast_to(small_out[8 + TAPS + 1 : 8 + TAPS + 2, :], (8, ch))
    small_out[8 + TAPS : 8 + TAPS + 1, 2 * LANES : 3 * LANES] = fine(skip_sum, pick)[0:1]
    dinner = turned[...]
    d_b = fine(dinner, c_in) * bcc_turn[:, :state]
    d_c = fine(dinner, b_in, ((0,), (0,))) * bcc_turn[:, state:]
    for b, grad in enumerate((d_b, d_c)):
        at = ch + b * LANES
        part = slice(b * LANES, (b + 1) * LANES)
        back, rows = conv_turn(grad, sums[:, at : at + LANES], bc_par[0:TAPS, part], valid)
        gbc_out[0:tokens, part] = back
        gbc_out[tokens : tokens + 8, part] = rows


def tall_far(first, second, pair, start, size):
    return jnp.concatenate(
        [r[start : start + size] for r in (first, second, pair)], axis=1
    )


def norm_factor(value):
    return lax.rsqrt(jnp.mean(value * value, axis=1, keepdims=True) + NORM_EPS)


def act_grad_kernel(
    inner, place, mine, over_col, over_row, over_both, wd, first, second, pair,
    own_out, far_out, ga_out, far_tmp,
):
    gather_quarters(place, mine, over_col, over_row, over_both, own_out, far_out, far_tmp)
    ff = wd.shape[0]
    ga_out[...] = dot_bt(own_out[...], wd[...]) + dot_bt(
        far_out[...], tall_far(first, second, pair, inner, ff)
    )


def feed_kernel(
    place, own, far, part, came, gain, gu, gu_first, gu_second, gu_pair, grad_act, wd,
    h2_out, n2_out, act_out, ggu_out, n2p_out, keep_out, send_out,
):
    half = own.shape[1]
    quarter = half // 2
    piece = half // 4
    h2_out[:, :half] = own[...].astype(F32) + (part[:, :half] + came[:, :half])
    h2_out[:, half:] = far[...].astype(F32) + (part[:, half:] + came[:, half:])
    h2 = h2_out[...]
    n2 = (h2 * norm_factor(h2) * gain[...]).astype(BF16)
    n2_out[...] = n2[:, :half]
    gu_far = jnp.concatenate(
        [gu_first[...], gu_pair[0:piece], gu_second[...], gu_pair[piece:]], axis=0
    )
    ff = wd.shape[0]
    gate_up = dot(n2[:, :half], gu[...]) + dot(n2[:, half:], gu_far)
    gate = gate_up[:, :ff]
    up = gate_up[:, ff:]
    silu, silu_grad = silu_turn(gate)
    act = (silu * up).astype(BF16)
    act_out[...] = act
    ga = grad_act[...]
    ggu_out[:, :ff] = (ga * up * silu_grad).astype(BF16)
    ggu_out[:, ff:] = (ga * silu).astype(BF16)
    ggu = ggu_out[...]
    n2p_out[:, :half] = dot_bt(ggu, gu[...])
    n2p_out[:, half:] = dot_bt(ggu, gu_far)
    down = dot(act, wd[...])
    first = place[0] == 0
    keep_out[...] = jnp.where(first, down[:, :quarter], down[:, quarter:])
    send_out[...] = jnp.where(first, down[:, quarter:], down[:, :quarter])


def permuted(left, source):
    width = left.shape[1]
    hot = jnp.where(iota((width, source.shape[1]), 0) == source, 1.0, 0.0).astype(BF16)
    return dot(left, hot).astype(BF16)


def pair_grad(left, right, send_out, keep_out, at, cut, rows):
    size = right.shape[1]
    send_out[:, at : at + size] = dot_at(left[:, cut + rows : cut + 2 * rows], right).astype(BF16)
    keep_out[:, at : at + size] = dot_at(left[:, cut : cut + rows], right)


def feed_grad_kernel(n2, act, ggu, dy, order, order2, g_send, g_keep, d_send, d_keep):
    rows = g_keep.shape[0]
    width = dy.shape[1]
    pair_grad(permuted(n2[...], order[...]), ggu[...], g_send, g_keep, 0, 0, rows)
    left = permuted(act[...], order2[...])
    for s in (0, 1):
        pair_grad(left, dy[...], d_send, d_keep, s * width, 2 * s * rows, rows)


def turn_kernel(
    place, dy_own, dy_far, h2, part, came, gain, wm, wa, first, second, pair, d_keep, d_came,
    dym_out, resid_out, low_out, gain_out, output_out,
):
    half = dy_own.shape[1]
    quarter = half // 2
    ch = wm.shape[0]
    value = h2[...]
    output_out[...] = (
        jnp.where(place[0] == 0, value[:, :quarter], value[:, quarter:half])
        + (d_keep[...] + d_came[...])
    ).astype(BF16)
    factor = norm_factor(value)
    dn2 = part[...] + came[...]
    gained = dn2 * gain[...]
    inner_sum = jnp.sum(gained * value, axis=1, keepdims=True)
    gain_out[...] = jnp.broadcast_to(
        jnp.sum(dn2[:, :half] * value[:, :half] * factor, axis=0, keepdims=True), gain_out.shape
    )
    slope = factor * factor * factor * inner_sum / (2 * half)
    change = factor * gained - value * slope
    dh_own = dy_own[...].astype(F32) + change[:, :half]
    dh_far = dy_far[...].astype(F32) + change[:, half:]
    resid_out[...] = dh_own
    low_own = dh_own.astype(BF16)
    low_out[...] = low_own
    dym = dot_bt(dh_far.astype(BF16), tall_far(first, second, pair, 0, dym_out.shape[1]))
    dym_out[:, :ch] = dym[:, :ch] + dot_bt(low_own, wm[...])
    dym_out[:, ch:] = dym[:, ch:] + dot_bt(low_own, wa[...])


def mix_grad_kernel(mixed, low, order, send_out, keep_out):
    rows = keep_out.shape[0]
    width = low.shape[1]
    left = permuted(mixed[...], order[...])
    for s in (0, 1):
        pair_grad(left, low[...], send_out, keep_out, s * width, 2 * s * rows, rows)


def grad_two_kernel(n1, g_two, order, send_out, keep_out):
    pair_grad(permuted(n1[...], order[...]), g_two[...], send_out, keep_out, 0, 0, keep_out.shape[0])


def back_kernel(g_two, gx, gdt, both, wx, wb, wd, wg, wq, wk, n1p_out, n1b_out):
    ch = wg.shape[1]
    nq = wq.shape[1]
    total = dot_bt(gx[...], wx[...]) + dot_bt(gdt[...], wd[...])
    total = total + dot_bt(g_two[:, :ch], wg[...]) + dot_bt(g_two[:, ch : ch + nq], wq[...])
    n1p_out[...] = total + dot_bt(g_two[:, ch + nq :], wk[...])
    n1b_out[...] = dot_bt(both[...], wb[...])


def grad_one_kernel(n1, gx, gdt, gbc, gbc_came, order, send_out, keep_out, both_out):
    tokens = n1.shape[0]
    left = permuted(n1[...], order[...])
    both = (gbc[0:tokens] + gbc_came[0:tokens]).astype(BF16)
    both_out[...] = both
    at = 0
    for right in (gx[...], both, gdt[...]):
        pair_grad(left, right, send_out, keep_out, at, 0, keep_out.shape[0])
        at += right.shape[1]


def close_kernel(own, part, came, n1b, gain, gbc, gbc_came, dn1_out, rows_out):
    tokens = part.shape[0]
    dn1 = (part[...] + came[...]) + n1b[...]
    dn1_out[...] = dn1
    rows_out[0:8, :] = token_sums(dn1 * gain[...] * own[...].astype(F32))
    rows_out[8:16, :] = gbc[tokens:] + gbc_came[tokens:]


def end_kernel(
    place, own, factor1, resid, dn1, gain, rows, rows_far, small, gain2, hidden_out, vector_out
):
    half = dn1.shape[1]
    quarter = half // 2
    hid = own[...].astype(F32)
    factor = factor1[:, :1]
    inner_sum = column(rows[0:8] + rows_far[0:8])[:, :1]
    value = dn1[...]
    change = resid[...] + factor * (value * gain[...]) - hid * (
        factor * factor * factor * inner_sum / (2 * half)
    )
    hidden_out[...] = jnp.where(place[0] == 0, change[:, :quarter], change[:, quarter:])
    count = small.shape[0]
    vector_out[...] = jnp.zeros_like(vector_out)
    vector_out[0:count] = small[...]
    vector_out[count : count + 8, 0 : rows.shape[1]] = jnp.where(
        place[2] == 0, rows[8:16], rows_far[8:16]
    )
    vector_out[count + 8 : count + 9, 0:half] = jnp.sum(value * hid * factor, axis=0, keepdims=True)
    vector_out[count + 9 : count + 10, 0:half] = gain2[0:1]


def stage_kernel(keep, came, send_out, keep_out):
    rows = keep_out.shape[0]
    total = keep[...] + came[...].astype(F32)
    send_out[...] = total[rows:].astype(BF16)
    keep_out[...] = total[:rows]


def stage_sum_kernel(keep, came, vector, vector_came, send_out, keep_out, vector_out):
    stage_kernel(keep, came, send_out, keep_out)
    vector_out[...] = vector[...] + vector_came[...]


def last_kernel(keep, came, *outs):
    total = keep[...] + came[...].astype(F32)
    at = 0
    for out in outs:
        out[...] = total[:, at : at + out.shape[1]]
        at += out.shape[1]


def last_tall_kernel(keep, came, *outs):
    total = keep[...] + came[...].astype(F32)
    width = outs[0].shape[1]
    tall = jnp.concatenate([total[:, :width], total[:, width:]], axis=0)
    at = 0
    for out in outs:
        out[...] = tall[at : at + out.shape[0]]
        at += out.shape[0]


def halving_order(steps):
    order = [0]
    for step in reversed(steps):
        order = order + [o | step for o in order]
    return order


class Scatter:
    def __init__(self, run, steps, send, keep, last, outs, vector=None):
        self.run, self.steps, self.last, self.outs = run, steps, last, outs
        self.at, self.keep, self.vector = 0, keep, vector
        self.came = swap(send, "dp", steps[0])
        self.results = None

    def add_vector(self, vector):
        self.vector = vector
        self.vector_came = swap(vector, "dp", self.steps[0])

    def advance(self):
        if self.results is not None:
            return
        self.at += 1
        if self.at == len(self.steps):
            self.results = self.run(self.last, self.outs, self.keep, self.came)
            if self.vector is not None:
                self.vector = self.vector + self.vector_came
            return
        rows, cols = self.keep.shape
        outs = [((rows // 2, cols), BF16), ((rows // 2, cols), F32)]
        step = self.steps[self.at]
        if self.vector is None:
            send, self.keep = self.run(stage_kernel, outs, self.keep, self.came)
        else:
            send, self.keep, self.vector = self.run(
                stage_sum_kernel,
                outs + [(self.vector.shape, F32)],
                self.keep, self.came, self.vector, self.vector_came,
            )
            self.vector_came = swap(self.vector, "dp", step)
        self.came = swap(send, "dp", step)


def shards(
    hidden,
    segment_ids,
    norm1_gain,
    w_gate,
    w_xin,
    w_dt,
    w_bc,
    w_query,
    w_kv,
    convx_weight,
    convx_bias,
    convbc_weight,
    convbc_bias,
    dt_bias,
    a_log,
    d_skip,
    w_mixout,
    w_attnout,
    norm2_gain,
    w_gateup,
    w_down,
    cotangent,
):
    row = lax.axis_index("row")
    col = lax.axis_index("col")
    me = lax.axis_index("dp")
    count = lax.axis_size("dp")
    spot = me & 3
    place = jnp.stack([col, spot, row]).astype(jnp.int32)
    tokens, quarter = hidden.shape
    half = 2 * quarter
    full_width = 4 * quarter
    piece = half // 4
    ch = w_xin.shape[1]
    nq = w_query.shape[1]
    nkv = w_kv.shape[2]
    nbc = w_bc.shape[1]
    heads = w_dt.shape[1]
    ff = w_down.shape[0]
    cq = convx_bias.shape[0]
    hq = dt_bias.shape[0]

    run = Chain()
    cols = ch + nbc + LANES + ch + nq + nkv
    inner = ch + nq
    over_row = swap(hidden, "row")
    over_col = swap(hidden, "col")
    over_both = swap(over_row, "col")

    gu = w_gateup.reshape(half, 2 * ff)
    t_mine, g_mine, cot = run(
        pieces_kernel,
        [((inner + ff, piece), BF16), ((piece, 2 * ff), BF16), ((tokens, quarter), BF16)],
        place, w_mixout, w_attnout, w_down, gu, cotangent,
        smem=(0,), direct=True, after=(over_row,), scratch=[(pltpu.SemaphoreType.DMA((5,)), None)],
    )
    t_first = swap(t_mine, "row")
    g_first = swap(g_mine, "row")
    wk = w_kv.reshape(half, nkv)
    wd = jnp.pad(w_dt, ((0, 0), (0, LANES - heads)))
    gain_one = norm1_gain.astype(F32)[None]
    n1, part, part_low, own, far, factor1 = run(
        project_kernel,
        [
            ((tokens, half), BF16),
            ((tokens, cols), F32),
            ((tokens, cols), BF16),
            ((tokens, half), BF16),
            ((tokens, half), BF16),
            ((tokens, LANES), F32),
        ],
        place, hidden, over_col, over_row, over_both, gain_one, w_xin, w_bc, wd, w_gate, w_query, wk,
        smem=(0,), scratch=[((tokens, half), BF16)],
    )
    part_came = swap(part_low, "row")
    cot_row = swap(cot, "row")
    cot_col = swap(cot, "col")
    cot_both = swap(cot_row, "col")
    t_second = swap(t_first, "dp", 1)
    g_second = swap(g_first, "dp", 2)
    t_cat, g_cat = run(
        hop_kernel,
        [((inner + ff, 2 * piece), BF16), ((2 * piece, 2 * ff), BF16)],
        t_first, t_second, g_first, g_second,
    )
    t_pair = swap(t_cat, "dp", 2)
    g_pair = swap(g_cat, "dp", 1)

    small = jnp.concatenate(
        [convx_weight.T.reshape(-1), convx_bias, dt_bias, a_log, d_skip, norm2_gain]
    )
    small_far = swap(small, "row")

    def joined(start, size):
        a = small[start : start + size]
        b = small_far[start : start + size]
        first = row == 0
        return jnp.concatenate([jnp.where(first, a, b), jnp.where(first, b, a)], 0).astype(F32)

    at = TAPS * cq
    x_par = jnp.stack(
        [joined(k * cq, cq) for k in range(TAPS + 1)]
        + [jnp.repeat(joined(at + cq + 2 * hq, hq), HEAD)]
        + [jnp.zeros((ch,), F32)] * 2
    )
    bc_par = jnp.concatenate(
        [convbc_weight.T, convbc_bias[None], jnp.zeros((3, nbc), BF16)], 0
    ).astype(F32)
    head_par = jnp.stack(
        [jnp.pad(joined(at + cq + k * hq, hq), (0, LANES - heads)) for k in (0, 1)]
        + [jnp.zeros((LANES,), F32)] * 6
    )
    gain2_far = jnp.concatenate(
        [
            lax.dynamic_slice_in_dim(small_far, at + cq + 3 * hq + (spot ^ j) * piece, piece, 0)
            for j in range(4)
        ]
    )
    gain_two = jnp.concatenate([norm2_gain, gain2_far]).astype(F32)[None]
    seg_row = segment_ids.astype(F32)
    seg_col = jnp.broadcast_to(segment_ids[0].astype(F32)[:, None], (tokens, LANES))

    near = [1 << b for b in range(count.bit_length() - 1)]
    turned = [near[1], near[0]] + near[2:]
    size = half // count
    within = jnp.asarray(np.tile(np.arange(size), count), jnp.int32)
    both_within = jnp.concatenate([within, within + size])

    def block_order(steps):
        return jnp.asarray(np.repeat(np.array(halving_order(steps)), size), jnp.int32) ^ me

    near_block = block_order(near)
    turned_block = block_order(turned)
    order_near = (near_block * size + within)[None]
    order_turned = (turned_block * size + within)[None]
    order_down = (jnp.concatenate([turned_block] * 2) * (ff // count) + both_within)[None]
    m_rows = ch // count
    a_rows = nq // count
    near_both = jnp.concatenate([near_block] * 2)
    order_mix = jnp.where(
        both_within < m_rows,
        near_both * m_rows + both_within,
        ch + near_both * a_rows + both_within - m_rows,
    )[None]

    dy_own, dy_far, grad_act = run(
        lambda *refs: act_grad_kernel(inner, *refs),
        [((tokens, half), BF16), ((tokens, half), BF16), ((tokens, ff), F32)],
        place, cot, cot_col, cot_row, cot_both, w_down, t_first, t_second, t_pair,
        smem=(0,), scratch=[((tokens, half), BF16)],
    )
    mixed, raw, pre, ys, mix_part = run(
        lambda *refs: mix_kernel(ch, nq, *refs),
        [
            ((tokens, inner), BF16),
            ((tokens, cols), F32),
            ((tokens, ch + nbc), F32),
            ((tokens, ch), F32),
            ((tokens, full_width), F32),
        ],
        seg_row, seg_col, part, part_came, x_par, bc_par, head_par,
        w_mixout, w_attnout, t_first, t_second, t_pair,
    )
    h2, n2, act, ggu, n2_part, down_keep, down_send = run(
        feed_kernel,
        [
            ((tokens, full_width), F32),
            ((tokens, half), BF16),
            ((tokens, ff), BF16),
            ((tokens, 2 * ff), BF16),
            ((tokens, full_width), F32),
            ((tokens, quarter), F32),
            ((tokens, quarter), F32),
        ],
        place, own, far, mix_part, swap(mix_part, "col"), gain_two,
        gu, g_first, g_second, g_pair, grad_act, w_down,
        smem=(0,),
    )
    n2_came = swap(n2_part, "col")
    down_came = swap(down_send, "col")
    rows = half // 2

    def halves(width):
        return [((rows, width), BF16), ((rows, width), F32)]

    g_send, g_keep, d_send, d_keep = run(
        feed_grad_kernel, halves(2 * ff) + halves(2 * half), n2, act, ggu, dy_own, order_near, order_down
    )
    s_gu = Scatter(run, near, g_send, g_keep, last_kernel, [((size, 2 * ff), F32)])
    s_down = Scatter(
        run, turned, d_send, d_keep, last_tall_kernel, [((2 * size, half), F32)]
    )
    dym, resid, low, gain2_sum, output = run(
        turn_kernel,
        [
            ((tokens, inner), F32),
            ((tokens, half), F32),
            ((tokens, half), BF16),
            ((8, half), F32),
            ((tokens, quarter), BF16),
        ],
        place, dy_own, dy_far, h2, n2_part, n2_came, gain_two,
        w_mixout, w_attnout, t_first, t_second, t_pair, down_keep, down_came,
        smem=(0,),
    )
    g_two = run(
        lambda *refs: unmix_two_kernel(ch, nq, *refs),
        [((tokens, ch + nq + nkv), BF16)],
        seg_row, seg_col, raw, pre, ys, dym, x_par,
    )[0]
    two_send, two_keep = run(grad_two_kernel, halves(ch + nq + nkv), n1, g_two, order_near)
    s_two = Scatter(
        run, near, two_send, two_keep, last_kernel,
        [((size, ch), F32), ((size, nq), F32), ((size, nkv), F32)],
    )
    s_down.advance()
    gx, gdt, gbc, small_sum = run(
        lambda *refs: unmix_one_kernel(ch, nq, *refs),
        [
            ((tokens, ch), BF16),
            ((tokens, LANES), BF16),
            ((tokens + 8, nbc), F32),
            ((16, ch), F32),
        ],
        seg_row, seg_col, raw, pre, ys, dym, x_par, bc_par, head_par,
        scratch=[((tokens, ch), F32), ((tokens, ch), F32), ((tokens, tokens), F32)],
    )
    gbc_came = swap(gbc, "col")
    m_send, m_keep = run(mix_grad_kernel, halves(2 * half), mixed, low, order_mix)
    s_mix = Scatter(
        run, near, m_send, m_keep, last_tall_kernel,
        [((m_rows, half), F32), ((a_rows, half), F32)],
    )
    one_send, one_keep, gbc_both = run(
        grad_one_kernel,
        halves(ch + nbc + LANES) + [((tokens, nbc), BF16)],
        n1, gx, gdt, gbc, gbc_came, order_turned,
    )
    s_one = Scatter(
        run, turned, one_send, one_keep, last_kernel,
        [((size, ch), F32), ((size, nbc), F32), ((size, LANES), F32)],
    )
    s_gu.advance()
    n1_part, n1_bc = run(
        back_kernel,
        [((tokens, half), F32), ((tokens, half), F32)],
        g_two, gx, gdt, gbc_both, w_xin, w_bc, wd, w_gate, w_query, wk,
    )
    n1_came = swap(n1_part, "col")
    s_two.advance()
    dn1, sum_rows = run(
        close_kernel,
        [((tokens, half), F32), ((16, tokens), F32)],
        own, n1_part, n1_came, n1_bc, gain_one, gbc, gbc_came,
    )
    rows_far = swap(sum_rows, "row")
    s_gu.advance()
    s_down.advance()
    grad_hidden, vector = run(
        end_kernel,
        [((tokens, quarter), F32), ((32, ch), F32)],
        place, own, factor1, resid, dn1, gain_one, sum_rows, rows_far, small_sum, gain2_sum,
        smem=(0,),
    )
    s_one.add_vector(vector)
    s_one.advance()
    s_mix.advance()
    scatters = (s_two, s_gu, s_down, s_one, s_mix)
    while any(s.results is None for s in scatters):
        for s in scatters:
            s.advance()
    vector = s_one.vector
    r_gate, r_query, r_kv = s_two.results
    r_xin, r_bc, r_dt = s_one.results
    r_mixout, r_attnout = s_mix.results

    def mine(values, width):
        return lax.dynamic_slice_in_dim(values, row * width, width, values.ndim - 1)

    return (
        output,
        grad_hidden,
        vector[24, :half],
        r_gate,
        r_xin,
        r_dt[:, :heads],
        r_bc,
        r_query,
        r_kv.reshape(size, 1, nkv),
        mine(vector[0:TAPS], cq).T,
        mine(vector[TAPS], cq),
        vector[16 : 16 + TAPS, :nbc].T,
        vector[16 + TAPS, :nbc],
        mine(vector[12, :heads], hq),
        mine(vector[12, LANES : LANES + heads], hq),
        mine(vector[12, 2 * LANES : 2 * LANES + heads], hq),
        r_mixout,
        r_attnout,
        vector[25, :half],
        s_gu.results[0].reshape(size, 2, ff),
        s_down.results[0],
    )


def solution(mesh):
    placed = (
        P("dp", ("row", "col")),
        P("dp", None),
        P("row"),
        P("row", "col"),
        P("row", "col"),
        P("row", "col"),
        P("row", None),
        P("row", "col"),
        P("row", "col", None),
        P(("col", "row"), None),
        P(("col", "row")),
        P(),
        P(),
        P(("col", "row")),
        P(("col", "row")),
        P(("col", "row")),
        P("col", "row"),
        P("col", "row"),
        P("row"),
        P("row", None, "col"),
        P("col", "row"),
        P("dp", ("row", "col")),
    )
    return jax.shard_map(
        shards,
        mesh=mesh,
        in_specs=placed,
        out_specs=(
            P("dp", ("row", "col")),
            P("dp", ("row", "col")),
            P("row"),
            P(("row", "dp"), "col"),
            P(("row", "dp"), "col"),
            P(("row", "dp"), "col"),
            P(("row", "dp"), None),
            P(("row", "dp"), "col"),
            P(("row", "dp"), "col", None),
            P(("col", "row"), None),
            P(("col", "row")),
            P(),
            P(),
            P(("col", "row")),
            P(("col", "row")),
            P(("col", "row")),
            P(("col", "dp"), "row"),
            P(("col", "dp"), "row"),
            P("row"),
            P(("row", "dp"), None, "col"),
            P(("col", "dp"), "row"),
        ),
        check_vma=False,
    )
```

```python
import jax
import jax.numpy as jnp
import numpy as np
from jax import lax
from jax.experimental import pallas as pl
from jax.experimental.pallas import tpu as pltpu
from jax.sharding import PartitionSpec as P

NORM_EPS = 1e-05
F32 = jnp.float32
BF16 = jnp.bfloat16
HEAD = 64
LANES = 128
TAPS = 4
FAR = -1e30


def swap(values, axis, step=1):
    count = lax.axis_size(axis)
    return lax.ppermute(values, axis, [(i, i ^ step) for i in range(count)])


def dot(left, right):
    return jnp.dot(left, right, preferred_element_type=F32)


def dot_bt(left, right):
    return lax.dot_general(left, right, (((1,), (1,)), ((), ())), preferred_element_type=F32)


def dot_at(left, right):
    return lax.dot_general(left, right, (((0,), (0,)), ((), ())), preferred_element_type=F32)


def fine(left, right, dims=((1,), (0,))):
    return lax.dot_general(
        left, right, (dims, ((), ())), precision=lax.Precision.HIGHEST, preferred_element_type=F32
    )


class Chain:
    def __init__(self):
        self.token = jnp.zeros((8, LANES), F32)

    def __call__(self, kernel, outs, *args, scratch=(), smem=(), direct=False, after=(), alias=None):
        plain = pl.ANY if direct else pltpu.VMEM
        specs = [
            pl.BlockSpec(memory_space=pltpu.SMEM if i in smem else plain)
            for i in range(len(args))
        ]
        extra = (self.token,) + tuple(after)
        count = len(args)
        held = count + len(extra)

        def body(*refs):
            refs[held][...] = jnp.zeros((8, LANES), F32)
            kernel(*refs[:count], *refs[held + 1 :])

        results = pl.pallas_call(
            body,
            out_shape=[jax.ShapeDtypeStruct((8, LANES), F32)]
            + [jax.ShapeDtypeStruct(s, d) for s, d in outs],
            in_specs=specs + [pl.BlockSpec(memory_space=pl.ANY)] * len(extra),
            out_specs=[pl.BlockSpec(memory_space=pltpu.VMEM)]
            + [pl.BlockSpec(memory_space=plain)] * len(outs),
            scratch_shapes=[pltpu.VMEM(s, d) if d is not None else s for s, d in scratch],
            compiler_params=pltpu.CompilerParams(vmem_limit_bytes=56 << 20),
            cost_estimate=pl.CostEstimate(flops=0, bytes_accessed=0, transcendentals=0),
            input_output_aliases=alias or {},
        )(*args, *extra)
        self.token = results[0]
        return results[1:]

    def touch(self, value):
        return self(
            lambda *refs: None, [(value.shape, value.dtype)], value, direct=True, alias={0: 1}
        )[0]


def iota(shape, dim):
    return lax.broadcasted_iota(jnp.int32, shape, dim)


def column(row_vector):
    ones = jnp.full((row_vector.shape[0], LANES), 1.0 / row_vector.shape[0], F32)
    return fine(row_vector, ones, ((0,), (0,)))


def token_sums(values):
    return fine(jnp.ones((8, values.shape[1]), F32), values, ((1,), (1,)))


def pieces_kernel(place, wm, wa, wd, cot, hid, out):
    piece = out.shape[1]
    at = pl.multiple_of(place[1] * piece, piece)
    row = 0
    for w in (wm, wa, wd):
        out[row : row + w.shape[0]] = w[:, pl.ds(at, piece)]
        row += w.shape[0]
    for value in (cot, hid):
        for j in range(value.shape[1] // piece):
            out[row : row + value.shape[0]] = value[:, j * piece : (j + 1) * piece]
            row += value.shape[0]


def split_kernel(got, cot, hid, first_out, pair_out):
    size = first_out.shape[0]
    tokens = cot.shape[0]
    piece = got.shape[1]
    first_out[...] = got[0:size]
    for i, value in enumerate((cot, hid)):
        at = 2 * i * tokens
        pair_out[at : at + tokens] = value[...]
        for j in range(value.shape[1] // piece):
            pair_out[at + tokens : at + 2 * tokens, j * piece : (j + 1) * piece] = got[
                size + at + j * tokens : size + at + (j + 1) * tokens
            ]


def gather_quarters(place, mine, came, at, own_out, far_out, far_tmp):
    width = own_out.shape[1] // 2
    piece = width // 2
    first = place[0] == 0
    tokens = own_out.shape[0]
    for i, out in enumerate((own_out, far_tmp)):
        rows = slice((at + i) * tokens, (at + i + 1) * tokens)
        a = mine[rows]
        b = came[rows]
        out[:, :width] = jnp.where(first, a, b)
        out[:, width:] = jnp.where(first, b, a)
    for j in range(4):
        at = pl.multiple_of((place[1] ^ j) * piece, piece)
        far_out[:, j * piece : (j + 1) * piece] = far_tmp[:, pl.ds(at, piece)]


def project_kernel(
    place, mine, came, gain, wx, wb, wd, wg, wq, wk,
    n1_out, p_out, low_out, own_out, far_out, factor_out, far_tmp,
):
    gather_quarters(place, mine, came, 2, own_out, far_out, far_tmp)
    own = own_out[...].astype(F32)
    far = far_tmp[...].astype(F32)
    mean = jnp.sum(own * own + far * far, axis=1, keepdims=True) / (2 * own.shape[1])
    factor = lax.rsqrt(mean + NORM_EPS)
    factor_out[...] = jnp.broadcast_to(factor, factor_out.shape)
    n1 = (own * factor * gain[...]).astype(BF16)
    n1_out[...] = n1
    at = 0
    for w in (wx, wb, wd, wg, wq, wk):
        size = w.shape[1]
        part = dot(n1, w[...])
        p_out[:, at : at + size] = part
        low_out[:, at : at + size] = part.astype(BF16)
        at += size


def hop_kernel(t_first, t_second, g_first, g_second, t_out, g_out):
    t_piece = t_first.shape[1]
    g_piece = g_first.shape[0]
    t_out[:, :t_piece] = t_first[...]
    t_out[:, t_piece:] = t_second[...]
    g_out[:g_piece] = g_first[...]
    g_out[g_piece:] = g_second[...]


def masks(seg_row, seg_col, turned):
    tokens = seg_row.shape[1]
    i = iota((tokens, tokens), 1 if turned else 0)
    j = iota((tokens, tokens), 0 if turned else 1)
    same = seg_col[:, :1] == seg_row[...]
    return jnp.where((i >= j) & same, 0.0, FAR)


def valids(seg_col):
    seg = seg_col[...]
    t = iota(seg.shape, 0)
    return [
        jnp.where((t >= k) & (pltpu.roll(seg, k, 0) == seg), 1.0, 0.0) for k in range(1, TAPS)
    ]


def conv(block, taps, bias, valid):
    total = block * taps[TAPS - 1 : TAPS] + bias
    for k in range(1, TAPS):
        total = total + (pltpu.roll(block, k, 0) * valid[k - 1]) * taps[TAPS - 1 - k : TAPS - k]
    return total


def conv_turn(grad, block, taps, valid):
    tokens = grad.shape[0]
    back = grad * taps[TAPS - 1 : TAPS]
    rows = [None] * TAPS
    rows[TAPS - 1] = jnp.sum(grad * block, axis=0, keepdims=True)
    for k in range(1, TAPS):
        kept = grad * valid[k - 1]
        back = back + pltpu.roll(kept, tokens - k, 0) * taps[TAPS - 1 - k : TAPS - k]
        rows[TAPS - 1 - k] = jnp.sum(kept * pltpu.roll(block, k, 0), axis=0, keepdims=True)
    rows.append(jnp.sum(grad, axis=0, keepdims=True))
    rows.append(jnp.zeros((8 - len(rows), grad.shape[1]), F32))
    return back, jnp.concatenate(rows, 0)


def silu_turn(value):
    sig = jax.nn.sigmoid(value)
    return value * sig, sig * (1.0 + value * (1.0 - sig))


def steps(dt_raw, head_par):
    shifted = dt_raw + head_par[0:1]
    return jnp.maximum(shifted, 0.0) + jnp.log1p(jnp.exp(-jnp.abs(shifted)))


def mix_kernel(
    ch, nq, seg_row, seg_col, own, came, x_par, bc_par, head_par,
    mixed_out, sums_out, pre_out, y_out,
):
    tokens = own.shape[0]
    nbc = bc_par.shape[1]
    state = nbc // 2
    sums_out[...] = own[...] + came[...].astype(F32)
    lane = iota((tokens, LANES), 1)
    low = lane < HEAD
    mask = masks(seg_row, seg_col, False)
    valid = valids(seg_col)
    for b in range(nbc // LANES):
        at = ch + b * LANES
        part = slice(b * LANES, (b + 1) * LANES)
        pre_out[:, at : at + LANES] = conv(
            sums_out[:, at : at + LANES], bc_par[0:TAPS, part], bc_par[TAPS : TAPS + 1, part], valid
        )
    bcc = pre_out[:, ch : ch + nbc]
    bcc = bcc * jax.nn.sigmoid(bcc)
    inner = fine(bcc[:, state:], bcc[:, :state], ((1,), (1,)))
    dt = steps(sums_out[:, ch + nbc : ch + nbc + LANES], head_par)
    tri = jnp.where(iota((tokens, tokens), 0) >= iota((tokens, tokens), 1), 1.0, 0.0)
    cum = fine(tri, dt * -jnp.exp(head_par[1:2]))
    cum_row = cum.T
    base = ch + nbc + LANES
    for p in range(ch // LANES):
        part = slice(p * LANES, (p + 1) * LANES)
        pre = conv(sums_out[:, part], x_par[0:TAPS, part], x_par[TAPS : TAPS + 1, part], valid)
        pre_out[:, part] = pre
        xc = pre * jax.nn.sigmoid(pre)
        h = 2 * p
        xdt = (xc * jnp.where(low, dt[:, h : h + 1], dt[:, h + 1 : h + 2])).astype(BF16)
        ys = []
        for e in (h, h + 1):
            decay = jnp.exp((cum[:, e : e + 1] - cum_row[e : e + 1]) + mask)
            ys.append(dot((inner * decay).astype(BF16), xdt))
        y = jnp.where(low, ys[0], ys[1])
        y_out[:, part] = y
        y = y + x_par[TAPS + 1 : TAPS + 2, part] * xc
        z = sums_out[:, base + p * LANES : base + (p + 1) * LANES]
        mixed_out[:, part] = (y * (z * jax.nn.sigmoid(z))).astype(BF16)
    at = base + ch
    kv = sums_out[:, at + nq : at + nq + LANES].astype(BF16)
    kv_turn = pltpu.roll(sums_out[:, at + nq : at + nq + LANES], HEAD, 1).astype(BF16)
    keys = jnp.where(low, kv, kv_turn)
    vals = jnp.where(low, kv_turn, kv)
    for p in range(nq // LANES):
        query = sums_out[:, at + p * LANES : at + (p + 1) * LANES] * (HEAD ** -0.5)
        outs = []
        for side in (low, ~low):
            score = dot_bt(jnp.where(side, query, 0.0).astype(BF16), keys) + mask
            score = jnp.exp(score - jnp.max(score, axis=1, keepdims=True))
            total = jnp.sum(score, axis=1, keepdims=True)
            outs.append(dot(score.astype(BF16), vals) / total)
        mixed_out[:, ch + p * LANES : ch + (p + 1) * LANES] = jnp.where(
            low, outs[0], outs[1]
        ).astype(BF16)


def unmix_two_kernel(ch, nq, seg_row, seg_col, sums, pre, ys, dym, x_par, gtwo_out):
    tokens = sums.shape[0]
    base = sums.shape[1] - (ch + nq + LANES)
    low = iota((tokens, LANES), 1) < HEAD
    mask = masks(seg_row, seg_col, True)
    for p in range(ch // LANES):
        part = slice(p * LANES, (p + 1) * LANES)
        value = pre[:, part]
        xc = value * jax.nn.sigmoid(value)
        _, gate_turn = silu_turn(sums[:, base + p * LANES : base + (p + 1) * LANES])
        y = ys[:, part] + x_par[TAPS + 1 : TAPS + 2, part] * xc
        gtwo_out[:, part] = (dym[:, part] * y * gate_turn).astype(BF16)
    at = base + ch
    kv = sums[:, at + nq : at + nq + LANES]
    kv_turn = pltpu.roll(kv, HEAD, 1)
    keys = jnp.where(low, kv, kv_turn).astype(BF16)
    vals = jnp.where(low, kv_turn, kv).astype(BF16)
    dk = jnp.zeros((tokens, LANES), F32)
    dv = jnp.zeros((tokens, LANES), F32)
    for p in range(nq // LANES):
        query = sums[:, at + p * LANES : at + (p + 1) * LANES] * (HEAD ** -0.5)
        grad = dym[:, ch + p * LANES : ch + (p + 1) * LANES]
        dqs = []
        for side in (low, ~low):
            q_low = jnp.where(side, query, 0.0).astype(BF16)
            g_low = jnp.where(side, grad, 0.0).astype(BF16)
            score = dot_bt(keys, q_low) + mask
            score = jnp.exp(score - jnp.max(score, axis=0, keepdims=True))
            prob = score * (1.0 / jnp.sum(score, axis=0, keepdims=True))
            dprob = dot_bt(vals, g_low)
            dv = dv + dot(prob.astype(BF16), g_low)
            inner_sum = jnp.sum(prob * dprob, axis=0, keepdims=True)
            dscore = (prob * (dprob - inner_sum)).astype(BF16)
            dk = dk + dot(dscore, q_low)
            dqs.append(dot_at(dscore, keys))
        gtwo_out[:, ch + p * LANES : ch + (p + 1) * LANES] = (
            jnp.where(low, dqs[0], dqs[1]) * (HEAD ** -0.5)
        ).astype(BF16)
    dk = dk + pltpu.roll(dk, HEAD, 1)
    dv = dv + pltpu.roll(dv, HEAD, 1)
    gtwo_out[:, ch + nq : ch + nq + LANES] = jnp.where(low, dk, dv).astype(BF16)

def unmix_one_kernel(
    ch, nq, seg_row, seg_col, sums, pre, ys, dym, x_par, bc_par, head_par,
    gx_out, gdt_out, gbc_out, small_out, prod_a, prod_b, turned,
):
    tokens = sums.shape[0]
    nbc = bc_par.shape[1]
    state = nbc // 2
    lane = iota((tokens, LANES), 1)
    low = lane < HEAD
    mask = masks(seg_row, seg_col, True)
    valid = valids(seg_col)
    bc_pre = pre[:, ch : ch + nbc]
    bcc, bcc_turn = silu_turn(bc_pre)
    b_in = bcc[:, :state]
    c_in = bcc[:, state:]
    inner = fine(b_in, c_in, ((1,), (1,)))
    dt_raw = sums[:, ch + nbc : ch + nbc + LANES]
    dt = steps(dt_raw, head_par)
    rate = jnp.exp(head_par[1:2])
    tri = jnp.where(iota((tokens, tokens), 0) >= iota((tokens, tokens), 1), 1.0, 0.0)
    cum = fine(tri, dt * -rate)
    cum_row = cum.T
    base = ch + nbc + LANES
    small_out[...] = jnp.zeros_like(small_out)
    turned[...] = jnp.zeros_like(turned)
    for p in range(ch // LANES):
        part = slice(p * LANES, (p + 1) * LANES)
        xc, xc_turn = silu_turn(pre[:, part])
        skip = x_par[TAPS + 1 : TAPS + 2, part]
        z = sums[:, base + p * LANES : base + (p + 1) * LANES]
        gate = z * jax.nn.sigmoid(z)
        dy_in = dym[:, part]
        y = ys[:, part]
        dy = dy_in * gate
        h = 2 * p
        dt_pair = jnp.where(low, dt[:, h : h + 1], dt[:, h + 1 : h + 2])
        xdt = xc * dt_pair
        dy_low = dy.astype(BF16)
        x_low = xdt.astype(BF16)
        sides = []
        for e, side in ((h, low), (h + 1, ~low)):
            decay = jnp.exp((cum_row[e : e + 1] - cum[:, e : e + 1]) + mask)
            turned[...] += dot_bt(jnp.where(side, xdt, 0.0).astype(BF16), dy_low) * decay
            sides.append(dot((inner * decay).astype(BF16), dy_low))
        dxdt = jnp.where(low, sides[0], sides[1])
        prod_a[:, part] = dy_low.astype(F32) * y - x_low.astype(F32) * dxdt
        prod_b[:, part] = dxdt * xc
        small_out[8 + TAPS + 1 : 8 + TAPS + 2, part] = jnp.sum(dy * xc, axis=0, keepdims=True)
        dpre = (skip * dy + dxdt * dt_pair) * xc_turn
        back, rows = conv_turn(dpre, sums[:, part], x_par[0:TAPS, part], valid)
        gx_out[:, part] = back.astype(BF16)
        small_out[0:8, part] = rows
    pick = jnp.where(iota((ch, LANES), 0) // HEAD == iota((ch, LANES), 1), 1.0, 0.0)
    dcum = fine(prod_a[...], pick)
    ddt = fine(prod_b[...], pick)
    after = fine(tri, dcum, ((0,), (0,)))
    ddt = ddt - rate * after
    ddt = ddt * jax.nn.sigmoid(dt_raw + head_par[0:1])
    gdt_out[...] = ddt.astype(BF16)
    small_out[8 + TAPS : 8 + TAPS + 1, 0:LANES] = jnp.sum(ddt, axis=0, keepdims=True)
    small_out[8 + TAPS : 8 + TAPS + 1, LANES : 2 * LANES] = jnp.sum(
        after * (-dt * rate), axis=0, keepdims=True
    )
    skip_sum = jnp.broadcast_to(small_out[8 + TAPS + 1 : 8 + TAPS + 2, :], (8, ch))
    small_out[8 + TAPS : 8 + TAPS + 1, 2 * LANES : 3 * LANES] = fine(skip_sum, pick)[0:1]
    dinner = turned[...]
    d_b = fine(dinner, c_in) * bcc_turn[:, :state]
    d_c = fine(dinner, b_in, ((0,), (0,))) * bcc_turn[:, state:]
    for b, grad in enumerate((d_b, d_c)):
        at = ch + b * LANES
        part = slice(b * LANES, (b + 1) * LANES)
        back, rows = conv_turn(grad, sums[:, at : at + LANES], bc_par[0:TAPS, part], valid)
        gbc_out[0:tokens, part] = back
        gbc_out[tokens : tokens + 8, part] = rows


def tall_far(first, second, pair, start, size):
    return jnp.concatenate(
        [r[start : start + size] for r in (first, second, pair)], axis=1
    )


def out_kernel(mixed, wm, wa, first, second, pair, part_out):
    half = wm.shape[1]
    ch = wm.shape[0]
    value = mixed[...]
    part_out[:, :half] = dot(value[:, :ch], wm[...]) + dot(value[:, ch:], wa[...])
    part_out[:, half:] = dot(value, tall_far(first, second, pair, 0, value.shape[1]))


def norm_factor(value):
    return lax.rsqrt(jnp.mean(value * value, axis=1, keepdims=True) + NORM_EPS)


def act_grad_kernel(
    inner, place, mine, came, wd, first, second, pair, own_out, far_out, ga_out, far_tmp
):
    gather_quarters(place, mine, came, 0, own_out, far_out, far_tmp)
    ff = wd.shape[0]
    ga_out[...] = dot_bt(own_out[...], wd[...]) + dot_bt(
        far_out[...], tall_far(first, second, pair, inner, ff)
    )


def feed_kernel(
    place, own, far, part, came, gain, gu, gu_first, gu_second, gu_pair, grad_act, wd,
    h2_out, n2_out, act_out, ggu_out, n2p_out, keep_out, send_out,
):
    half = own.shape[1]
    quarter = half // 2
    piece = half // 4
    h2_out[:, :half] = own[...].astype(F32) + (part[:, :half] + came[:, :half])
    h2_out[:, half:] = far[...].astype(F32) + (part[:, half:] + came[:, half:])
    h2 = h2_out[...]
    n2 = (h2 * norm_factor(h2) * gain[...]).astype(BF16)
    n2_out[...] = n2[:, :half]
    gu_far = jnp.concatenate(
        [gu_first[...], gu_pair[0:piece], gu_second[...], gu_pair[piece:]], axis=0
    )
    ff = wd.shape[0]
    gate_up = dot(n2[:, :half], gu[...]) + dot(n2[:, half:], gu_far)
    gate = gate_up[:, :ff]
    up = gate_up[:, ff:]
    silu, silu_grad = silu_turn(gate)
    act = (silu * up).astype(BF16)
    act_out[...] = act
    ga = grad_act[...]
    ggu_out[:, :ff] = (ga * up * silu_grad).astype(BF16)
    ggu_out[:, ff:] = (ga * silu).astype(BF16)
    ggu = ggu_out[...]
    n2p_out[:, :half] = dot_bt(ggu, gu[...])
    n2p_out[:, half:] = dot_bt(ggu, gu_far)
    down = dot(act, wd[...])
    first = place[0] == 0
    keep_out[...] = jnp.where(first, down[:, :quarter], down[:, quarter:])
    send_out[...] = jnp.where(first, down[:, quarter:], down[:, :quarter])


def permuted(left, source):
    width = left.shape[1]
    hot = jnp.where(iota((width, source.shape[1]), 0) == source, 1.0, 0.0).astype(BF16)
    return dot(left, hot).astype(BF16)


def pair_grad(left, right, send_out, keep_out, at, cut, rows):
    size = right.shape[1]
    send_out[:, at : at + size] = dot_at(left[:, cut + rows : cut + 2 * rows], right).astype(BF16)
    keep_out[:, at : at + size] = dot_at(left[:, cut : cut + rows], right)


def feed_grad_kernel(n2, act, ggu, dy, order, order2, g_send, g_keep, d_send, d_keep):
    rows = g_keep.shape[0]
    width = dy.shape[1]
    pair_grad(permuted(n2[...], order[...]), ggu[...], g_send, g_keep, 0, 0, rows)
    left = permuted(act[...], order2[...])
    for s in (0, 1):
        pair_grad(left, dy[...], d_send, d_keep, s * width, 2 * s * rows, rows)


def turn_kernel(
    place, dy_own, dy_far, h2, part, came, gain, wm, wa, first, second, pair, d_keep, d_came,
    dym_out, resid_out, low_out, gain_out, output_out,
):
    half = dy_own.shape[1]
    quarter = half // 2
    ch = wm.shape[0]
    value = h2[...]
    output_out[...] = (
        jnp.where(place[0] == 0, value[:, :quarter], value[:, quarter:half])
        + (d_keep[...] + d_came[...])
    ).astype(BF16)
    factor = norm_factor(value)
    dn2 = part[...] + came[...]
    gained = dn2 * gain[...]
    inner_sum = jnp.sum(gained * value, axis=1, keepdims=True)
    gain_out[...] = jnp.broadcast_to(
        jnp.sum(dn2[:, :half] * value[:, :half] * factor, axis=0, keepdims=True), gain_out.shape
    )
    slope = factor * factor * factor * inner_sum / (2 * half)
    change = factor * gained - value * slope
    dh_own = dy_own[...].astype(F32) + change[:, :half]
    dh_far = dy_far[...].astype(F32) + change[:, half:]
    resid_out[...] = dh_own
    low_own = dh_own.astype(BF16)
    low_out[...] = low_own
    dym = dot_bt(dh_far.astype(BF16), tall_far(first, second, pair, 0, dym_out.shape[1]))
    dym_out[:, :ch] = dym[:, :ch] + dot_bt(low_own, wm[...])
    dym_out[:, ch:] = dym[:, ch:] + dot_bt(low_own, wa[...])


def mix_grad_kernel(mixed, low, order, send_out, keep_out):
    rows = keep_out.shape[0]
    width = low.shape[1]
    left = permuted(mixed[...], order[...])
    for s in (0, 1):
        pair_grad(left, low[...], send_out, keep_out, s * width, 2 * s * rows, rows)


def grad_two_kernel(n1, g_two, order, send_out, keep_out):
    pair_grad(permuted(n1[...], order[...]), g_two[...], send_out, keep_out, 0, 0, keep_out.shape[0])


def back_kernel(
    g_two, gx, gdt, gbc, gbc_came, wx, wb, wd, wg, wq, wk, n1p_out, n1b_out, both_out
):
    tokens = gx.shape[0]
    both = (gbc[0:tokens] + gbc_came[0:tokens]).astype(BF16)
    both_out[...] = both
    ch = wg.shape[1]
    nq = wq.shape[1]
    total = dot_bt(gx[...], wx[...]) + dot_bt(gdt[...], wd[...])
    total = total + dot_bt(g_two[:, :ch], wg[...]) + dot_bt(g_two[:, ch : ch + nq], wq[...])
    n1p_out[...] = total + dot_bt(g_two[:, ch + nq :], wk[...])
    n1b_out[...] = dot_bt(both, wb[...])


def grad_one_kernel(n1, gx, gdt, both, order, send_out, keep_out):
    left = permuted(n1[...], order[...])
    at = 0
    for right in (gx[...], both[...], gdt[...]):
        pair_grad(left, right, send_out, keep_out, at, 0, keep_out.shape[0])
        at += right.shape[1]


def close_kernel(own, part, came, n1b, gain, gbc, gbc_came, dn1_out, rows_out):
    tokens = part.shape[0]
    dn1 = (part[...] + came[...]) + n1b[...]
    dn1_out[...] = dn1
    rows_out[0:8, :] = token_sums(dn1 * gain[...] * own[...].astype(F32))
    rows_out[8:16, :] = gbc[tokens:] + gbc_came[tokens:]


def end_kernel(
    place, own, factor1, resid, dn1, gain, rows, rows_far, small, gain2, hidden_out, vector_out
):
    half = dn1.shape[1]
    quarter = half // 2
    hid = own[...].astype(F32)
    factor = factor1[:, :1]
    inner_sum = column(rows[0:8] + rows_far[0:8])[:, :1]
    value = dn1[...]
    change = resid[...] + factor * (value * gain[...]) - hid * (
        factor * factor * factor * inner_sum / (2 * half)
    )
    hidden_out[...] = jnp.where(place[0] == 0, change[:, :quarter], change[:, quarter:])
    count = small.shape[0]
    vector_out[...] = jnp.zeros_like(vector_out)
    vector_out[0:count] = small[...]
    vector_out[count : count + 8, 0 : rows.shape[1]] = jnp.where(
        place[2] == 0, rows[8:16], rows_far[8:16]
    )
    vector_out[count + 8 : count + 9, 0:half] = jnp.sum(value * hid * factor, axis=0, keepdims=True)
    vector_out[count + 9 : count + 10, 0:half] = gain2[0:1]


def stage_kernel(keep, came, send_out, keep_out):
    rows = keep_out.shape[0]
    total = keep[...] + came[...].astype(F32)
    send_out[...] = total[rows:].astype(BF16)
    keep_out[...] = total[:rows]


def stage_sum_kernel(keep, came, vector, vector_came, send_out, keep_out, vector_out):
    stage_kernel(keep, came, send_out, keep_out)
    vector_out[...] = vector[...] + vector_came[...]


def join_kernel(keep_a, came_a, keep_b, came_b, send_out, keep_out):
    rows, width = keep_out.shape
    width = width // 2
    for i, (keep, came) in enumerate(((keep_a, came_a), (keep_b, came_b))):
        total = keep[...] + came[...].astype(F32)
        send_out[:, i * width : (i + 1) * width] = total[rows:].astype(BF16)
        keep_out[:, i * width : (i + 1) * width] = total[:rows]


def last_kernel(keep, came, *outs):
    total = keep[...] + came[...].astype(F32)
    at = 0
    for out in outs:
        out[...] = total[:, at : at + out.shape[1]]
        at += out.shape[1]


def last_tall_kernel(keep, came, *outs):
    total = keep[...] + came[...].astype(F32)
    width = outs[0].shape[1]
    outs[0][...] = jnp.concatenate([total[:, :width], total[:, width : 2 * width]], axis=0)
    tall = jnp.concatenate([total[:, 2 * width : 3 * width], total[:, 3 * width :]], axis=0)
    size = outs[1].shape[0]
    outs[1][...] = tall[:size]
    outs[2][...] = tall[size:]


def halving_order(steps):
    order = [0]
    for step in reversed(steps):
        order = order + [o | step for o in order]
    return order


class Scatter:
    def __init__(self, run, steps, send, keep, last=None, outs=(), at=0):
        self.run, self.steps, self.last, self.outs = run, steps, last, outs
        self.at, self.keep, self.vector = at, keep, None
        self.came = swap(send, "dp", steps[at])
        self.results = None

    def add_vector(self, vector):
        self.vector = vector
        self.vector_came = swap(vector, "dp", self.steps[0])

    def advance(self):
        if self.results is not None:
            return
        self.at += 1
        if self.at == len(self.steps):
            self.results = self.run(self.last, self.outs, self.keep, self.came)
            if self.vector is not None:
                self.vector = self.vector + self.vector_came
            return
        rows, cols = self.keep.shape
        outs = [((rows // 2, cols), BF16), ((rows // 2, cols), F32)]
        step = self.steps[self.at]
        if self.vector is None:
            send, self.keep = self.run(stage_kernel, outs, self.keep, self.came)
        else:
            send, self.keep, self.vector = self.run(
                stage_sum_kernel,
                outs + [(self.vector.shape, F32)],
                self.keep, self.came, self.vector, self.vector_came,
            )
            self.vector_came = swap(self.vector, "dp", step)
        self.came = swap(send, "dp", step)


def shards(
    hidden,
    segment_ids,
    norm1_gain,
    w_gate,
    w_xin,
    w_dt,
    w_bc,
    w_query,
    w_kv,
    convx_weight,
    convx_bias,
    convbc_weight,
    convbc_bias,
    dt_bias,
    a_log,
    d_skip,
    w_mixout,
    w_attnout,
    norm2_gain,
    w_gateup,
    w_down,
    cotangent,
):
    row = lax.axis_index("row")
    col = lax.axis_index("col")
    me = lax.axis_index("dp")
    count = lax.axis_size("dp")
    spot = me & 3
    place = jnp.stack([col, spot, row]).astype(jnp.int32)
    tokens, quarter = hidden.shape
    half = 2 * quarter
    full_width = 4 * quarter
    piece = half // 4
    ch = w_xin.shape[1]
    nq = w_query.shape[1]
    nkv = w_kv.shape[2]
    nbc = w_bc.shape[1]
    heads = w_dt.shape[1]
    ff = w_down.shape[0]
    cq = convx_bias.shape[0]
    hq = dt_bias.shape[0]

    run = Chain()
    cols = ch + nbc + LANES + ch + nq + nkv
    inner = ch + nq

    t_mine = run(
        pieces_kernel,
        [((inner + ff + 4 * tokens, piece), BF16)],
        place, w_mixout, w_attnout, w_down, cotangent, hidden,
        smem=(0,),
    )[0]
    t_got = swap(t_mine, "row")
    gu = w_gateup.reshape(half, 2 * ff)
    g_first = swap(lax.dynamic_slice_in_dim(gu, spot * piece, piece, 0), "row")
    wk = w_kv.reshape(half, nkv)
    wd = jnp.pad(w_dt, ((0, 0), (0, LANES - heads)))
    gain_one = norm1_gain.astype(F32)[None]
    t_first, in_pair = run(
        split_kernel,
        [((inner + ff, piece), BF16), ((4 * tokens, quarter), BF16)],
        t_got, cotangent, hidden,
    )
    t_second = swap(t_first, "dp", 1)
    in_came = swap(in_pair, "col")
    n1, part, part_low, own, far, factor1 = run(
        project_kernel,
        [
            ((tokens, half), BF16),
            ((tokens, cols), F32),
            ((tokens, cols), BF16),
            ((tokens, half), BF16),
            ((tokens, half), BF16),
            ((tokens, LANES), F32),
        ],
        place, in_pair, in_came, gain_one, w_xin, w_bc, wd, w_gate, w_query, wk,
        smem=(0,), scratch=[((tokens, half), BF16)],
    )
    part_came = swap(part_low, "row")
    g_first = run.touch(g_first)
    g_second = swap(g_first, "dp", 2)
    t_cat, g_cat = run(
        hop_kernel,
        [((inner + ff, 2 * piece), BF16), ((2 * piece, 2 * ff), BF16)],
        t_first, t_second, g_first, g_second,
    )
    t_pair = swap(t_cat, "dp", 2)
    g_pair = swap(g_cat, "dp", 1)

    small = jnp.concatenate(
        [convx_weight.T.reshape(-1), convx_bias, dt_bias, a_log, d_skip, norm2_gain]
    )
    small_far = swap(small, "row")

    def joined(start, size):
        a = small[start : start + size]
        b = small_far[start : start + size]
        first = row == 0
        return jnp.concatenate([jnp.where(first, a, b), jnp.where(first, b, a)], 0).astype(F32)

    at = TAPS * cq
    x_par = jnp.stack(
        [joined(k * cq, cq) for k in range(TAPS + 1)]
        + [jnp.repeat(joined(at + cq + 2 * hq, hq), HEAD)]
        + [jnp.zeros((ch,), F32)] * 2
    )
    bc_par = jnp.concatenate(
        [convbc_weight.T, convbc_bias[None], jnp.zeros((3, nbc), BF16)], 0
    ).astype(F32)
    head_par = jnp.stack(
        [jnp.pad(joined(at + cq + k * hq, hq), (0, LANES - heads)) for k in (0, 1)]
        + [jnp.zeros((LANES,), F32)] * 6
    )
    gain2_far = jnp.concatenate(
        [
            lax.dynamic_slice_in_dim(small_far, at + cq + 3 * hq + (spot ^ j) * piece, piece, 0)
            for j in range(4)
        ]
    )
    gain_two = jnp.concatenate([norm2_gain, gain2_far]).astype(F32)[None]
    seg_row = segment_ids.astype(F32)
    seg_col = jnp.broadcast_to(segment_ids[0].astype(F32)[:, None], (tokens, LANES))

    near = [1 << b for b in range(count.bit_length() - 1)]
    turned = [near[1], near[0]] + near[2:]
    size = half // count
    within = jnp.asarray(np.tile(np.arange(size), count), jnp.int32)
    both_within = jnp.concatenate([within, within + size])

    def block_order(steps):
        return jnp.asarray(np.repeat(np.array(halving_order(steps)), size), jnp.int32) ^ me

    near_block = block_order(near)
    turned_block = block_order(turned)
    turned_both = jnp.concatenate([turned_block] * 2)
    order_near = (near_block * size + within)[None]
    order_down = (turned_both * (ff // count) + both_within)[None]
    m_rows = ch // count
    a_rows = nq // count
    order_mix = jnp.where(
        both_within < m_rows,
        turned_both * m_rows + both_within,
        ch + turned_both * a_rows + both_within - m_rows,
    )[None]

    mixed, raw, pre, ys = run(
        lambda *refs: mix_kernel(ch, nq, *refs),
        [
            ((tokens, inner), BF16),
            ((tokens, cols), F32),
            ((tokens, ch + nbc), F32),
            ((tokens, ch), F32),
        ],
        seg_row, seg_col, part, part_came, x_par, bc_par, head_par,
    )
    mix_part = run(
        out_kernel,
        [((tokens, full_width), F32)],
        mixed, w_mixout, w_attnout, t_first, t_second, t_pair,
    )[0]
    mix_came = swap(mix_part, "col")
    dy_own, dy_far, grad_act = run(
        lambda *refs: act_grad_kernel(inner, *refs),
        [((tokens, half), BF16), ((tokens, half), BF16), ((tokens, ff), F32)],
        place, in_pair, in_came, w_down, t_first, t_second, t_pair,
        smem=(0,), scratch=[((tokens, half), BF16)],
    )
    h2, n2, act, ggu, n2_part, down_keep, down_send = run(
        feed_kernel,
        [
            ((tokens, full_width), F32),
            ((tokens, half), BF16),
            ((tokens, ff), BF16),
            ((tokens, 2 * ff), BF16),
            ((tokens, full_width), F32),
            ((tokens, quarter), F32),
            ((tokens, quarter), F32),
        ],
        place, own, far, mix_part, mix_came, gain_two,
        gu, g_first, g_second, g_pair, grad_act, w_down,
        smem=(0,),
    )
    n2_came = swap(n2_part, "col")
    down_came = swap(down_send, "col")
    rows = half // 2

    def halves(width):
        return [((rows, width), BF16), ((rows, width), F32)]

    g_send, g_keep, d_send, d_keep = run(
        feed_grad_kernel, halves(2 * ff) + halves(2 * half), n2, act, ggu, dy_own, order_near, order_down
    )
    s_gu = Scatter(run, near, g_send, g_keep, last_kernel, [((size, 2 * ff), F32)])
    s_down = Scatter(run, turned, d_send, d_keep)
    dym, resid, low, gain2_sum, output = run(
        turn_kernel,
        [
            ((tokens, inner), F32),
            ((tokens, half), F32),
            ((tokens, half), BF16),
            ((8, half), F32),
            ((tokens, quarter), BF16),
        ],
        place, dy_own, dy_far, h2, n2_part, n2_came, gain_two,
        w_mixout, w_attnout, t_first, t_second, t_pair, down_keep, down_came,
        smem=(0,),
    )
    g_two = run(
        lambda *refs: unmix_two_kernel(ch, nq, *refs),
        [((tokens, ch + nq + nkv), BF16)],
        seg_row, seg_col, raw, pre, ys, dym, x_par,
    )[0]
    two_send, two_keep = run(grad_two_kernel, halves(ch + nq + nkv), n1, g_two, order_near)
    s_two = Scatter(
        run, near, two_send, two_keep, last_kernel,
        [((size, ch), F32), ((size, nq), F32), ((size, nkv), F32)],
    )
    m_send, m_keep = run(mix_grad_kernel, halves(2 * half), mixed, low, order_mix)
    s_mix = Scatter(run, turned, m_send, m_keep)
    s_down.advance()
    gx, gdt, gbc, small_sum = run(
        lambda *refs: unmix_one_kernel(ch, nq, *refs),
        [
            ((tokens, ch), BF16),
            ((tokens, LANES), BF16),
            ((tokens + 8, nbc), F32),
            ((16, ch), F32),
        ],
        seg_row, seg_col, raw, pre, ys, dym, x_par, bc_par, head_par,
        scratch=[((tokens, ch), F32), ((tokens, ch), F32), ((tokens, tokens), F32)],
    )
    gbc_came = swap(gbc, "col")
    n1_part, n1_bc, gbc_both = run(
        back_kernel,
        [((tokens, half), F32), ((tokens, half), F32), ((tokens, nbc), BF16)],
        g_two, gx, gdt, gbc, gbc_came, w_xin, w_bc, wd, w_gate, w_query, wk,
    )
    n1_came = swap(n1_part, "col")
    s_gu.advance()
    s_mix.advance()
    s_two.advance()
    one_send, one_keep = run(
        grad_one_kernel, halves(ch + nbc + LANES), n1, gx, gdt, gbc_both, order_near
    )
    s_one = Scatter(
        run, near, one_send, one_keep, last_kernel,
        [((size, ch), F32), ((size, nbc), F32), ((size, LANES), F32)],
    )
    dn1, sum_rows = run(
        close_kernel,
        [((tokens, half), F32), ((16, tokens), F32)],
        own, n1_part, n1_came, n1_bc, gain_one, gbc, gbc_came,
    )
    rows_far = swap(sum_rows, "row")
    s_gu.advance()
    grad_hidden, vector = run(
        end_kernel,
        [((tokens, quarter), F32), ((32, ch), F32)],
        place, own, factor1, resid, dn1, gain_one, sum_rows, rows_far, small_sum, gain2_sum,
        smem=(0,),
    )
    s_one.add_vector(vector)
    s_one.advance()
    tall_send, tall_keep = run(
        join_kernel,
        [((rows // 4, 4 * half), BF16), ((rows // 4, 4 * half), F32)],
        s_down.keep, s_down.came, s_mix.keep, s_mix.came,
    )
    s_tall = Scatter(
        run, turned, tall_send, tall_keep, last_tall_kernel,
        [((2 * size, half), F32), ((m_rows, half), F32), ((a_rows, half), F32)],
        at=2,
    )
    scatters = (s_two, s_gu, s_one, s_tall)
    while any(s.results is None for s in scatters):
        for s in scatters:
            s.advance()
    vector = s_one.vector
    r_gate, r_query, r_kv = s_two.results
    r_xin, r_bc, r_dt = s_one.results
    r_down, r_mixout, r_attnout = s_tall.results

    def mine(values, width):
        return lax.dynamic_slice_in_dim(values, row * width, width, values.ndim - 1)

    return (
        output,
        grad_hidden,
        vector[24, :half],
        r_gate,
        r_xin,
        r_dt[:, :heads],
        r_bc,
        r_query,
        r_kv.reshape(size, 1, nkv),
        mine(vector[0:TAPS], cq).T,
        mine(vector[TAPS], cq),
        vector[16 : 16 + TAPS, :nbc].T,
        vector[16 + TAPS, :nbc],
        mine(vector[12, :heads], hq),
        mine(vector[12, LANES : LANES + heads], hq),
        mine(vector[12, 2 * LANES : 2 * LANES + heads], hq),
        r_mixout,
        r_attnout,
        vector[25, :half],
        s_gu.results[0].reshape(size, 2, ff),
        r_down,
    )


def solution(mesh):
    placed = (
        P("dp", ("row", "col")),
        P("dp", None),
        P("row"),
        P("row", "col"),
        P("row", "col"),
        P("row", "col"),
        P("row", None),
        P("row", "col"),
        P("row", "col", None),
        P(("col", "row"), None),
        P(("col", "row")),
        P(),
        P(),
        P(("col", "row")),
        P(("col", "row")),
        P(("col", "row")),
        P("col", "row"),
        P("col", "row"),
        P("row"),
        P("row", None, "col"),
        P("col", "row"),
        P("dp", ("row", "col")),
    )
    return jax.shard_map(
        shards,
        mesh=mesh,
        in_specs=placed,
        out_specs=(
            P("dp", ("row", "col")),
            P("dp", ("row", "col")),
            P("row"),
            P(("row", "dp"), "col"),
            P(("row", "dp"), "col"),
            P(("row", "dp"), "col"),
            P(("row", "dp"), None),
            P(("row", "dp"), "col"),
            P(("row", "dp"), "col", None),
            P(("col", "row"), None),
            P(("col", "row")),
            P(),
            P(),
            P(("col", "row")),
            P(("col", "row")),
            P(("col", "row")),
            P(("col", "dp"), "row"),
            P(("col", "dp"), "row"),
            P("row"),
            P(("row", "dp"), None, "col"),
            P(("col", "dp"), "row"),
        ),
        check_vma=False,
    )
```

```python
import jax
import jax.numpy as jnp
import numpy as np
from jax import lax
from jax.experimental import pallas as pl
from jax.experimental.pallas import tpu as pltpu
from jax.sharding import PartitionSpec as P

NORM_EPS = 1e-05
F32 = jnp.float32
BF16 = jnp.bfloat16
HEAD = 64
LANES = 128
TAPS = 4
FAR = -1e30


def swap(values, axis, step=1):
    count = lax.axis_size(axis)
    return lax.ppermute(values, axis, [(i, i ^ step) for i in range(count)])


def dot(left, right):
    return jnp.dot(left, right, preferred_element_type=F32)


def dot_bt(left, right):
    return lax.dot_general(left, right, (((1,), (1,)), ((), ())), preferred_element_type=F32)


def dot_at(left, right):
    return lax.dot_general(left, right, (((0,), (0,)), ((), ())), preferred_element_type=F32)


def fine(left, right, dims=((1,), (0,))):
    return lax.dot_general(
        left, right, (dims, ((), ())), precision=lax.Precision.HIGHEST, preferred_element_type=F32
    )


class Chain:
    def __init__(self):
        self.token = jnp.zeros((8, LANES), F32)

    def __call__(self, kernel, outs, *args, scratch=(), smem=(), after=()):
        plain = pltpu.VMEM
        specs = [
            pl.BlockSpec(memory_space=pltpu.SMEM if i in smem else plain)
            for i in range(len(args))
        ]
        extra = (self.token,) + tuple(after)
        count = len(args)
        held = count + len(extra)

        def body(*refs):
            refs[held][...] = jnp.zeros((8, LANES), F32)
            kernel(*refs[:count], *refs[held + 1 :])

        results = pl.pallas_call(
            body,
            out_shape=[jax.ShapeDtypeStruct((8, LANES), F32)]
            + [jax.ShapeDtypeStruct(s, d) for s, d in outs],
            in_specs=specs + [pl.BlockSpec(memory_space=pl.ANY)] * len(extra),
            out_specs=[pl.BlockSpec(memory_space=pltpu.VMEM)]
            + [pl.BlockSpec(memory_space=plain)] * len(outs),
            scratch_shapes=[pltpu.VMEM(s, d) if d is not None else s for s, d in scratch],
            compiler_params=pltpu.CompilerParams(vmem_limit_bytes=56 << 20),
            cost_estimate=pl.CostEstimate(flops=0, bytes_accessed=0, transcendentals=0),
        )(*args, *extra)
        self.token = results[0]
        return results[1:]


def iota(shape, dim):
    return lax.broadcasted_iota(jnp.int32, shape, dim)


def column(row_vector):
    ones = jnp.full((row_vector.shape[0], LANES), 1.0 / row_vector.shape[0], F32)
    return fine(row_vector, ones, ((0,), (0,)))


def token_sums(values):
    return fine(jnp.ones((8, values.shape[1]), F32), values, ((1,), (1,)))


def pieces_kernel(place, wm, wa, wd, gu, cot, hid, small, out):
    piece = out.shape[1]
    at = pl.multiple_of(place[1] * piece, piece)
    row = 0
    for w in (wm, wa, wd):
        out[row : row + w.shape[0]] = w[:, pl.ds(at, piece)]
        row += w.shape[0]
    for value in (gu[pl.ds(at, piece), :], cot[...], hid[...]):
        for j in range(value.shape[1] // piece):
            out[row : row + value.shape[0]] = value[:, j * piece : (j + 1) * piece]
            row += value.shape[0]
    out[row:] = small[...]


def join_small(place, heads, own, far, x_par_out, head_out, gain_out):
    first = place[2] == 0
    a = jnp.where(first, own, far)
    b = jnp.where(first, far, own)
    width = x_par_out.shape[1] // 2
    count = width // LANES
    x_par_out[...] = jnp.zeros_like(x_par_out)
    for k in range(TAPS + 1):
        for i in range(count):
            at = k * count + i
            x_par_out[k : k + 1, i * LANES : (i + 1) * LANES] = a[at : at + 1]
            x_par_out[k : k + 1, width + i * LANES : width + (i + 1) * LANES] = b[at : at + 1]
    row = (TAPS + 1) * count
    pieces = gain_out.shape[1] // (2 * LANES)
    for j in range(pieces):
        gain_out[:, j * LANES : (j + 1) * LANES] = own[row + j : row + j + 1]
        block = jnp.zeros((1, LANES), F32)
        for i in range(pieces):
            block = block + jnp.where((place[1] ^ j) == i, far[row + i : row + i + 1], 0.0)
        at = (pieces + j) * LANES
        gain_out[:, at : at + LANES] = block
    row += pieces
    joined = a[row : row + 8] + pltpu.roll(b[row : row + 8], heads // 2, 1)
    head_out[...] = joined
    pick = jnp.where(
        iota((LANES, 2 * width), 0) == iota((LANES, 2 * width), 1) // HEAD, 1.0, 0.0
    )
    x_par_out[TAPS + 1 : TAPS + 2] = fine(joined, pick)[2:3]


def split_kernel(
    heads, place, got, cot, hid, small, t_out, g_out, pair_out, x_par_out, head_out, gain_out
):
    piece = got.shape[1]
    tokens = cot.shape[0]
    row = t_out.shape[0]
    t_out[...] = got[0:row]
    for j in range(g_out.shape[1] // piece):
        g_out[:, j * piece : (j + 1) * piece] = got[row : row + piece]
        row += piece
    for i, value in enumerate((cot, hid)):
        at = 2 * i * tokens
        pair_out[at : at + tokens] = value[...]
        for j in range(value.shape[1] // piece):
            pair_out[at + tokens : at + 2 * tokens, j * piece : (j + 1) * piece] = got[
                row : row + tokens
            ]
            row += tokens
    own = small[...].astype(F32)
    far = got[row:].astype(F32)
    join_small(place, heads, own, far, x_par_out, head_out, gain_out)


def gather_quarters(place, mine, came, at, own_out, far_out, far_tmp):
    width = own_out.shape[1] // 2
    piece = width // 2
    first = place[0] == 0
    tokens = own_out.shape[0]
    for i, out in enumerate((own_out, far_tmp)):
        rows = slice((at + i) * tokens, (at + i + 1) * tokens)
        a = mine[rows]
        b = came[rows]
        out[:, :width] = jnp.where(first, a, b)
        out[:, width:] = jnp.where(first, b, a)
    for j in range(4):
        at = pl.multiple_of((place[1] ^ j) * piece, piece)
        far_out[:, j * piece : (j + 1) * piece] = far_tmp[:, pl.ds(at, piece)]


def project_kernel(
    place, mine, came, gain, wx, wb, wd, wg, wq, wk,
    n1_out, p_out, low_out, own_out, far_out, factor_out, far_tmp,
):
    gather_quarters(place, mine, came, 2, own_out, far_out, far_tmp)
    own = own_out[...].astype(F32)
    far = far_tmp[...].astype(F32)
    mean = jnp.sum(own * own + far * far, axis=1, keepdims=True) / (2 * own.shape[1])
    factor = lax.rsqrt(mean + NORM_EPS)
    factor_out[...] = jnp.broadcast_to(factor, factor_out.shape)
    n1 = (own * factor * gain[...]).astype(BF16)
    n1_out[...] = n1
    at = 0
    for w in (wx, wb, wd, wg, wq, wk):
        size = w.shape[1]
        part = dot(n1, w[...])
        p_out[:, at : at + size] = part
        low_out[:, at : at + size] = part.astype(BF16)
        at += size


def hop_kernel(t_first, t_second, g_first, g_second, n1, order, t_out, g_out, left_out):
    t_piece = t_first.shape[1]
    g_piece = g_first.shape[0]
    t_out[:, :t_piece] = t_first[...]
    t_out[:, t_piece:] = t_second[...]
    g_out[:g_piece] = g_first[...]
    g_out[g_piece:] = g_second[...]
    left_out[...] = permuted(n1[...], order[...])


def masks(seg_row, seg_col, turned):
    tokens = seg_row.shape[1]
    i = iota((tokens, tokens), 1 if turned else 0)
    j = iota((tokens, tokens), 0 if turned else 1)
    same = seg_col[:, :1] == seg_row[...]
    return jnp.where((i >= j) & same, 0.0, FAR)


def valids(seg_col):
    seg = seg_col[...]
    t = iota(seg.shape, 0)
    return [
        jnp.where((t >= k) & (pltpu.roll(seg, k, 0) == seg), 1.0, 0.0) for k in range(1, TAPS)
    ]


def conv(block, taps, bias, valid):
    total = block * taps[TAPS - 1 : TAPS] + bias
    for k in range(1, TAPS):
        total = total + (pltpu.roll(block, k, 0) * valid[k - 1]) * taps[TAPS - 1 - k : TAPS - k]
    return total


def conv_turn(grad, block, taps, valid):
    tokens = grad.shape[0]
    back = grad * taps[TAPS - 1 : TAPS]
    rows = [None] * TAPS
    rows[TAPS - 1] = jnp.sum(grad * block, axis=0, keepdims=True)
    for k in range(1, TAPS):
        kept = grad * valid[k - 1]
        back = back + pltpu.roll(kept, tokens - k, 0) * taps[TAPS - 1 - k : TAPS - k]
        rows[TAPS - 1 - k] = jnp.sum(kept * pltpu.roll(block, k, 0), axis=0, keepdims=True)
    rows.append(jnp.sum(grad, axis=0, keepdims=True))
    rows.append(jnp.zeros((8 - len(rows), grad.shape[1]), F32))
    return back, jnp.concatenate(rows, 0)


def silu_turn(value):
    sig = jax.nn.sigmoid(value)
    return value * sig, sig * (1.0 + value * (1.0 - sig))


def steps(dt_raw, head_par):
    shifted = dt_raw + head_par[0:1]
    return jnp.maximum(shifted, 0.0) + jnp.log1p(jnp.exp(-jnp.abs(shifted)))


def mix_kernel(
    ch, nq, seg_row, seg_col, own, came, x_par, bc_par, head_par,
    mixed_out, sums_out, pre_out, y_out,
):
    tokens = own.shape[0]
    nbc = bc_par.shape[1]
    state = nbc // 2
    sums_out[...] = own[...] + came[...].astype(F32)
    lane = iota((tokens, LANES), 1)
    low = lane < HEAD
    mask = masks(seg_row, seg_col, False)
    valid = valids(seg_col)
    for b in range(nbc // LANES):
        at = ch + b * LANES
        part = slice(b * LANES, (b + 1) * LANES)
        pre_out[:, at : at + LANES] = conv(
            sums_out[:, at : at + LANES], bc_par[0:TAPS, part], bc_par[TAPS : TAPS + 1, part], valid
        )
    bcc = pre_out[:, ch : ch + nbc]
    bcc = bcc * jax.nn.sigmoid(bcc)
    inner = fine(bcc[:, state:], bcc[:, :state], ((1,), (1,)))
    dt = steps(sums_out[:, ch + nbc : ch + nbc + LANES], head_par)
    tri = jnp.where(iota((tokens, tokens), 0) >= iota((tokens, tokens), 1), 1.0, 0.0)
    cum = fine(tri, dt * -jnp.exp(head_par[1:2]))
    cum_row = cum.T
    base = ch + nbc + LANES
    for p in range(ch // LANES):
        part = slice(p * LANES, (p + 1) * LANES)
        pre = conv(sums_out[:, part], x_par[0:TAPS, part], x_par[TAPS : TAPS + 1, part], valid)
        pre_out[:, part] = pre
        xc = pre * jax.nn.sigmoid(pre)
        h = 2 * p
        xdt = (xc * jnp.where(low, dt[:, h : h + 1], dt[:, h + 1 : h + 2])).astype(BF16)
        ys = []
        for e in (h, h + 1):
            decay = jnp.exp((cum[:, e : e + 1] - cum_row[e : e + 1]) + mask)
            ys.append(dot((inner * decay).astype(BF16), xdt))
        y = jnp.where(low, ys[0], ys[1])
        y_out[:, part] = y
        y = y + x_par[TAPS + 1 : TAPS + 2, part] * xc
        z = sums_out[:, base + p * LANES : base + (p + 1) * LANES]
        mixed_out[:, part] = (y * (z * jax.nn.sigmoid(z))).astype(BF16)
    at = base + ch
    kv = sums_out[:, at + nq : at + nq + LANES].astype(BF16)
    kv_turn = pltpu.roll(sums_out[:, at + nq : at + nq + LANES], HEAD, 1).astype(BF16)
    keys = jnp.where(low, kv, kv_turn)
    vals = jnp.where(low, kv_turn, kv)
    for p in range(nq // LANES):
        query = sums_out[:, at + p * LANES : at + (p + 1) * LANES] * (HEAD ** -0.5)
        outs = []
        for side in (low, ~low):
            score = dot_bt(jnp.where(side, query, 0.0).astype(BF16), keys) + mask
            score = jnp.exp(score - jnp.max(score, axis=1, keepdims=True))
            total = jnp.sum(score, axis=1, keepdims=True)
            outs.append(dot(score.astype(BF16), vals) / total)
        mixed_out[:, ch + p * LANES : ch + (p + 1) * LANES] = jnp.where(
            low, outs[0], outs[1]
        ).astype(BF16)


def unmix_two_kernel(ch, nq, seg_row, seg_col, sums, pre, ys, dym, x_par, gtwo_out):
    tokens = sums.shape[0]
    base = sums.shape[1] - (ch + nq + LANES)
    low = iota((tokens, LANES), 1) < HEAD
    mask = masks(seg_row, seg_col, True)
    for p in range(ch // LANES):
        part = slice(p * LANES, (p + 1) * LANES)
        value = pre[:, part]
        xc = value * jax.nn.sigmoid(value)
        _, gate_turn = silu_turn(sums[:, base + p * LANES : base + (p + 1) * LANES])
        y = ys[:, part] + x_par[TAPS + 1 : TAPS + 2, part] * xc
        gtwo_out[:, part] = (dym[:, part] * y * gate_turn).astype(BF16)
    at = base + ch
    kv = sums[:, at + nq : at + nq + LANES]
    kv_turn = pltpu.roll(kv, HEAD, 1)
    keys = jnp.where(low, kv, kv_turn).astype(BF16)
    vals = jnp.where(low, kv_turn, kv).astype(BF16)
    dk = jnp.zeros((tokens, LANES), F32)
    dv = jnp.zeros((tokens, LANES), F32)
    for p in range(nq // LANES):
        query = sums[:, at + p * LANES : at + (p + 1) * LANES] * (HEAD ** -0.5)
        grad = dym[:, ch + p * LANES : ch + (p + 1) * LANES]
        dqs = []
        for side in (low, ~low):
            q_low = jnp.where(side, query, 0.0).astype(BF16)
            g_low = jnp.where(side, grad, 0.0).astype(BF16)
            score = dot_bt(keys, q_low) + mask
            score = jnp.exp(score - jnp.max(score, axis=0, keepdims=True))
            prob = score * (1.0 / jnp.sum(score, axis=0, keepdims=True))
            dprob = dot_bt(vals, g_low)
            dv = dv + dot(prob.astype(BF16), g_low)
            inner_sum = jnp.sum(prob * dprob, axis=0, keepdims=True)
            dscore = (prob * (dprob - inner_sum)).astype(BF16)
            dk = dk + dot(dscore, q_low)
            dqs.append(dot_at(dscore, keys))
        gtwo_out[:, ch + p * LANES : ch + (p + 1) * LANES] = (
            jnp.where(low, dqs[0], dqs[1]) * (HEAD ** -0.5)
        ).astype(BF16)
    dk = dk + pltpu.roll(dk, HEAD, 1)
    dv = dv + pltpu.roll(dv, HEAD, 1)
    gtwo_out[:, ch + nq : ch + nq + LANES] = jnp.where(low, dk, dv).astype(BF16)

def unmix_one_kernel(
    ch, nq, seg_row, seg_col, sums, pre, ys, dym, x_par, bc_par, head_par,
    gx_out, gdt_out, gbc_out, small_out, prod_a, prod_b, turned,
):
    tokens = sums.shape[0]
    nbc = bc_par.shape[1]
    state = nbc // 2
    lane = iota((tokens, LANES), 1)
    low = lane < HEAD
    mask = masks(seg_row, seg_col, True)
    valid = valids(seg_col)
    bc_pre = pre[:, ch : ch + nbc]
    bcc, bcc_turn = silu_turn(bc_pre)
    b_in = bcc[:, :state]
    c_in = bcc[:, state:]
    inner = fine(b_in, c_in, ((1,), (1,)))
    dt_raw = sums[:, ch + nbc : ch + nbc + LANES]
    dt = steps(dt_raw, head_par)
    rate = jnp.exp(head_par[1:2])
    tri = jnp.where(iota((tokens, tokens), 0) >= iota((tokens, tokens), 1), 1.0, 0.0)
    cum = fine(tri, dt * -rate)
    cum_row = cum.T
    base = ch + nbc + LANES
    small_out[...] = jnp.zeros_like(small_out)
    turned[...] = jnp.zeros_like(turned)
    for p in range(ch // LANES):
        part = slice(p * LANES, (p + 1) * LANES)
        xc, xc_turn = silu_turn(pre[:, part])
        skip = x_par[TAPS + 1 : TAPS + 2, part]
        z = sums[:, base + p * LANES : base + (p + 1) * LANES]
        gate = z * jax.nn.sigmoid(z)
        dy_in = dym[:, part]
        y = ys[:, part]
        dy = dy_in * gate
        h = 2 * p
        dt_pair = jnp.where(low, dt[:, h : h + 1], dt[:, h + 1 : h + 2])
        xdt = xc * dt_pair
        dy_low = dy.astype(BF16)
        x_low = xdt.astype(BF16)
        sides = []
        for e, side in ((h, low), (h + 1, ~low)):
            decay = jnp.exp((cum_row[e : e + 1] - cum[:, e : e + 1]) + mask)
            turned[...] += dot_bt(jnp.where(side, xdt, 0.0).astype(BF16), dy_low) * decay
            sides.append(dot((inner * decay).astype(BF16), dy_low))
        dxdt = jnp.where(low, sides[0], sides[1])
        prod_a[:, part] = dy_low.astype(F32) * y - x_low.astype(F32) * dxdt
        prod_b[:, part] = dxdt * xc
        small_out[8 + TAPS + 1 : 8 + TAPS + 2, part] = jnp.sum(dy * xc, axis=0, keepdims=True)
        dpre = (skip * dy + dxdt * dt_pair) * xc_turn
        back, rows = conv_turn(dpre, sums[:, part], x_par[0:TAPS, part], valid)
        gx_out[:, part] = back.astype(BF16)
        small_out[0:8, part] = rows
    pick = jnp.where(iota((ch, LANES), 0) // HEAD == iota((ch, LANES), 1), 1.0, 0.0)
    dcum = fine(prod_a[...], pick)
    ddt = fine(prod_b[...], pick)
    after = fine(tri, dcum, ((0,), (0,)))
    ddt = ddt - rate * after
    ddt = ddt * jax.nn.sigmoid(dt_raw + head_par[0:1])
    gdt_out[...] = ddt.astype(BF16)
    small_out[8 + TAPS : 8 + TAPS + 1, 0:LANES] = jnp.sum(ddt, axis=0, keepdims=True)
    small_out[8 + TAPS : 8 + TAPS + 1, LANES : 2 * LANES] = jnp.sum(
        after * (-dt * rate), axis=0, keepdims=True
    )
    skip_sum = jnp.broadcast_to(small_out[8 + TAPS + 1 : 8 + TAPS + 2, :], (8, ch))
    small_out[8 + TAPS : 8 + TAPS + 1, 2 * LANES : 3 * LANES] = fine(skip_sum, pick)[0:1]
    dinner = turned[...]
    d_b = fine(dinner, c_in) * bcc_turn[:, :state]
    d_c = fine(dinner, b_in, ((0,), (0,))) * bcc_turn[:, state:]
    for b, grad in enumerate((d_b, d_c)):
        at = ch + b * LANES
        part = slice(b * LANES, (b + 1) * LANES)
        back, rows = conv_turn(grad, sums[:, at : at + LANES], bc_par[0:TAPS, part], valid)
        gbc_out[0:tokens, part] = back
        gbc_out[tokens : tokens + 8, part] = rows


def tall_far(first, second, pair, start, size):
    return jnp.concatenate(
        [r[start : start + size] for r in (first, second, pair)], axis=1
    )


def out_kernel(mixed, wm, wa, first, second, pair, part_out):
    half = wm.shape[1]
    ch = wm.shape[0]
    value = mixed[...]
    part_out[:, :half] = dot(value[:, :ch], wm[...]) + dot(value[:, ch:], wa[...])
    part_out[:, half:] = dot(value, tall_far(first, second, pair, 0, value.shape[1]))


def norm_factor(value):
    return lax.rsqrt(jnp.mean(value * value, axis=1, keepdims=True) + NORM_EPS)


def act_grad_kernel(
    inner, place, mine, came, wd, first, second, pair, own_out, far_out, ga_out, far_tmp
):
    gather_quarters(place, mine, came, 0, own_out, far_out, far_tmp)
    ff = wd.shape[0]
    ga_out[...] = dot_bt(own_out[...], wd[...]) + dot_bt(
        far_out[...], tall_far(first, second, pair, inner, ff)
    )


def feed_kernel(
    place, own, far, part, came, gain, gu, gu_first, gu_second, gu_pair, grad_act, wd,
    h2_out, n2_out, act_out, ggu_out, n2p_out, keep_out, send_out,
):
    half = own.shape[1]
    quarter = half // 2
    piece = half // 4
    h2_out[:, :half] = own[...].astype(F32) + (part[:, :half] + came[:, :half])
    h2_out[:, half:] = far[...].astype(F32) + (part[:, half:] + came[:, half:])
    h2 = h2_out[...]
    n2 = (h2 * norm_factor(h2) * gain[...]).astype(BF16)
    n2_out[...] = n2[:, :half]
    gu_far = jnp.concatenate(
        [gu_first[...], gu_pair[0:piece], gu_second[...], gu_pair[piece:]], axis=0
    )
    ff = wd.shape[0]
    gate_up = dot(n2[:, :half], gu[...]) + dot(n2[:, half:], gu_far)
    gate = gate_up[:, :ff]
    up = gate_up[:, ff:]
    silu, silu_grad = silu_turn(gate)
    act = (silu * up).astype(BF16)
    act_out[...] = act
    ga = grad_act[...]
    ggu_out[:, :ff] = (ga * up * silu_grad).astype(BF16)
    ggu_out[:, ff:] = (ga * silu).astype(BF16)
    ggu = ggu_out[...]
    n2p_out[:, :half] = dot_bt(ggu, gu[...])
    n2p_out[:, half:] = dot_bt(ggu, gu_far)
    down = dot(act, wd[...])
    first = place[0] == 0
    keep_out[...] = jnp.where(first, down[:, :quarter], down[:, quarter:])
    send_out[...] = jnp.where(first, down[:, quarter:], down[:, :quarter])


def permuted(left, source):
    width = left.shape[1]
    hot = jnp.where(iota((width, source.shape[1]), 0) == source, 1.0, 0.0).astype(BF16)
    return dot(left, hot).astype(BF16)


def feed_grad_kernel(
    n2, act, ggu, dy, order, order2, g_send, d_send, g_left, d_left
):
    rows = g_send.shape[0]
    width = dy.shape[1]
    left = permuted(n2[...], order[...])
    g_send[...] = dot_at(left[:, rows:], ggu[...]).astype(BF16)
    g_left[...] = left[:, :rows]
    left = permuted(act[...], order2[...])
    for s in (0, 1):
        cut = 2 * s * rows
        d_send[:, s * width : (s + 1) * width] = dot_at(
            left[:, cut + rows : cut + 2 * rows], dy[...]
        ).astype(BF16)
        d_left[:, s * rows : (s + 1) * rows] = left[:, cut : cut + rows]


def turn_kernel(
    ch, nq, place, dy_own, dy_far, h2, part, came, gain, wm, wa, first, second, pair, d_keep, d_came,
    mixed, order_mix, seg_row, seg_col, sums, pre, ys, x_par, left1,
    dym_out, resid_out, low_out, gain_out, output_out, m_send, m_left, gtwo_out, two_send,
):
    half = dy_own.shape[1]
    quarter = half // 2
    value = h2[...]
    output_out[...] = (
        jnp.where(place[0] == 0, value[:, :quarter], value[:, quarter:half])
        + (d_keep[...] + d_came[...])
    ).astype(BF16)
    factor = norm_factor(value)
    dn2 = part[...] + came[...]
    gained = dn2 * gain[...]
    inner_sum = jnp.sum(gained * value, axis=1, keepdims=True)
    gain_out[...] = jnp.broadcast_to(
        jnp.sum(dn2[:, :half] * value[:, :half] * factor, axis=0, keepdims=True), gain_out.shape
    )
    slope = factor * factor * factor * inner_sum / (2 * half)
    change = factor * gained - value * slope
    dh_own = dy_own[...].astype(F32) + change[:, :half]
    dh_far = dy_far[...].astype(F32) + change[:, half:]
    resid_out[...] = dh_own
    low_own = dh_own.astype(BF16)
    low_out[...] = low_own
    dym = dot_bt(dh_far.astype(BF16), tall_far(first, second, pair, 0, dym_out.shape[1]))
    dym_out[:, :ch] = dym[:, :ch] + dot_bt(low_own, wm[...])
    dym_out[:, ch:] = dym[:, ch:] + dot_bt(low_own, wa[...])
    unmix_two_kernel(ch, nq, seg_row, seg_col, sums, pre, ys, dym_out, x_par, gtwo_out)
    rows = two_send.shape[0]
    two_send[...] = dot_at(left1[:, rows:], gtwo_out[...]).astype(BF16)
    left = permuted(mixed[...], order_mix[...])
    for s in (0, 1):
        cut = 2 * s * rows
        m_send[:, s * half : (s + 1) * half] = dot_at(
            left[:, cut + rows : cut + 2 * rows], low_own
        ).astype(BF16)
        m_left[:, s * rows : (s + 1) * rows] = left[:, cut : cut + rows]


def back_kernel(
    g_two, gx, gdt, gbc, gbc_came, wx, wb, wd, wg, wq, wk, left1,
    n1p_out, n1b_out, both_out, one_send,
):
    tokens = gx.shape[0]
    both = (gbc[0:tokens] + gbc_came[0:tokens]).astype(BF16)
    both_out[...] = both
    rows = one_send.shape[0]
    left = left1[:, rows:]
    at = 0
    for right in (gx[...], both, gdt[...]):
        size = right.shape[1]
        one_send[:, at : at + size] = dot_at(left, right).astype(BF16)
        at += size
    ch = wg.shape[1]
    nq = wq.shape[1]
    total = dot_bt(gx[...], wx[...]) + dot_bt(gdt[...], wd[...])
    total = total + dot_bt(g_two[:, :ch], wg[...]) + dot_bt(g_two[:, ch : ch + nq], wq[...])
    n1p_out[...] = total + dot_bt(g_two[:, ch + nq :], wk[...])
    n1b_out[...] = dot_bt(both, wb[...])


def store_halves(total, at, send_out, keep_out, skip=0):
    rows = keep_out.shape[0]
    size = total.shape[1]
    send_out[skip:, at : at + size] = total[rows:].astype(BF16)
    keep_out[:, at : at + size] = total[:rows]


def wide_kernel(left, right, came, send_out, keep_out):
    total = dot_at(left[:, : came.shape[0]], right[...]) + came[...].astype(F32)
    store_halves(total, 0, send_out, keep_out)


def tall_kernel(d_left, dy, d_came, m_left, low, m_came, send_out, keep_out):
    at = 0
    for left, right, came in ((d_left, dy, d_came), (m_left, low, m_came)):
        rows = came.shape[0]
        width = right.shape[1]
        for s in (0, 1):
            total = dot_at(left[:, s * rows : (s + 1) * rows], right[...])
            total = total + came[:, s * width : (s + 1) * width].astype(F32)
            store_halves(total, at, send_out, keep_out)
            at += width


def pack_vector(value, out):
    rows, width = value.shape
    high = value.astype(BF16)
    low = (value - high.astype(F32)).astype(BF16)
    out[0:rows, 0:width] = high
    out[rows : 2 * rows, 0:width] = low
    out[0 : 2 * rows, width:] = jnp.zeros((2 * rows, out.shape[1] - width), BF16)
    return high.astype(F32) + low.astype(F32)


def read_vector(came, shape):
    rows, width = shape
    return came[0:rows, 0:width].astype(F32) + came[rows : 2 * rows, 0:width].astype(F32)


def one_kernel(left1, gx, both, gdt, came, vector, vector_came, send_out, keep_out, vector_out):
    left = left1[:, : came.shape[0]]
    skip = 2 * vector.shape[0]
    at = 0
    for right in (gx[...], both[...], gdt[...]):
        size = right.shape[1]
        total = dot_at(left, right) + came[:, at : at + size].astype(F32)
        store_halves(total, at, send_out, keep_out, skip)
        at += size
    vector_out[...] = pack_vector(vector[...] + vector_came[...], send_out)


def one_stage_kernel(keep, came, vector, send_out, keep_out, vector_out):
    skip = 2 * vector.shape[0]
    total = keep[...] + came[skip:].astype(F32)
    store_halves(total, 0, send_out, keep_out, skip)
    vector_out[...] = pack_vector(vector[...] + read_vector(came, vector.shape), send_out)


def one_last_kernel(
    heads, place, keep, came, vector, x_out, bc_out, dt_out,
    n1_out, n2_out, xw_out, xb_out, bw_out, bb_out, dtb_out, alog_out, skip_out,
):
    skip = 2 * vector.shape[0]
    total = keep[...] + came[skip:].astype(F32)
    ch = x_out.shape[1]
    nbc = bc_out.shape[1]
    x_out[...] = total[:, :ch]
    bc_out[...] = total[:, ch : ch + nbc]
    dt_out[...] = total[:, ch + nbc : ch + nbc + heads]
    value = vector[...] + read_vector(came, vector.shape)
    first = place[2] == 0
    half = n1_out.shape[1]
    cq = xb_out.shape[1]
    n1_out[...] = value[24:25, :half]
    n2_out[...] = value[25:26, :half]
    mine = jnp.where(first, value[0:8, :cq], value[0:8, cq : 2 * cq])
    xw_out[...] = mine[0:TAPS]
    xb_out[...] = mine[TAPS : TAPS + 1]
    bw_out[...] = value[16 : 16 + TAPS, :nbc]
    bb_out[...] = value[16 + TAPS : 17 + TAPS, :nbc]
    hq = dtb_out.shape[1]
    for i, out in enumerate((dtb_out, alog_out, skip_out)):
        at = i * LANES
        out[...] = jnp.where(
            first, value[12:13, at : at + hq], value[12:13, at + hq : at + 2 * hq]
        )


def close_kernel(own, part, came, n1b, gain, gbc, gbc_came, dn1_out, rows_out):
    tokens = part.shape[0]
    dn1 = (part[...] + came[...]) + n1b[...]
    dn1_out[...] = dn1
    rows_out[0:8, :] = token_sums(dn1 * gain[...] * own[...].astype(F32))
    rows_out[8:16, :] = gbc[tokens:] + gbc_came[tokens:]


def end_kernel(
    place, own, factor1, resid, dn1, gain, rows, rows_far, small, gain2, hidden_out, vector_out
):
    half = dn1.shape[1]
    quarter = half // 2
    hid = own[...].astype(F32)
    factor = factor1[:, :1]
    inner_sum = column(rows[0:8] + rows_far[0:8])[:, :1]
    value = dn1[...]
    change = resid[...] + factor * (value * gain[...]) - hid * (
        factor * factor * factor * inner_sum / (2 * half)
    )
    hidden_out[...] = jnp.where(place[0] == 0, change[:, :quarter], change[:, quarter:])
    count = small.shape[0]
    vector_out[...] = jnp.zeros_like(vector_out)
    vector_out[0:count] = small[...]
    vector_out[count : count + 8, 0 : rows.shape[1]] = jnp.where(
        place[2] == 0, rows[8:16], rows_far[8:16]
    )
    vector_out[count + 8 : count + 9, 0:half] = jnp.sum(value * hid * factor, axis=0, keepdims=True)
    vector_out[count + 9 : count + 10, 0:half] = gain2[0:1]


def stage_kernel(keep, came, send_out, keep_out):
    rows = keep_out.shape[0]
    total = keep[...] + came[...].astype(F32)
    send_out[...] = total[rows:].astype(BF16)
    keep_out[...] = total[:rows]


def last_kernel(keep, came, *outs):
    total = keep[...] + came[...].astype(F32)
    at = 0
    for out in outs:
        out[...] = total[:, at : at + out.shape[1]]
        at += out.shape[1]


def last_tall_kernel(keep, came, *outs):
    total = keep[...] + came[...].astype(F32)
    width = outs[0].shape[1]
    outs[0][...] = jnp.concatenate([total[:, :width], total[:, width : 2 * width]], axis=0)
    tall = jnp.concatenate([total[:, 2 * width : 3 * width], total[:, 3 * width :]], axis=0)
    size = outs[1].shape[0]
    outs[1][...] = tall[:size]
    outs[2][...] = tall[size:]


def halving_order(steps):
    order = [0]
    for step in reversed(steps):
        order = order + [o | step for o in order]
    return order


def halve(run, steps, at, send, keep, last, outs):
    while True:
        came = swap(send, "dp", steps[at])
        yield None
        at += 1
        if at == len(steps):
            break
        rows, cols = keep.shape
        send, keep = run(
            stage_kernel, [((rows // 2, cols), BF16), ((rows // 2, cols), F32)], keep, came
        )
    yield run(last, outs, keep, came)


def shards(
    hidden,
    segment_ids,
    norm1_gain,
    w_gate,
    w_xin,
    w_dt,
    w_bc,
    w_query,
    w_kv,
    convx_weight,
    convx_bias,
    convbc_weight,
    convbc_bias,
    dt_bias,
    a_log,
    d_skip,
    w_mixout,
    w_attnout,
    norm2_gain,
    w_gateup,
    w_down,
    cotangent,
):
    row = lax.axis_index("row")
    col = lax.axis_index("col")
    me = lax.axis_index("dp")
    count = lax.axis_size("dp")
    spot = me & 3
    place = jnp.stack([col, spot, row]).astype(jnp.int32)
    tokens, quarter = hidden.shape
    half = 2 * quarter
    full_width = 4 * quarter
    piece = half // 4
    ch = w_xin.shape[1]
    nq = w_query.shape[1]
    nkv = w_kv.shape[2]
    nbc = w_bc.shape[1]
    heads = w_dt.shape[1]
    ff = w_down.shape[0]
    cq = convx_bias.shape[0]
    hq = dt_bias.shape[0]

    run = Chain()
    cols = ch + nbc + LANES + ch + nq + nkv
    inner = ch + nq

    near = [1 << b for b in range(count.bit_length() - 1)]
    turned = [near[1], near[0]] + near[2:]
    size = half // count
    within = jnp.asarray(np.tile(np.arange(size), count), jnp.int32)
    both_within = jnp.concatenate([within, within + size])

    def block_order(steps):
        return jnp.asarray(np.repeat(np.array(halving_order(steps)), size), jnp.int32) ^ me

    near_block = block_order(near)
    turned_both = jnp.concatenate([block_order(turned)] * 2)
    order_near = (near_block * size + within)[None]
    order_down = (turned_both * (ff // count) + both_within)[None]
    m_rows = ch // count
    a_rows = nq // count
    order_mix = jnp.where(
        both_within < m_rows,
        turned_both * m_rows + both_within,
        ch + turned_both * a_rows + both_within - m_rows,
    )[None]

    def padded(value):
        return jnp.pad(value, (0, LANES - hq))

    small = jnp.concatenate(
        [convx_weight.T.reshape(-1), convx_bias, norm2_gain, padded(dt_bias), padded(a_log), padded(d_skip)]
    )
    small_rows = 16 * pl.cdiv(small.shape[0] // LANES + 8, 16)
    small = jnp.pad(small, (0, small_rows * LANES - small.shape[0])).reshape(small_rows, LANES)
    gu = w_gateup.reshape(half, 2 * ff)
    mine = run(
        pieces_kernel,
        [((inner + 3 * ff + 4 * tokens + small_rows, piece), BF16)],
        place, w_mixout, w_attnout, w_down, gu, cotangent, hidden, small,
        smem=(0,),
    )[0]
    got = swap(mine, "row")
    wk = w_kv.reshape(half, nkv)
    wd = jnp.pad(w_dt, ((0, 0), (0, LANES - heads)))
    gain_one = norm1_gain.astype(F32)[None]
    t_first, g_first, in_pair, x_par, head_par, gain_two = run(
        lambda *refs: split_kernel(heads, *refs),
        [
            ((inner + ff, piece), BF16),
            ((piece, 2 * ff), BF16),
            ((4 * tokens, quarter), BF16),
            ((8, ch), F32),
            ((8, LANES), F32),
            ((1, full_width), F32),
        ],
        place, got, cotangent, hidden, small,
        smem=(0,),
    )
    t_second = swap(t_first, "dp", 1)
    g_second = swap(g_first, "dp", 2)
    in_came = swap(in_pair, "col")
    n1, part, part_low, own, far, factor1 = run(
        project_kernel,
        [
            ((tokens, half), BF16),
            ((tokens, cols), F32),
            ((tokens, cols), BF16),
            ((tokens, half), BF16),
            ((tokens, half), BF16),
            ((tokens, LANES), F32),
        ],
        place, in_pair, in_came, gain_one, w_xin, w_bc, wd, w_gate, w_query, wk,
        smem=(0,), scratch=[((tokens, half), BF16)],
    )
    part_came = swap(part_low, "row")
    t_cat, g_cat, left1 = run(
        hop_kernel,
        [((inner + ff, 2 * piece), BF16), ((2 * piece, 2 * ff), BF16), ((tokens, half), BF16)],
        t_first, t_second, g_first, g_second, n1, order_near,
    )
    t_pair = swap(t_cat, "dp", 2)
    g_pair = swap(g_cat, "dp", 1)

    bc_par = jnp.concatenate(
        [convbc_weight.T, convbc_bias[None], jnp.zeros((3, nbc), BF16)], 0
    ).astype(F32)
    seg_row = segment_ids.astype(F32)
    seg_col = jnp.broadcast_to(segment_ids[0].astype(F32)[:, None], (tokens, LANES))

    mixed, raw, pre, ys = run(
        lambda *refs: mix_kernel(ch, nq, *refs),
        [
            ((tokens, inner), BF16),
            ((tokens, cols), F32),
            ((tokens, ch + nbc), F32),
            ((tokens, ch), F32),
        ],
        seg_row, seg_col, part, part_came, x_par, bc_par, head_par,
    )
    mix_part = run(
        out_kernel,
        [((tokens, full_width), F32)],
        mixed, w_mixout, w_attnout, t_first, t_second, t_pair,
    )[0]
    mix_came = swap(mix_part, "col")
    dy_own, dy_far, grad_act = run(
        lambda *refs: act_grad_kernel(inner, *refs),
        [((tokens, half), BF16), ((tokens, half), BF16), ((tokens, ff), F32)],
        place, in_pair, in_came, w_down, t_first, t_second, t_pair,
        smem=(0,), scratch=[((tokens, half), BF16)],
    )
    h2, n2, act, ggu, n2_part, down_keep, down_send = run(
        feed_kernel,
        [
            ((tokens, full_width), F32),
            ((tokens, half), BF16),
            ((tokens, ff), BF16),
            ((tokens, 2 * ff), BF16),
            ((tokens, full_width), F32),
            ((tokens, quarter), F32),
            ((tokens, quarter), F32),
        ],
        place, own, far, mix_part, mix_came, gain_two,
        gu, g_first, g_second, g_pair, grad_act, w_down,
        smem=(0,),
    )
    n2_came = swap(n2_part, "col")
    down_came = swap(down_send, "col")
    rows = half // 2

    g_send, d_send, g_left, d_left = run(
        feed_grad_kernel,
        [
            ((rows, 2 * ff), BF16),
            ((rows, 2 * half), BF16),
            ((tokens, rows), BF16),
            ((tokens, half), BF16),
        ],
        n2, act, ggu, dy_own, order_near, order_down,
    )
    g_came = swap(g_send, "dp", near[0])
    d_came = swap(d_send, "dp", turned[0])
    dym, resid, low, gain2_sum, output, m_send, m_left, g_two, two_send = run(
        lambda *refs: turn_kernel(ch, nq, *refs),
        [
            ((tokens, inner), F32),
            ((tokens, half), F32),
            ((tokens, half), BF16),
            ((8, half), F32),
            ((tokens, quarter), BF16),
            ((rows, 2 * half), BF16),
            ((tokens, half), BF16),
            ((tokens, ch + nq + nkv), BF16),
            ((rows, ch + nq + nkv), BF16),
        ],
        place, dy_own, dy_far, h2, n2_part, n2_came, gain_two,
        w_mixout, w_attnout, t_first, t_second, t_pair, down_keep, down_came,
        mixed, order_mix, seg_row, seg_col, raw, pre, ys, x_par, left1,
        smem=(0,),
    )
    two_came = swap(two_send, "dp", near[0])
    m_came = swap(m_send, "dp", turned[0])
    gx, gdt, gbc, small_sum = run(
        lambda *refs: unmix_one_kernel(ch, nq, *refs),
        [
            ((tokens, ch), BF16),
            ((tokens, LANES), BF16),
            ((tokens + 8, nbc), F32),
            ((16, ch), F32),
        ],
        seg_row, seg_col, raw, pre, ys, dym, x_par, bc_par, head_par,
        scratch=[((tokens, ch), F32), ((tokens, ch), F32), ((tokens, tokens), F32)],
    )
    gbc_came = swap(gbc, "col")

    def quarters(width):
        return [((rows // 2, width), BF16), ((rows // 2, width), F32)]

    g_send, g_keep = run(wide_kernel, quarters(2 * ff), g_left, ggu, g_came)
    s_gu = halve(run, near, 1, g_send, g_keep, last_kernel, [((size, 2 * ff), F32)])
    next(s_gu)
    n1_part, n1_bc, gbc_both, one_send = run(
        back_kernel,
        [
            ((tokens, half), F32),
            ((tokens, half), F32),
            ((tokens, nbc), BF16),
            ((rows, ch + nbc + LANES), BF16),
        ],
        g_two, gx, gdt, gbc, gbc_came, w_xin, w_bc, wd, w_gate, w_query, wk, left1,
    )
    one_came = swap(one_send, "dp", near[0])
    n1_came = swap(n1_part, "col")
    tall_send, tall_keep = run(
        tall_kernel, quarters(4 * half), d_left, dy_own, d_came, m_left, low, m_came
    )
    s_tall = halve(
        run, turned, 1, tall_send, tall_keep, last_tall_kernel,
        [((2 * size, half), F32), ((m_rows, half), F32), ((a_rows, half), F32)],
    )
    next(s_tall)
    two_send, two_keep = run(wide_kernel, quarters(ch + nq + nkv), left1, g_two, two_came)
    s_two = halve(
        run, near, 1, two_send, two_keep, last_kernel,
        [((size, ch), F32), ((size, nq), F32), ((size, nkv), F32)],
    )
    next(s_two)
    dn1, sum_rows = run(
        close_kernel,
        [((tokens, half), F32), ((16, tokens), F32)],
        own, n1_part, n1_came, n1_bc, gain_one, gbc, gbc_came,
    )
    rows_far = swap(sum_rows, "row")
    r_gu = next(s_gu)
    grad_hidden, vector = run(
        end_kernel,
        [((tokens, quarter), F32), ((32, ch), F32)],
        place, own, factor1, resid, dn1, gain_one, sum_rows, rows_far, small_sum, gain2_sum,
        smem=(0,),
    )
    vector_came = swap(vector, "dp", near[0])
    r_two = next(s_two)
    r_gu = r_gu or next(s_gu)
    r_two = r_two or next(s_two)
    r_tall = next(s_tall)

    def one_outs(keep):
        width = ch + nbc + LANES
        return [((keep + 64, width), BF16), ((keep, width), F32), ((32, ch), F32)]

    one_send, one_keep, vector = run(
        one_kernel, one_outs(rows // 2),
        left1, gx, gbc_both, gdt, one_came, vector, vector_came,
    )
    r_tall = r_tall or next(s_tall)
    for step in near[1:-1]:
        one_came = swap(one_send, "dp", step)
        one_send, one_keep, vector = run(
            one_stage_kernel, one_outs(one_keep.shape[0] // 2), one_keep, one_came, vector
        )
        r_gu = r_gu or next(s_gu)
        r_tall = r_tall or next(s_tall)
        r_two = r_two or next(s_two)
    one_came = swap(one_send, "dp", near[-1])
    r_gu = r_gu or next(s_gu)
    r_tall = r_tall or next(s_tall)
    r_two = r_two or next(s_two)
    (
        r_xin, r_bc, r_dt, o_norm1, o_norm2, o_cxw, o_cxb, o_cbw, o_cbb, o_dtb, o_alog, o_dsk
    ) = run(
        lambda *refs: one_last_kernel(heads, *refs),
        [
            ((size, ch), F32),
            ((size, nbc), F32),
            ((size, heads), F32),
            ((1, half), F32),
            ((1, half), F32),
            ((TAPS, cq), F32),
            ((1, cq), F32),
            ((TAPS, nbc), F32),
            ((1, nbc), F32),
            ((1, hq), F32),
            ((1, hq), F32),
            ((1, hq), F32),
        ],
        place, one_keep, one_came, vector,
        smem=(0,),
    )
    r_gate, r_query, r_kv = r_two
    r_down, r_mixout, r_attnout = r_tall
    return (
        output,
        grad_hidden,
        o_norm1[0],
        r_gate,
        r_xin,
        r_dt,
        r_bc,
        r_query,
        r_kv.reshape(size, 1, nkv),
        o_cxw.T,
        o_cxb[0],
        o_cbw.T,
        o_cbb[0],
        o_dtb[0],
        o_alog[0],
        o_dsk[0],
        r_mixout,
        r_attnout,
        o_norm2[0],
        r_gu[0].reshape(size, 2, ff),
        r_down,
    )


def solution(mesh):
    placed = (
        P("dp", ("row", "col")),
        P("dp", None),
        P("row"),
        P("row", "col"),
        P("row", "col"),
        P("row", "col"),
        P("row", None),
        P("row", "col"),
        P("row", "col", None),
        P(("col", "row"), None),
        P(("col", "row")),
        P(),
        P(),
        P(("col", "row")),
        P(("col", "row")),
        P(("col", "row")),
        P("col", "row"),
        P("col", "row"),
        P("row"),
        P("row", None, "col"),
        P("col", "row"),
        P("dp", ("row", "col")),
    )
    return jax.shard_map(
        shards,
        mesh=mesh,
        in_specs=placed,
        out_specs=(
            P("dp", ("row", "col")),
            P("dp", ("row", "col")),
            P("row"),
            P(("row", "dp"), "col"),
            P(("row", "dp"), "col"),
            P(("row", "dp"), "col"),
            P(("row", "dp"), None),
            P(("row", "dp"), "col"),
            P(("row", "dp"), "col", None),
            P(("col", "row"), None),
            P(("col", "row")),
            P(),
            P(),
            P(("col", "row")),
            P(("col", "row")),
            P(("col", "row")),
            P(("col", "dp"), "row"),
            P(("col", "dp"), "row"),
            P("row"),
            P(("row", "dp"), None, "col"),
            P(("col", "dp"), "row"),
        ),
        check_vma=False,
    )
```

```python
import jax
import jax.numpy as jnp
import numpy as np
from jax import lax
from jax.experimental import pallas as pl
from jax.experimental.pallas import tpu as pltpu
from jax.sharding import PartitionSpec as P

NORM_EPS = 1e-05
F32 = jnp.float32
BF16 = jnp.bfloat16
HEAD = 64
LANES = 128
TAPS = 4
FAR = -1e30


def swap(values, axis, step=1):
    count = lax.axis_size(axis)
    return lax.ppermute(values, axis, [(i, i ^ step) for i in range(count)])


def dot(left, right):
    return jnp.dot(left, right, preferred_element_type=F32)


def dot_bt(left, right):
    return lax.dot_general(left, right, (((1,), (1,)), ((), ())), preferred_element_type=F32)


def dot_at(left, right):
    return lax.dot_general(left, right, (((0,), (0,)), ((), ())), preferred_element_type=F32)


def fine(left, right, dims=((1,), (0,))):
    return lax.dot_general(
        left, right, (dims, ((), ())), precision=lax.Precision.HIGHEST, preferred_element_type=F32
    )


class Chain:
    def __init__(self):
        self.token = jnp.zeros((8, LANES), F32)

    def __call__(self, kernel, outs, *args, scratch=(), smem=(), after=()):
        plain = pltpu.VMEM
        specs = [
            pl.BlockSpec(memory_space=pltpu.SMEM if i in smem else plain)
            for i in range(len(args))
        ]
        extra = (self.token,) + tuple(after)
        count = len(args)
        held = count + len(extra)

        def body(*refs):
            refs[held][...] = jnp.zeros((8, LANES), F32)
            kernel(*refs[:count], *refs[held + 1 :])

        results = pl.pallas_call(
            body,
            out_shape=[jax.ShapeDtypeStruct((8, LANES), F32)]
            + [jax.ShapeDtypeStruct(s, d) for s, d in outs],
            in_specs=specs + [pl.BlockSpec(memory_space=pl.ANY)] * len(extra),
            out_specs=[pl.BlockSpec(memory_space=pltpu.VMEM)]
            + [pl.BlockSpec(memory_space=plain)] * len(outs),
            scratch_shapes=[pltpu.VMEM(s, d) if d is not None else s for s, d in scratch],
            compiler_params=pltpu.CompilerParams(vmem_limit_bytes=62 << 20),
            cost_estimate=pl.CostEstimate(flops=0, bytes_accessed=0, transcendentals=0),
        )(*args, *extra)
        self.token = results[0]
        return results[1:]


def two_parts(value):
    high = value.astype(BF16)
    return high, (value - high.astype(F32)).astype(BF16)


def dot_three(product, left, right):
    return product(left[0], right[0]) + (product(left[1], right[0]) + product(left[0], right[1]))


def iota(shape, dim):
    return lax.broadcasted_iota(jnp.int32, shape, dim)


def column(row_vector):
    ones = jnp.full((row_vector.shape[0], LANES), 1.0 / row_vector.shape[0], F32)
    return fine(row_vector, ones, ((0,), (0,)))


def token_sums(values):
    return fine(jnp.ones((8, values.shape[1]), F32), values, ((1,), (1,)))


def pieces_kernel(place, wm, wa, wd, gu, cot, hid, small, out):
    piece = out.shape[1]
    at = pl.multiple_of(place[1] * piece, piece)
    row = 0
    for w in (wm, wa, wd):
        out[row : row + w.shape[0]] = w[:, pl.ds(at, piece)]
        row += w.shape[0]
    for value in (gu, cot, hid):
        for j in range(value.shape[1] // piece):
            out[row : row + value.shape[0]] = value[:, j * piece : (j + 1) * piece]
            row += value.shape[0]
    out[row:] = small[...]


def join_small(place, heads, own, far, x_par_out, head_out, gain_out):
    first = place[2] == 0
    a = jnp.where(first, own, far)
    b = jnp.where(first, far, own)
    width = x_par_out.shape[1] // 2
    count = width // LANES
    x_par_out[...] = jnp.zeros_like(x_par_out)
    for k in range(TAPS + 1):
        for i in range(count):
            at = k * count + i
            x_par_out[k : k + 1, i * LANES : (i + 1) * LANES] = a[at : at + 1]
            x_par_out[k : k + 1, width + i * LANES : width + (i + 1) * LANES] = b[at : at + 1]
    row = (TAPS + 1) * count
    pieces = gain_out.shape[1] // (2 * LANES)
    for j in range(pieces):
        gain_out[:, j * LANES : (j + 1) * LANES] = own[row + j : row + j + 1]
        block = jnp.zeros((1, LANES), F32)
        for i in range(pieces):
            block = block + jnp.where((place[1] ^ j) == i, far[row + i : row + i + 1], 0.0)
        at = (pieces + j) * LANES
        gain_out[:, at : at + LANES] = block
    row += pieces
    joined = a[row : row + 8] + pltpu.roll(b[row : row + 8], heads // 2, 1)
    head_out[...] = joined
    pick = jnp.where(
        iota((LANES, 2 * width), 0) == iota((LANES, 2 * width), 1) // HEAD, 1.0, 0.0
    )
    x_par_out[TAPS + 1 : TAPS + 2] = fine(joined, pick)[2:3]


def split_kernel(
    heads, place, got, cot, small, t_out, g_out, pair_out, x_par_out, head_out, gain_out
):
    piece = got.shape[1]
    tokens = cot.shape[0]
    row = t_out.shape[0]
    t_out[...] = got[0:row]
    for j in range(g_out.shape[1] // piece):
        g_out[:, j * piece : (j + 1) * piece] = got[row : row + piece]
        row += piece
    pair_out[0:tokens] = cot[...]
    for i in (1, 2):
        for j in range(cot.shape[1] // piece):
            pair_out[i * tokens : (i + 1) * tokens, j * piece : (j + 1) * piece] = got[
                row : row + tokens
            ]
            row += tokens
    own = small[...].astype(F32)
    far = got[row:].astype(F32)
    join_small(place, heads, own, far, x_par_out, head_out, gain_out)


def far_order(place, value, out):
    piece = value.shape[1] // 4
    for j in range(4):
        at = pl.multiple_of((place[1] ^ j) * piece, piece)
        out[:, j * piece : (j + 1) * piece] = value[:, pl.ds(at, piece)]


def side_by_side(place, a, b, out):
    width = a.shape[1]
    first = place[0] == 0
    out[:, :width] = jnp.where(first, a, b)
    out[:, width:] = jnp.where(first, b, a)


def project_kernel(place, mine, came, gain, wx, wb, wd, wg, wq, wk, own_out, p_out, low_out):
    side_by_side(place, mine[...], came[...], own_out)
    high, low = two_parts(own_out[...].astype(F32) * gain[...])
    at = 0
    for w in (wx, wb, wd, wg, wq, wk):
        size = w.shape[1]
        part = dot(high, w[...]) + dot(low, w[...])
        p_out[:, at : at + size] = part
        low_out[:, at : at + size] = part.astype(BF16)
        at += size


def norm_kernel(
    place, pair, came, own, gain, order,
    far_out, dy_own, dy_far, factor_out, n1_out, left_out, far_tmp,
):
    tokens = own.shape[0]
    side_by_side(place, pair[0:tokens], came[0:tokens], dy_own)
    side_by_side(place, pair[tokens : 2 * tokens], came[tokens : 2 * tokens], far_tmp)
    far_order(place, far_tmp, dy_far)
    side_by_side(place, pair[2 * tokens :], came[2 * tokens :], far_tmp)
    far_order(place, far_tmp, far_out)
    hid = own[...].astype(F32)
    far = far_out[...].astype(F32)
    mean = jnp.sum(hid * hid + far * far, axis=1, keepdims=True) / (2 * hid.shape[1])
    factor = lax.rsqrt(mean + NORM_EPS)
    factor_out[...] = jnp.broadcast_to(factor, factor_out.shape)
    n1_out[...] = (hid * factor * gain[...]).astype(BF16)
    left_out[...] = permuted(n1_out[...], order[...])


def masks(seg_row, seg_col, turned):
    tokens = seg_row.shape[1]
    i = iota((tokens, tokens), 1 if turned else 0)
    j = iota((tokens, tokens), 0 if turned else 1)
    same = seg_col[:, :1] == seg_row[...]
    return jnp.where((i >= j) & same, 0.0, FAR)


def valids(seg_col):
    seg = seg_col[...]
    t = iota(seg.shape, 0)
    return [
        jnp.where((t >= k) & (pltpu.roll(seg, k, 0) == seg), 1.0, 0.0) for k in range(1, TAPS)
    ]


def conv(block, taps, bias, valid):
    total = block * taps[TAPS - 1 : TAPS] + bias
    for k in range(1, TAPS):
        total = total + (pltpu.roll(block, k, 0) * valid[k - 1]) * taps[TAPS - 1 - k : TAPS - k]
    return total


def conv_turn(grad, block, taps, valid):
    tokens = grad.shape[0]
    back = grad * taps[TAPS - 1 : TAPS]
    rows = [None] * TAPS
    rows[TAPS - 1] = jnp.sum(grad * block, axis=0, keepdims=True)
    for k in range(1, TAPS):
        kept = grad * valid[k - 1]
        back = back + pltpu.roll(kept, tokens - k, 0) * taps[TAPS - 1 - k : TAPS - k]
        rows[TAPS - 1 - k] = jnp.sum(kept * pltpu.roll(block, k, 0), axis=0, keepdims=True)
    rows.append(jnp.sum(grad, axis=0, keepdims=True))
    rows.append(jnp.zeros((8 - len(rows), grad.shape[1]), F32))
    return back, jnp.concatenate(rows, 0)


def silu_turn(value):
    sig = jax.nn.sigmoid(value)
    return value * sig, sig * (1.0 + value * (1.0 - sig))


def steps(dt_raw, head_par):
    shifted = dt_raw + head_par[0:1]
    return jnp.maximum(shifted, 0.0) + jnp.log1p(jnp.exp(-jnp.abs(shifted)))


def mix_kernel(
    ch, nq, seg_row, seg_col, factor, own, came, x_par, bc_par, head_par,
    mixed_out, sums_out, pre_out, y_out,
):
    tokens = own.shape[0]
    nbc = bc_par.shape[1]
    state = nbc // 2
    sums_out[...] = factor[:, :1] * (own[...] + came[...].astype(F32))
    lane = iota((tokens, LANES), 1)
    low = lane < HEAD
    mask = masks(seg_row, seg_col, False)
    valid = valids(seg_col)
    for b in range(nbc // LANES):
        at = ch + b * LANES
        part = slice(b * LANES, (b + 1) * LANES)
        pre_out[:, at : at + LANES] = conv(
            sums_out[:, at : at + LANES], bc_par[0:TAPS, part], bc_par[TAPS : TAPS + 1, part], valid
        )
    bcc = pre_out[:, ch : ch + nbc]
    bcc = bcc * jax.nn.sigmoid(bcc)
    inner = fine(bcc[:, state:], bcc[:, :state], ((1,), (1,)))
    dt = steps(sums_out[:, ch + nbc : ch + nbc + LANES], head_par)
    tri = jnp.where(iota((tokens, tokens), 0) >= iota((tokens, tokens), 1), 1.0, 0.0)
    cum = fine(tri, dt * -jnp.exp(head_par[1:2]))
    cum_row = cum.T
    base = ch + nbc + LANES
    for p in range(ch // LANES):
        part = slice(p * LANES, (p + 1) * LANES)
        pre = conv(sums_out[:, part], x_par[0:TAPS, part], x_par[TAPS : TAPS + 1, part], valid)
        pre_out[:, part] = pre
        xc = pre * jax.nn.sigmoid(pre)
        h = 2 * p
        xdt = (xc * jnp.where(low, dt[:, h : h + 1], dt[:, h + 1 : h + 2])).astype(BF16)
        ys = []
        for e in (h, h + 1):
            decay = jnp.exp((cum[:, e : e + 1] - cum_row[e : e + 1]) + mask)
            ys.append(dot((inner * decay).astype(BF16), xdt))
        y = jnp.where(low, ys[0], ys[1])
        y_out[:, part] = y
        y = y + x_par[TAPS + 1 : TAPS + 2, part] * xc
        z = sums_out[:, base + p * LANES : base + (p + 1) * LANES]
        mixed_out[:, part] = (y * (z * jax.nn.sigmoid(z))).astype(BF16)
    at = base + ch
    kv = sums_out[:, at + nq : at + nq + LANES]
    kv_turn = pltpu.roll(kv, HEAD, 1)
    keys = two_parts(jnp.where(low, kv, kv_turn))
    vals = two_parts(jnp.where(low, kv_turn, kv))
    for p in range(nq // LANES):
        query = sums_out[:, at + p * LANES : at + (p + 1) * LANES] * (HEAD ** -0.5)
        outs = []
        for side in (low, ~low):
            score = dot_three(dot_bt, two_parts(jnp.where(side, query, 0.0)), keys) + mask
            score = jnp.exp(score - jnp.max(score, axis=1, keepdims=True))
            total = jnp.sum(score, axis=1, keepdims=True)
            outs.append(dot_three(dot, two_parts(score), vals) / total)
        mixed_out[:, ch + p * LANES : ch + (p + 1) * LANES] = jnp.where(
            low, outs[0], outs[1]
        ).astype(BF16)


def unmix_two_kernel(ch, nq, seg_row, seg_col, sums, pre, ys, dym, x_par, gtwo_out):
    tokens = sums.shape[0]
    base = sums.shape[1] - (ch + nq + LANES)
    low = iota((tokens, LANES), 1) < HEAD
    mask = masks(seg_row, seg_col, True)
    for p in range(ch // LANES):
        part = slice(p * LANES, (p + 1) * LANES)
        value = pre[:, part]
        xc = value * jax.nn.sigmoid(value)
        _, gate_turn = silu_turn(sums[:, base + p * LANES : base + (p + 1) * LANES])
        y = ys[:, part] + x_par[TAPS + 1 : TAPS + 2, part] * xc
        gtwo_out[:, part] = (dym[:, part] * y * gate_turn).astype(BF16)
    at = base + ch
    kv = sums[:, at + nq : at + nq + LANES]
    kv_turn = pltpu.roll(kv, HEAD, 1)
    keys = jnp.where(low, kv, kv_turn).astype(BF16)
    vals = jnp.where(low, kv_turn, kv).astype(BF16)
    dk = jnp.zeros((tokens, LANES), F32)
    dv = jnp.zeros((tokens, LANES), F32)
    for p in range(nq // LANES):
        query = sums[:, at + p * LANES : at + (p + 1) * LANES] * (HEAD ** -0.5)
        grad = dym[:, ch + p * LANES : ch + (p + 1) * LANES]
        dqs = []
        for side in (low, ~low):
            q_low = jnp.where(side, query, 0.0).astype(BF16)
            g_low = jnp.where(side, grad, 0.0).astype(BF16)
            score = dot_bt(keys, q_low) + mask
            score = jnp.exp(score - jnp.max(score, axis=0, keepdims=True))
            prob = score * (1.0 / jnp.sum(score, axis=0, keepdims=True))
            dprob = dot_bt(vals, g_low)
            dv = dv + dot(prob.astype(BF16), g_low)
            inner_sum = jnp.sum(prob * dprob, axis=0, keepdims=True)
            dscore = (prob * (dprob - inner_sum)).astype(BF16)
            dk = dk + dot(dscore, q_low)
            dqs.append(dot_at(dscore, keys))
        gtwo_out[:, ch + p * LANES : ch + (p + 1) * LANES] = (
            jnp.where(low, dqs[0], dqs[1]) * (HEAD ** -0.5)
        ).astype(BF16)
    dk = dk + pltpu.roll(dk, HEAD, 1)
    dv = dv + pltpu.roll(dv, HEAD, 1)
    gtwo_out[:, ch + nq : ch + nq + LANES] = jnp.where(low, dk, dv).astype(BF16)

def unmix_one_kernel(
    ch, nq, seg_row, seg_col, sums, pre, ys, dym, x_par, bc_par, head_par,
    gx_out, gdt_out, gbc_out, small_out, prod_a, prod_b, turned,
):
    tokens = sums.shape[0]
    nbc = bc_par.shape[1]
    state = nbc // 2
    lane = iota((tokens, LANES), 1)
    low = lane < HEAD
    mask = masks(seg_row, seg_col, True)
    valid = valids(seg_col)
    bc_pre = pre[:, ch : ch + nbc]
    bcc, bcc_turn = silu_turn(bc_pre)
    b_in = bcc[:, :state]
    c_in = bcc[:, state:]
    inner = fine(b_in, c_in, ((1,), (1,)))
    dt_raw = sums[:, ch + nbc : ch + nbc + LANES]
    dt = steps(dt_raw, head_par)
    rate = jnp.exp(head_par[1:2])
    tri = jnp.where(iota((tokens, tokens), 0) >= iota((tokens, tokens), 1), 1.0, 0.0)
    cum = fine(tri, dt * -rate)
    cum_row = cum.T
    base = ch + nbc + LANES
    small_out[...] = jnp.zeros_like(small_out)
    turned[...] = jnp.zeros_like(turned)
    for p in range(ch // LANES):
        part = slice(p * LANES, (p + 1) * LANES)
        xc, xc_turn = silu_turn(pre[:, part])
        skip = x_par[TAPS + 1 : TAPS + 2, part]
        z = sums[:, base + p * LANES : base + (p + 1) * LANES]
        gate = z * jax.nn.sigmoid(z)
        dy_in = dym[:, part]
        y = ys[:, part]
        dy = dy_in * gate
        h = 2 * p
        dt_pair = jnp.where(low, dt[:, h : h + 1], dt[:, h + 1 : h + 2])
        xdt = xc * dt_pair
        dy_low = dy.astype(BF16)
        x_low = xdt.astype(BF16)
        sides = []
        for e, side in ((h, low), (h + 1, ~low)):
            decay = jnp.exp((cum_row[e : e + 1] - cum[:, e : e + 1]) + mask)
            turned[...] += dot_bt(jnp.where(side, xdt, 0.0).astype(BF16), dy_low) * decay
            sides.append(dot((inner * decay).astype(BF16), dy_low))
        dxdt = jnp.where(low, sides[0], sides[1])
        prod_a[:, part] = dy_low.astype(F32) * y - x_low.astype(F32) * dxdt
        prod_b[:, part] = dxdt * xc
        small_out[8 + TAPS + 1 : 8 + TAPS + 2, part] = jnp.sum(dy * xc, axis=0, keepdims=True)
        dpre = (skip * dy + dxdt * dt_pair) * xc_turn
        back, rows = conv_turn(dpre, sums[:, part], x_par[0:TAPS, part], valid)
        gx_out[:, part] = back.astype(BF16)
        small_out[0:8, part] = rows
    pick = jnp.where(iota((ch, LANES), 0) // HEAD == iota((ch, LANES), 1), 1.0, 0.0)
    dcum = fine(prod_a[...], pick)
    ddt = fine(prod_b[...], pick)
    after = fine(tri, dcum, ((0,), (0,)))
    ddt = ddt - rate * after
    ddt = ddt * jax.nn.sigmoid(dt_raw + head_par[0:1])
    gdt_out[...] = ddt.astype(BF16)
    small_out[8 + TAPS : 8 + TAPS + 1, 0:LANES] = jnp.sum(ddt, axis=0, keepdims=True)
    small_out[8 + TAPS : 8 + TAPS + 1, LANES : 2 * LANES] = jnp.sum(
        after * (-dt * rate), axis=0, keepdims=True
    )
    skip_sum = jnp.broadcast_to(small_out[8 + TAPS + 1 : 8 + TAPS + 2, :], (8, ch))
    small_out[8 + TAPS : 8 + TAPS + 1, 2 * LANES : 3 * LANES] = fine(skip_sum, pick)[0:1]
    dinner = turned[...]
    d_b = fine(dinner, c_in) * bcc_turn[:, :state]
    d_c = fine(dinner, b_in, ((0,), (0,))) * bcc_turn[:, state:]
    for b, grad in enumerate((d_b, d_c)):
        at = ch + b * LANES
        part = slice(b * LANES, (b + 1) * LANES)
        back, rows = conv_turn(grad, sums[:, at : at + LANES], bc_par[0:TAPS, part], valid)
        gbc_out[0:tokens, part] = back
        gbc_out[tokens : tokens + 8, part] = rows


def tall_far(fetch, start, size):
    return jnp.concatenate(
        [r[start : start + size] for r in fetch], axis=1
    )


def out_kernel(mixed, wm, wa, t0, t1, t2, t3, part_out):
    fetch = (t0, t1, t2, t3)
    half = wm.shape[1]
    ch = wm.shape[0]
    value = mixed[...]
    part_out[:, :half] = dot(value[:, :ch], wm[...]) + dot(value[:, ch:], wa[...])
    part_out[:, half:] = dot(value, tall_far(fetch, 0, value.shape[1]))


def norm_factor(value):
    return lax.rsqrt(jnp.mean(value * value, axis=1, keepdims=True) + NORM_EPS)


def act_grad_kernel(inner, dy_own, dy_far, wd, t0, t1, t2, t3, ga_out):
    fetch = (t0, t1, t2, t3)
    ff = wd.shape[0]
    ga_out[...] = dot_bt(dy_own[...], wd[...]) + dot_bt(
        dy_far[...], tall_far(fetch, inner, ff)
    )


def feed_kernel(
    place, own, far, part, came, gain, gu, gu0, gu1, gu2, gu3, grad_act, wd,
    h2_out, n2_out, act_out, ggu_out, n2p_out, keep_out, send_out,
):
    half = own.shape[1]
    quarter = half // 2
    h2_out[:, :half] = own[...].astype(F32) + (part[:, :half] + came[:, :half])
    h2_out[:, half:] = far[...].astype(F32) + (part[:, half:] + came[:, half:])
    h2 = h2_out[...]
    n2 = (h2 * norm_factor(h2) * gain[...]).astype(BF16)
    n2_out[...] = n2[:, :half]
    gu_far = jnp.concatenate([gu0[...], gu1[...], gu2[...], gu3[...]], axis=0)
    ff = wd.shape[0]
    gate_up = dot(n2[:, :half], gu[...]) + dot(n2[:, half:], gu_far)
    gate = gate_up[:, :ff]
    up = gate_up[:, ff:]
    silu, silu_grad = silu_turn(gate)
    act = (silu * up).astype(BF16)
    act_out[...] = act
    ga = grad_act[...]
    ggu_out[:, :ff] = (ga * up * silu_grad).astype(BF16)
    ggu_out[:, ff:] = (ga * silu).astype(BF16)
    ggu = ggu_out[...]
    n2p_out[:, :half] = dot_bt(ggu, gu[...])
    n2p_out[:, half:] = dot_bt(ggu, gu_far)
    down = dot(act, wd[...])
    first = place[0] == 0
    keep_out[...] = jnp.where(first, down[:, :quarter], down[:, quarter:])
    send_out[...] = jnp.where(first, down[:, quarter:], down[:, :quarter])


def permuted(left, source):
    width = left.shape[1]
    hot = jnp.where(iota((width, source.shape[1]), 0) == source, 1.0, 0.0).astype(BF16)
    return dot(left, hot).astype(BF16)


def feed_grad_kernel(
    n2, act, ggu, dy, order, order2, g_send, d_send, g_left, d_left
):
    rows = g_send.shape[0]
    width = dy.shape[1]
    left = permuted(n2[...], order[...])
    g_send[...] = dot_at(left[:, rows:], ggu[...]).astype(BF16)
    g_left[...] = left[:, :rows]
    left = permuted(act[...], order2[...])
    for s in (0, 1):
        cut = 2 * s * rows
        d_send[:, s * width : (s + 1) * width] = dot_at(
            left[:, cut + rows : cut + 2 * rows], dy[...]
        ).astype(BF16)
        d_left[:, s * rows : (s + 1) * rows] = left[:, cut : cut + rows]


def turn_kernel(
    ch, nq, place, dy_own, dy_far, h2, part, came, gain, wm, wa, t0, t1, t2, t3, d_keep, d_came,
    mixed, order_mix, seg_row, seg_col, sums, pre, ys, x_par, left1,
    dym_out, resid_out, low_out, gain_out, output_out, m_send, m_left, gtwo_out, two_send,
):
    fetch = (t0, t1, t2, t3)
    half = dy_own.shape[1]
    quarter = half // 2
    value = h2[...]
    output_out[...] = (
        jnp.where(place[0] == 0, value[:, :quarter], value[:, quarter:half])
        + (d_keep[...] + d_came[...])
    ).astype(BF16)
    factor = norm_factor(value)
    dn2 = part[...] + came[...]
    gained = dn2 * gain[...]
    inner_sum = jnp.sum(gained * value, axis=1, keepdims=True)
    gain_out[...] = jnp.broadcast_to(
        jnp.sum(dn2[:, :half] * value[:, :half] * factor, axis=0, keepdims=True), gain_out.shape
    )
    slope = factor * factor * factor * inner_sum / (2 * half)
    change = factor * gained - value * slope
    dh_own = dy_own[...].astype(F32) + change[:, :half]
    dh_far = dy_far[...].astype(F32) + change[:, half:]
    resid_out[...] = dh_own
    low_own = dh_own.astype(BF16)
    low_out[...] = low_own
    dym = dot_bt(dh_far.astype(BF16), tall_far(fetch, 0, dym_out.shape[1]))
    dym_out[:, :ch] = dym[:, :ch] + dot_bt(low_own, wm[...])
    dym_out[:, ch:] = dym[:, ch:] + dot_bt(low_own, wa[...])
    unmix_two_kernel(ch, nq, seg_row, seg_col, sums, pre, ys, dym_out, x_par, gtwo_out)
    rows = two_send.shape[0]
    two_send[...] = dot_at(left1[:, rows:], gtwo_out[...]).astype(BF16)
    left = permuted(mixed[...], order_mix[...])
    for s in (0, 1):
        cut = 2 * s * rows
        m_send[:, s * half : (s + 1) * half] = dot_at(
            left[:, cut + rows : cut + 2 * rows], low_own
        ).astype(BF16)
        m_left[:, s * rows : (s + 1) * rows] = left[:, cut : cut + rows]


def back_kernel(
    g_two, gx, gdt, gbc, gbc_came, wx, wb, wd, wg, wq, wk, left1,
    n1p_out, n1b_out, both_out, one_send,
):
    tokens = gx.shape[0]
    both = (gbc[0:tokens] + gbc_came[0:tokens]).astype(BF16)
    both_out[...] = both
    rows = one_send.shape[0]
    left = left1[:, rows:]
    at = 0
    for right in (gx[...], both, gdt[...]):
        size = right.shape[1]
        one_send[:, at : at + size] = dot_at(left, right).astype(BF16)
        at += size
    ch = wg.shape[1]
    nq = wq.shape[1]
    total = dot_bt(gx[...], wx[...]) + dot_bt(gdt[...], wd[...])
    total = total + dot_bt(g_two[:, :ch], wg[...]) + dot_bt(g_two[:, ch : ch + nq], wq[...])
    n1p_out[...] = total + dot_bt(g_two[:, ch + nq :], wk[...])
    n1b_out[...] = dot_bt(both, wb[...])


def store_halves(total, at, send_out, keep_out, skip=0):
    rows = keep_out.shape[0]
    size = total.shape[1]
    send_out[skip:, at : at + size] = total[rows:].astype(BF16)
    keep_out[:, at : at + size] = total[:rows]


def wide_kernel(left, right, came, send_out, keep_out):
    total = dot_at(left[:, : came.shape[0]], right[...]) + came[...].astype(F32)
    store_halves(total, 0, send_out, keep_out)


def tall_kernel(d_left, dy, d_came, m_left, low, m_came, send_out, keep_out):
    at = 0
    for left, right, came in ((d_left, dy, d_came), (m_left, low, m_came)):
        rows = came.shape[0]
        width = right.shape[1]
        for s in (0, 1):
            total = dot_at(left[:, s * rows : (s + 1) * rows], right[...])
            total = total + came[:, s * width : (s + 1) * width].astype(F32)
            store_halves(total, at, send_out, keep_out)
            at += width


def pack_vector(value, out):
    rows, width = value.shape
    high = value.astype(BF16)
    low = (value - high.astype(F32)).astype(BF16)
    out[0:rows, 0:width] = high
    out[rows : 2 * rows, 0:width] = low
    out[0 : 2 * rows, width:] = jnp.zeros((2 * rows, out.shape[1] - width), BF16)
    return high.astype(F32) + low.astype(F32)


def read_vector(came, shape):
    rows, width = shape
    return came[0:rows, 0:width].astype(F32) + came[rows : 2 * rows, 0:width].astype(F32)


def one_kernel(left1, gx, both, gdt, came, vector, vector_came, send_out, keep_out, vector_out):
    left = left1[:, : came.shape[0]]
    skip = 2 * vector.shape[0]
    at = 0
    for right in (gx[...], both[...], gdt[...]):
        size = right.shape[1]
        total = dot_at(left, right) + came[:, at : at + size].astype(F32)
        store_halves(total, at, send_out, keep_out, skip)
        at += size
    vector_out[...] = pack_vector(vector[...] + vector_came[...], send_out)


def one_stage_kernel(keep, came, vector, send_out, keep_out, vector_out):
    skip = 2 * vector.shape[0]
    total = keep[...] + came[skip:].astype(F32)
    store_halves(total, 0, send_out, keep_out, skip)
    vector_out[...] = pack_vector(vector[...] + read_vector(came, vector.shape), send_out)


def one_last_kernel(
    heads, place, keep, came, vector, x_out, bc_out, dt_out,
    n1_out, n2_out, xw_out, xb_out, bw_out, bb_out, dtb_out, alog_out, skip_out,
):
    skip = 2 * vector.shape[0]
    total = keep[...] + came[skip:].astype(F32)
    ch = x_out.shape[1]
    nbc = bc_out.shape[1]
    x_out[...] = total[:, :ch]
    bc_out[...] = total[:, ch : ch + nbc]
    dt_out[...] = total[:, ch + nbc : ch + nbc + heads]
    value = vector[...] + read_vector(came, vector.shape)
    first = place[2] == 0
    half = n1_out.shape[1]
    cq = xb_out.shape[1]
    n1_out[...] = value[6:7, :half]
    n2_out[...] = value[7:8, :half]
    mine = jnp.where(first, value[0:8, :cq], value[0:8, cq : 2 * cq])
    xw_out[...] = mine[0:TAPS]
    xb_out[...] = mine[TAPS : TAPS + 1]
    bw_out[...] = jnp.concatenate(
        [
            value[6:7, half : half + nbc],
            value[7:8, half : half + nbc],
            value[8:9, :nbc],
            value[8:9, nbc : 2 * nbc],
        ],
        axis=0,
    )
    bb_out[...] = value[5:6, 3 * LANES : 3 * LANES + nbc]
    hq = dtb_out.shape[1]
    for i, out in enumerate((dtb_out, alog_out, skip_out)):
        at = i * LANES
        out[...] = jnp.where(
            first, value[5:6, at : at + hq], value[5:6, at + hq : at + 2 * hq]
        )


def close_kernel(own, part, came, n1b, gain, gbc, gbc_came, dn1_out, rows_out):
    tokens = part.shape[0]
    dn1 = (part[...] + came[...]) + n1b[...]
    dn1_out[...] = dn1
    rows_out[0:8, :] = token_sums(dn1 * gain[...] * own[...].astype(F32))
    rows_out[8:16, :] = gbc[tokens:] + gbc_came[tokens:]


def end_kernel(
    place, own, factor1, resid, dn1, gain, rows, rows_far, small, gain2, hidden_out, vector_out
):
    half = dn1.shape[1]
    quarter = half // 2
    hid = own[...].astype(F32)
    factor = factor1[:, :1]
    inner_sum = column(rows[0:8] + rows_far[0:8])[:, :1]
    value = dn1[...]
    change = resid[...] + factor * (value * gain[...]) - hid * (
        factor * factor * factor * inner_sum / (2 * half)
    )
    hidden_out[...] = jnp.where(place[0] == 0, change[:, :quarter], change[:, quarter:])
    shared = jnp.where(place[2] == 0, rows[8:16], rows_far[8:16])
    nbc = rows.shape[1]
    heads = 3 * LANES
    vector_out[...] = jnp.zeros_like(vector_out)
    vector_out[0 : TAPS + 1] = small[0 : TAPS + 1]
    vector_out[5:6, 0:heads] = small[8 + TAPS : 9 + TAPS, 0:heads]
    vector_out[5:6, heads : heads + nbc] = shared[TAPS : TAPS + 1]
    vector_out[6:7, 0:half] = jnp.sum(value * hid * factor, axis=0, keepdims=True)
    vector_out[7:8, 0:half] = gain2[0:1]
    vector_out[6:7, half : half + nbc] = shared[0:1]
    vector_out[7:8, half : half + nbc] = shared[1:2]
    vector_out[8:9, 0:nbc] = shared[2:3]
    vector_out[8:9, nbc : 2 * nbc] = shared[3:4]


def stage_kernel(keep, came, send_out, keep_out):
    rows = keep_out.shape[0]
    total = keep[...] + came[...].astype(F32)
    send_out[...] = total[rows:].astype(BF16)
    keep_out[...] = total[:rows]


def last_kernel(keep, came, *outs):
    total = keep[...] + came[...].astype(F32)
    at = 0
    for out in outs:
        out[...] = total[:, at : at + out.shape[1]]
        at += out.shape[1]


def last_tall_kernel(keep, came, *outs):
    total = keep[...] + came[...].astype(F32)
    width = outs[0].shape[1]
    outs[0][...] = jnp.concatenate([total[:, :width], total[:, width : 2 * width]], axis=0)
    tall = jnp.concatenate([total[:, 2 * width : 3 * width], total[:, 3 * width :]], axis=0)
    size = outs[1].shape[0]
    outs[1][...] = tall[:size]
    outs[2][...] = tall[size:]


def halving_order(steps):
    order = [0]
    for step in reversed(steps):
        order = order + [o | step for o in order]
    return order


def halve(run, steps, at, send, keep, last, outs):
    while True:
        came = swap(send, "dp", steps[at])
        yield None
        at += 1
        if at == len(steps):
            break
        rows, cols = keep.shape
        send, keep = run(
            stage_kernel, [((rows // 2, cols), BF16), ((rows // 2, cols), F32)], keep, came
        )
    yield run(last, outs, keep, came)


def finish(steps):
    result = None
    while result is None:
        result = next(steps)
    return result


def shards(
    hidden,
    segment_ids,
    norm1_gain,
    w_gate,
    w_xin,
    w_dt,
    w_bc,
    w_query,
    w_kv,
    convx_weight,
    convx_bias,
    convbc_weight,
    convbc_bias,
    dt_bias,
    a_log,
    d_skip,
    w_mixout,
    w_attnout,
    norm2_gain,
    w_gateup,
    w_down,
    cotangent,
):
    row = lax.axis_index("row")
    col = lax.axis_index("col")
    me = lax.axis_index("dp")
    count = lax.axis_size("dp")
    spot = me & 3
    place = jnp.stack([col, spot, row]).astype(jnp.int32)
    tokens, quarter = hidden.shape
    half = 2 * quarter
    full_width = 4 * quarter
    piece = half // 4
    ch = w_xin.shape[1]
    nq = w_query.shape[1]
    nkv = w_kv.shape[2]
    nbc = w_bc.shape[1]
    heads = w_dt.shape[1]
    ff = w_down.shape[0]
    cq = convx_bias.shape[0]
    hq = dt_bias.shape[0]

    run = Chain()
    cols = ch + nbc + LANES + ch + nq + nkv
    inner = ch + nq

    near = [1 << b for b in range(count.bit_length() - 1)]
    turned = [near[1], near[0]] + near[2:]
    size = half // count
    within = jnp.asarray(np.tile(np.arange(size), count), jnp.int32)
    both_within = jnp.concatenate([within, within + size])

    def block_order(steps):
        return jnp.asarray(np.repeat(np.array(halving_order(steps)), size), jnp.int32) ^ me

    near_block = block_order(near)
    turned_both = jnp.concatenate([block_order(turned)] * 2)
    order_near = (near_block * size + within)[None]
    order_down = (turned_both * (ff // count) + both_within)[None]
    m_rows = ch // count
    a_rows = nq // count
    order_mix = jnp.where(
        both_within < m_rows,
        turned_both * m_rows + both_within,
        ch + turned_both * a_rows + both_within - m_rows,
    )[None]

    def padded(value):
        return jnp.pad(value, (0, LANES - hq))

    small = jnp.concatenate(
        [convx_weight.T.reshape(-1), convx_bias, norm2_gain, padded(dt_bias), padded(a_log), padded(d_skip)]
    )
    small_rows = 16 * pl.cdiv(small.shape[0] // LANES + 8, 16)
    small = jnp.pad(small, (0, small_rows * LANES - small.shape[0])).reshape(small_rows, LANES)
    gu_mine = lax.dynamic_slice_in_dim(w_gateup, spot * piece, piece, 0).reshape(piece, 2 * ff)
    hid_came = swap(hidden, "col")
    mine = run(
        pieces_kernel,
        [((inner + 3 * ff + 4 * tokens + small_rows, piece), BF16)],
        place, w_mixout, w_attnout, w_down, gu_mine, cotangent, hidden, small,
        smem=(0,),
    )[0]
    got = swap(mine, "row")
    wk = w_kv.reshape(half, nkv)
    wd = jnp.pad(w_dt, ((0, 0), (0, LANES - heads)))
    gain_one = norm1_gain.astype(F32)[None]
    own, part, part_low = run(
        project_kernel,
        [((tokens, half), BF16), ((tokens, cols), F32), ((tokens, cols), BF16)],
        place, hidden, hid_came, gain_one, w_xin, w_bc, wd, w_gate, w_query, wk,
        smem=(0,),
    )
    part_came = swap(part_low, "row")
    t_first, g_first, in_pair, x_par, head_par, gain_two = run(
        lambda *refs: split_kernel(heads, *refs),
        [
            ((inner + ff, piece), BF16),
            ((piece, 2 * ff), BF16),
            ((3 * tokens, quarter), BF16),
            ((8, ch), F32),
            ((8, LANES), F32),
            ((1, full_width), F32),
        ],
        place, got, cotangent, small,
        smem=(0,),
    )
    t_second = swap(t_first, "dp", 1)
    g_second = swap(g_first, "dp", 2)
    t_third = swap(t_first, "dp", 2)
    g_third = swap(g_first, "dp", 1)
    in_came = swap(in_pair, "col")
    gu = w_gateup.reshape(half, 2 * ff)
    far, dy_own, dy_far, factor1, n1, left1 = run(
        norm_kernel,
        [
            ((tokens, half), BF16),
            ((tokens, half), BF16),
            ((tokens, half), BF16),
            ((tokens, LANES), F32),
            ((tokens, half), BF16),
            ((tokens, half), BF16),
        ],
        place, in_pair, in_came, own, gain_one, order_near,
        smem=(0,), scratch=[((tokens, half), BF16)], after=(t_second, g_second),
    )
    t_fourth = swap(t_second, "dp", 2)
    g_fourth = swap(g_second, "dp", 1)
    tall_fetch = (t_first, t_second, t_third, t_fourth)

    bc_par = jnp.concatenate(
        [convbc_weight.T, convbc_bias[None], jnp.zeros((3, nbc), BF16)], 0
    ).astype(F32)
    seg_row = segment_ids.astype(F32)
    seg_col = jnp.broadcast_to(segment_ids[0].astype(F32)[:, None], (tokens, LANES))

    mixed, raw, pre, ys = run(
        lambda *refs: mix_kernel(ch, nq, *refs),
        [
            ((tokens, inner), BF16),
            ((tokens, cols), F32),
            ((tokens, ch + nbc), F32),
            ((tokens, ch), F32),
        ],
        seg_row, seg_col, factor1, part, part_came, x_par, bc_par, head_par,
        after=(g_third,),
    )
    mix_part = run(
        out_kernel,
        [((tokens, full_width), F32)],
        mixed, w_mixout, w_attnout, *tall_fetch,
        after=(g_fourth,),
    )[0]
    mix_came = swap(mix_part, "col")
    grad_act = run(
        lambda *refs: act_grad_kernel(inner, *refs),
        [((tokens, ff), F32)],
        dy_own, dy_far, w_down, *tall_fetch,
    )[0]
    h2, n2, act, ggu, n2_part, down_keep, down_send = run(
        feed_kernel,
        [
            ((tokens, full_width), F32),
            ((tokens, half), BF16),
            ((tokens, ff), BF16),
            ((tokens, 2 * ff), BF16),
            ((tokens, full_width), F32),
            ((tokens, quarter), F32),
            ((tokens, quarter), F32),
        ],
        place, own, far, mix_part, mix_came, gain_two,
        gu, g_first, g_third, g_second, g_fourth, grad_act, w_down,
        smem=(0,),
    )
    n2_came = swap(n2_part, "col")
    down_came = swap(down_send, "col")
    rows = half // 2

    g_send, d_send, g_left, d_left = run(
        feed_grad_kernel,
        [
            ((rows, 2 * ff), BF16),
            ((rows, 2 * half), BF16),
            ((tokens, rows), BF16),
            ((tokens, half), BF16),
        ],
        n2, act, ggu, dy_own, order_near, order_down,
    )
    g_came = swap(g_send, "dp", near[0])
    d_came = swap(d_send, "dp", turned[0])
    dym, resid, low, gain2_sum, output, m_send, m_left, g_two, two_send = run(
        lambda *refs: turn_kernel(ch, nq, *refs),
        [
            ((tokens, inner), F32),
            ((tokens, half), F32),
            ((tokens, half), BF16),
            ((8, half), F32),
            ((tokens, quarter), BF16),
            ((rows, 2 * half), BF16),
            ((tokens, half), BF16),
            ((tokens, ch + nq + nkv), BF16),
            ((rows, ch + nq + nkv), BF16),
        ],
        place, dy_own, dy_far, h2, n2_part, n2_came, gain_two,
        w_mixout, w_attnout, *tall_fetch, down_keep, down_came,
        mixed, order_mix, seg_row, seg_col, raw, pre, ys, x_par, left1,
        smem=(0,),
    )
    two_came = swap(two_send, "dp", near[0])
    m_came = swap(m_send, "dp", turned[0])
    gx, gdt, gbc, small_sum = run(
        lambda *refs: unmix_one_kernel(ch, nq, *refs),
        [
            ((tokens, ch), BF16),
            ((tokens, LANES), BF16),
            ((tokens + 8, nbc), F32),
            ((16, ch), F32),
        ],
        seg_row, seg_col, raw, pre, ys, dym, x_par, bc_par, head_par,
        scratch=[((tokens, ch), F32), ((tokens, ch), F32), ((tokens, tokens), F32)],
    )
    gbc_came = swap(gbc, "col")

    def quarters(width):
        return [((rows // 2, width), BF16), ((rows // 2, width), F32)]

    g_send, g_keep = run(wide_kernel, quarters(2 * ff), g_left, ggu, g_came)
    s_gu = halve(run, near, 1, g_send, g_keep, last_kernel, [((size, 2 * ff), F32)])
    next(s_gu)
    n1_part, n1_bc, gbc_both, one_send = run(
        back_kernel,
        [
            ((tokens, half), F32),
            ((tokens, half), F32),
            ((tokens, nbc), BF16),
            ((rows, ch + nbc + LANES), BF16),
        ],
        g_two, gx, gdt, gbc, gbc_came, w_xin, w_bc, wd, w_gate, w_query, wk, left1,
    )
    one_came = swap(one_send, "dp", near[0])
    n1_came = swap(n1_part, "col")
    def one_outs(keep):
        width = ch + nbc + LANES
        return [((keep + 32, width), BF16), ((keep, width), F32), ((16, ch), F32)]

    tall_send, tall_keep = run(
        tall_kernel, quarters(4 * half), d_left, dy_own, d_came, m_left, low, m_came
    )
    s_tall = halve(
        run, turned, 1, tall_send, tall_keep, last_tall_kernel,
        [((2 * size, half), F32), ((m_rows, half), F32), ((a_rows, half), F32)],
    )
    next(s_tall)
    two_send, two_keep = run(wide_kernel, quarters(ch + nq + nkv), left1, g_two, two_came)
    s_two = halve(
        run, near, 1, two_send, two_keep, last_kernel,
        [((size, ch), F32), ((size, nq), F32), ((size, nkv), F32)],
    )
    next(s_two)
    dn1, sum_rows = run(
        close_kernel,
        [((tokens, half), F32), ((16, tokens), F32)],
        own, n1_part, n1_came, n1_bc, gain_one, gbc, gbc_came,
    )
    rows_far = swap(sum_rows, "row")
    next(s_gu)
    grad_hidden, vector = run(
        end_kernel,
        [((tokens, quarter), F32), ((16, ch), F32)],
        place, own, factor1, resid, dn1, gain_one, sum_rows, rows_far, small_sum, gain2_sum,
        smem=(0,),
    )
    vector_came = swap(vector, "dp", near[0])
    next(s_two)
    r_gu = finish(s_gu)
    one_send, one_keep, vector = run(
        one_kernel, one_outs(rows // 2),
        left1, gx, gbc_both, gdt, one_came, vector, vector_came,
    )
    next(s_tall)
    r_two = finish(s_two)
    for step in near[1:-1]:
        one_came = swap(one_send, "dp", step)
        one_send, one_keep, vector = run(
            one_stage_kernel, one_outs(one_keep.shape[0] // 2), one_keep, one_came, vector
        )
    one_came = swap(one_send, "dp", near[-1])
    r_tall = finish(s_tall)
    (
        r_xin, r_bc, r_dt, o_norm1, o_norm2, o_cxw, o_cxb, o_cbw, o_cbb, o_dtb, o_alog, o_dsk
    ) = run(
        lambda *refs: one_last_kernel(heads, *refs),
        [
            ((size, ch), F32),
            ((size, nbc), F32),
            ((size, heads), F32),
            ((1, half), F32),
            ((1, half), F32),
            ((TAPS, cq), F32),
            ((1, cq), F32),
            ((TAPS, nbc), F32),
            ((1, nbc), F32),
            ((1, hq), F32),
            ((1, hq), F32),
            ((1, hq), F32),
        ],
        place, one_keep, one_came, vector,
        smem=(0,),
    )
    r_gate, r_query, r_kv = r_two
    r_down, r_mixout, r_attnout = r_tall
    return (
        output,
        grad_hidden,
        o_norm1[0],
        r_gate,
        r_xin,
        r_dt,
        r_bc,
        r_query,
        r_kv.reshape(size, 1, nkv),
        o_cxw.T,
        o_cxb[0],
        o_cbw.T,
        o_cbb[0],
        o_dtb[0],
        o_alog[0],
        o_dsk[0],
        r_mixout,
        r_attnout,
        o_norm2[0],
        r_gu[0].reshape(size, 2, ff),
        r_down,
    )


def solution(mesh):
    placed = (
        P("dp", ("row", "col")),
        P("dp", None),
        P("row"),
        P("row", "col"),
        P("row", "col"),
        P("row", "col"),
        P("row", None),
        P("row", "col"),
        P("row", "col", None),
        P(("col", "row"), None),
        P(("col", "row")),
        P(),
        P(),
        P(("col", "row")),
        P(("col", "row")),
        P(("col", "row")),
        P("col", "row"),
        P("col", "row"),
        P("row"),
        P("row", None, "col"),
        P("col", "row"),
        P("dp", ("row", "col")),
    )
    return jax.shard_map(
        shards,
        mesh=mesh,
        in_specs=placed,
        out_specs=(
            P("dp", ("row", "col")),
            P("dp", ("row", "col")),
            P("row"),
            P(("row", "dp"), "col"),
            P(("row", "dp"), "col"),
            P(("row", "dp"), "col"),
            P(("row", "dp"), None),
            P(("row", "dp"), "col"),
            P(("row", "dp"), "col", None),
            P(("col", "row"), None),
            P(("col", "row")),
            P(),
            P(),
            P(("col", "row")),
            P(("col", "row")),
            P(("col", "row")),
            P(("col", "dp"), "row"),
            P(("col", "dp"), "row"),
            P("row"),
            P(("row", "dp"), None, "col"),
            P(("col", "dp"), "row"),
        ),
        check_vma=False,
    )
```

```python
import jax
import jax.numpy as jnp
import numpy as np
from jax import lax
from jax.experimental import pallas as pl
from jax.experimental.pallas import tpu as pltpu
from jax.sharding import PartitionSpec as P

NORM_EPS = 1e-05
F32 = jnp.float32
BF16 = jnp.bfloat16
HEAD = 64
LANES = 128
TAPS = 4
FAR = -1e30


def swap(values, axis, step=1):
    count = lax.axis_size(axis)
    return lax.ppermute(values, axis, [(i, i ^ step) for i in range(count)])


def dot(left, right):
    return jnp.dot(left, right, preferred_element_type=F32)


def dot_bt(left, right):
    return lax.dot_general(left, right, (((1,), (1,)), ((), ())), preferred_element_type=F32)


def dot_at(left, right):
    return lax.dot_general(left, right, (((0,), (0,)), ((), ())), preferred_element_type=F32)


def fine(left, right, dims=((1,), (0,))):
    return lax.dot_general(
        left, right, (dims, ((), ())), precision=lax.Precision.HIGHEST, preferred_element_type=F32
    )


class Chain:
    def __init__(self):
        self.token = jnp.zeros((8, LANES), F32)

    def __call__(self, kernel, outs, *args, scratch=(), smem=(), after=()):
        plain = pltpu.VMEM
        specs = [
            pl.BlockSpec(memory_space=pltpu.SMEM if i in smem else plain)
            for i in range(len(args))
        ]
        extra = (self.token,) + tuple(after)
        count = len(args)
        held = count + len(extra)

        def body(*refs):
            refs[held][...] = jnp.zeros((8, LANES), F32)
            kernel(*refs[:count], *refs[held + 1 :])

        results = pl.pallas_call(
            body,
            out_shape=[jax.ShapeDtypeStruct((8, LANES), F32)]
            + [jax.ShapeDtypeStruct(s, d) for s, d in outs],
            in_specs=specs + [pl.BlockSpec(memory_space=pl.ANY)] * len(extra),
            out_specs=[pl.BlockSpec(memory_space=pltpu.VMEM)]
            + [pl.BlockSpec(memory_space=plain)] * len(outs),
            scratch_shapes=[pltpu.VMEM(s, d) if d is not None else s for s, d in scratch],
            compiler_params=pltpu.CompilerParams(vmem_limit_bytes=64 << 20),
            cost_estimate=pl.CostEstimate(flops=0, bytes_accessed=0, transcendentals=0),
        )(*args, *extra)
        self.token = results[0]
        return results[1:]


def two_parts(value):
    high = value.astype(BF16)
    return high, (value - high.astype(F32)).astype(BF16)


def dot_three(product, left, right):
    return product(left[0], right[0]) + (product(left[1], right[0]) + product(left[0], right[1]))


def iota(shape, dim):
    return lax.broadcasted_iota(jnp.int32, shape, dim)


def column(row_vector):
    ones = jnp.full((row_vector.shape[0], LANES), 1.0 / row_vector.shape[0], F32)
    return fine(row_vector, ones, ((0,), (0,)))


def token_sums(values):
    return fine(jnp.ones((8, values.shape[1]), F32), values, ((1,), (1,)))


def pieces_kernel(place, wm, wa, wd, gu, cot, hid, small, out):
    piece = out.shape[1]
    at = pl.multiple_of(place[1] * piece, piece)
    row = 0
    for w in (wm, wa, wd):
        out[row : row + w.shape[0]] = w[:, pl.ds(at, piece)]
        row += w.shape[0]
    for value in (gu, cot, hid):
        for j in range(value.shape[1] // piece):
            out[row : row + value.shape[0]] = value[:, j * piece : (j + 1) * piece]
            row += value.shape[0]
    out[row:] = small[...]


def join_small(place, heads, own, far, x_par_out, head_out, gain_out):
    first = place[2] == 0
    a = jnp.where(first, own, far)
    b = jnp.where(first, far, own)
    width = x_par_out.shape[1] // 2
    count = width // LANES
    x_par_out[...] = jnp.zeros_like(x_par_out)
    for k in range(TAPS + 1):
        for i in range(count):
            at = k * count + i
            x_par_out[k : k + 1, i * LANES : (i + 1) * LANES] = a[at : at + 1]
            x_par_out[k : k + 1, width + i * LANES : width + (i + 1) * LANES] = b[at : at + 1]
    row = (TAPS + 1) * count
    pieces = gain_out.shape[1] // (2 * LANES)
    for j in range(pieces):
        gain_out[:, j * LANES : (j + 1) * LANES] = own[row + j : row + j + 1]
        block = jnp.zeros((1, LANES), F32)
        for i in range(pieces):
            block = block + jnp.where((place[1] ^ j) == i, far[row + i : row + i + 1], 0.0)
        at = (pieces + j) * LANES
        gain_out[:, at : at + LANES] = block
    row += pieces
    joined = a[row : row + 8] + pltpu.roll(b[row : row + 8], heads // 2, 1)
    head_out[...] = joined
    pick = jnp.where(
        iota((LANES, 2 * width), 0) == iota((LANES, 2 * width), 1) // HEAD, 1.0, 0.0
    )
    x_par_out[TAPS + 1 : TAPS + 2] = fine(joined, pick)[2:3]


def split_kernel(
    heads, place, got, cot, small, t_out, g_out, pair_out, x_par_out, head_out, gain_out
):
    piece = got.shape[1]
    tokens = cot.shape[0]
    row = t_out.shape[0]
    t_out[...] = got[0:row]
    for j in range(g_out.shape[1] // piece):
        g_out[:, j * piece : (j + 1) * piece] = got[row : row + piece]
        row += piece
    pair_out[0:tokens] = cot[...]
    for i in (1, 2):
        for j in range(cot.shape[1] // piece):
            pair_out[i * tokens : (i + 1) * tokens, j * piece : (j + 1) * piece] = got[
                row : row + tokens
            ]
            row += tokens
    own = small[...].astype(F32)
    far = got[row:].astype(F32)
    join_small(place, heads, own, far, x_par_out, head_out, gain_out)


def far_order(place, value, out):
    piece = value.shape[1] // 4
    for j in range(4):
        at = pl.multiple_of((place[1] ^ j) * piece, piece)
        out[:, j * piece : (j + 1) * piece] = value[:, pl.ds(at, piece)]


def side_by_side(place, a, b, out):
    width = a.shape[1]
    first = place[0] == 0
    out[:, :width] = jnp.where(first, a, b)
    out[:, width:] = jnp.where(first, b, a)


def project_kernel(place, mine, came, gain, wx, wb, wd, wg, wq, wk, own_out, p_out, low_out):
    side_by_side(place, mine[...], came[...], own_out)
    high, low = two_parts(own_out[...].astype(F32) * gain[...])
    at = 0
    for w in (wx, wb, wd, wg, wq, wk):
        size = w.shape[1]
        part = dot(high, w[...]) + dot(low, w[...])
        p_out[:, at : at + size] = part
        low_out[:, at : at + size] = part.astype(BF16)
        at += size


def norm_kernel(
    place, pair, came, own, gain, order,
    far_out, dy_own, dy_far, factor_out, n1_out, left_out, far_tmp,
):
    tokens = own.shape[0]
    side_by_side(place, pair[0:tokens], came[0:tokens], dy_own)
    side_by_side(place, pair[tokens : 2 * tokens], came[tokens : 2 * tokens], far_tmp)
    far_order(place, far_tmp, dy_far)
    side_by_side(place, pair[2 * tokens :], came[2 * tokens :], far_tmp)
    far_order(place, far_tmp, far_out)
    hid = own[...].astype(F32)
    far = far_out[...].astype(F32)
    mean = jnp.sum(hid * hid + far * far, axis=1, keepdims=True) / (2 * hid.shape[1])
    factor = lax.rsqrt(mean + NORM_EPS)
    factor_out[...] = jnp.broadcast_to(factor, factor_out.shape)
    n1_out[...] = (hid * factor * gain[...]).astype(BF16)
    left_out[...] = permuted(n1_out[...], order[...])


def masks(seg_row, seg_col, turned):
    tokens = seg_row.shape[1]
    i = iota((tokens, tokens), 1 if turned else 0)
    j = iota((tokens, tokens), 0 if turned else 1)
    same = seg_col[:, :1] == seg_row[...]
    return jnp.where((i >= j) & same, 0.0, FAR)


def valids(seg_col):
    seg = seg_col[...]
    t = iota(seg.shape, 0)
    return [
        jnp.where((t >= k) & (pltpu.roll(seg, k, 0) == seg), 1.0, 0.0) for k in range(1, TAPS)
    ]


def conv(block, taps, bias, valid):
    total = block * taps[TAPS - 1 : TAPS] + bias
    for k in range(1, TAPS):
        total = total + (pltpu.roll(block, k, 0) * valid[k - 1]) * taps[TAPS - 1 - k : TAPS - k]
    return total


def conv_turn(grad, block, taps, valid):
    tokens = grad.shape[0]
    back = grad * taps[TAPS - 1 : TAPS]
    rows = [None] * TAPS
    rows[TAPS - 1] = jnp.sum(grad * block, axis=0, keepdims=True)
    for k in range(1, TAPS):
        kept = grad * valid[k - 1]
        back = back + pltpu.roll(kept, tokens - k, 0) * taps[TAPS - 1 - k : TAPS - k]
        rows[TAPS - 1 - k] = jnp.sum(kept * pltpu.roll(block, k, 0), axis=0, keepdims=True)
    rows.append(jnp.sum(grad, axis=0, keepdims=True))
    rows.append(jnp.zeros((8 - len(rows), grad.shape[1]), F32))
    return back, jnp.concatenate(rows, 0)


def silu_turn(value):
    sig = jax.nn.sigmoid(value)
    return value * sig, sig * (1.0 + value * (1.0 - sig))


def steps(dt_raw, head_par):
    shifted = dt_raw + head_par[0:1]
    return jnp.maximum(shifted, 0.0) + jnp.log1p(jnp.exp(-jnp.abs(shifted)))


def mix_kernel(
    ch, nq, seg_row, seg_col, factor, own, came, x_par, bc_par, head_par,
    mixed_out, sums_out, pre_out, y_out,
):
    tokens = own.shape[0]
    nbc = bc_par.shape[1]
    state = nbc // 2
    sums_out[...] = factor[:, :1] * (own[...] + came[...].astype(F32))
    lane = iota((tokens, LANES), 1)
    low = lane < HEAD
    mask = masks(seg_row, seg_col, False)
    valid = valids(seg_col)
    for b in range(nbc // LANES):
        at = ch + b * LANES
        part = slice(b * LANES, (b + 1) * LANES)
        pre_out[:, at : at + LANES] = conv(
            sums_out[:, at : at + LANES], bc_par[0:TAPS, part], bc_par[TAPS : TAPS + 1, part], valid
        )
    bcc = pre_out[:, ch : ch + nbc]
    bcc = bcc * jax.nn.sigmoid(bcc)
    inner = fine(bcc[:, state:], bcc[:, :state], ((1,), (1,)))
    dt = steps(sums_out[:, ch + nbc : ch + nbc + LANES], head_par)
    tri = jnp.where(iota((tokens, tokens), 0) >= iota((tokens, tokens), 1), 1.0, 0.0)
    cum = fine(tri, dt * -jnp.exp(head_par[1:2]))
    cum_row = cum.T
    base = ch + nbc + LANES
    for p in range(ch // LANES):
        part = slice(p * LANES, (p + 1) * LANES)
        pre = conv(sums_out[:, part], x_par[0:TAPS, part], x_par[TAPS : TAPS + 1, part], valid)
        pre_out[:, part] = pre
        xc = pre * jax.nn.sigmoid(pre)
        h = 2 * p
        xdt = (xc * jnp.where(low, dt[:, h : h + 1], dt[:, h + 1 : h + 2])).astype(BF16)
        ys = []
        for e in (h, h + 1):
            decay = jnp.exp((cum[:, e : e + 1] - cum_row[e : e + 1]) + mask)
            ys.append(dot((inner * decay).astype(BF16), xdt))
        y = jnp.where(low, ys[0], ys[1])
        y_out[:, part] = y
        y = y + x_par[TAPS + 1 : TAPS + 2, part] * xc
        z = sums_out[:, base + p * LANES : base + (p + 1) * LANES]
        mixed_out[:, part] = (y * (z * jax.nn.sigmoid(z))).astype(BF16)
    at = base + ch
    kv = sums_out[:, at + nq : at + nq + LANES]
    kv_turn = pltpu.roll(kv, HEAD, 1)
    keys = two_parts(jnp.where(low, kv, kv_turn))
    vals = two_parts(jnp.where(low, kv_turn, kv))
    for p in range(nq // LANES):
        query = sums_out[:, at + p * LANES : at + (p + 1) * LANES] * (HEAD ** -0.5)
        outs = []
        for side in (low, ~low):
            score = dot_three(dot_bt, two_parts(jnp.where(side, query, 0.0)), keys) + mask
            score = jnp.exp(score - jnp.max(score, axis=1, keepdims=True))
            total = jnp.sum(score, axis=1, keepdims=True)
            outs.append(dot_three(dot, two_parts(score), vals) / total)
        mixed_out[:, ch + p * LANES : ch + (p + 1) * LANES] = jnp.where(
            low, outs[0], outs[1]
        ).astype(BF16)


def unmix_two_kernel(ch, nq, seg_row, seg_col, sums, pre, ys, dym, x_par, gtwo_out):
    tokens = sums.shape[0]
    base = sums.shape[1] - (ch + nq + LANES)
    low = iota((tokens, LANES), 1) < HEAD
    mask = masks(seg_row, seg_col, True)
    for p in range(ch // LANES):
        part = slice(p * LANES, (p + 1) * LANES)
        value = pre[:, part]
        xc = value * jax.nn.sigmoid(value)
        _, gate_turn = silu_turn(sums[:, base + p * LANES : base + (p + 1) * LANES])
        y = ys[:, part] + x_par[TAPS + 1 : TAPS + 2, part] * xc
        gtwo_out[:, part] = (dym[:, part] * y * gate_turn).astype(BF16)
    at = base + ch
    kv = sums[:, at + nq : at + nq + LANES]
    kv_turn = pltpu.roll(kv, HEAD, 1)
    keys = jnp.where(low, kv, kv_turn).astype(BF16)
    vals = jnp.where(low, kv_turn, kv).astype(BF16)
    dk = jnp.zeros((tokens, LANES), F32)
    dv = jnp.zeros((tokens, LANES), F32)
    for p in range(nq // LANES):
        query = sums[:, at + p * LANES : at + (p + 1) * LANES] * (HEAD ** -0.5)
        grad = dym[:, ch + p * LANES : ch + (p + 1) * LANES]
        dqs = []
        for side in (low, ~low):
            q_low = jnp.where(side, query, 0.0).astype(BF16)
            g_low = jnp.where(side, grad, 0.0).astype(BF16)
            score = dot_bt(keys, q_low) + mask
            score = jnp.exp(score - jnp.max(score, axis=0, keepdims=True))
            prob = score * (1.0 / jnp.sum(score, axis=0, keepdims=True))
            dprob = dot_bt(vals, g_low)
            dv = dv + dot(prob.astype(BF16), g_low)
            inner_sum = jnp.sum(prob * dprob, axis=0, keepdims=True)
            dscore = (prob * (dprob - inner_sum)).astype(BF16)
            dk = dk + dot(dscore, q_low)
            dqs.append(dot_at(dscore, keys))
        gtwo_out[:, ch + p * LANES : ch + (p + 1) * LANES] = (
            jnp.where(low, dqs[0], dqs[1]) * (HEAD ** -0.5)
        ).astype(BF16)
    dk = dk + pltpu.roll(dk, HEAD, 1)
    dv = dv + pltpu.roll(dv, HEAD, 1)
    gtwo_out[:, ch + nq : ch + nq + LANES] = jnp.where(low, dk, dv).astype(BF16)

def unmix_one_kernel(
    ch, nq, seg_row, seg_col, sums, pre, ys, dym, x_par, bc_par, head_par,
    gx_out, gdt_out, gbc_out, small_out, prod_a, prod_b, turned,
):
    tokens = sums.shape[0]
    nbc = bc_par.shape[1]
    state = nbc // 2
    lane = iota((tokens, LANES), 1)
    low = lane < HEAD
    mask = masks(seg_row, seg_col, True)
    valid = valids(seg_col)
    bc_pre = pre[:, ch : ch + nbc]
    bcc, bcc_turn = silu_turn(bc_pre)
    b_in = bcc[:, :state]
    c_in = bcc[:, state:]
    inner = fine(b_in, c_in, ((1,), (1,)))
    dt_raw = sums[:, ch + nbc : ch + nbc + LANES]
    dt = steps(dt_raw, head_par)
    rate = jnp.exp(head_par[1:2])
    tri = jnp.where(iota((tokens, tokens), 0) >= iota((tokens, tokens), 1), 1.0, 0.0)
    cum = fine(tri, dt * -rate)
    cum_row = cum.T
    base = ch + nbc + LANES
    small_out[...] = jnp.zeros_like(small_out)
    turned[...] = jnp.zeros_like(turned)
    for p in range(ch // LANES):
        part = slice(p * LANES, (p + 1) * LANES)
        xc, xc_turn = silu_turn(pre[:, part])
        skip = x_par[TAPS + 1 : TAPS + 2, part]
        z = sums[:, base + p * LANES : base + (p + 1) * LANES]
        gate = z * jax.nn.sigmoid(z)
        dy_in = dym[:, part]
        y = ys[:, part]
        dy = dy_in * gate
        h = 2 * p
        dt_pair = jnp.where(low, dt[:, h : h + 1], dt[:, h + 1 : h + 2])
        xdt = xc * dt_pair
        dy_low = dy.astype(BF16)
        x_low = xdt.astype(BF16)
        sides = []
        for e, side in ((h, low), (h + 1, ~low)):
            decay = jnp.exp((cum_row[e : e + 1] - cum[:, e : e + 1]) + mask)
            turned[...] += dot_bt(jnp.where(side, xdt, 0.0).astype(BF16), dy_low) * decay
            sides.append(dot((inner * decay).astype(BF16), dy_low))
        dxdt = jnp.where(low, sides[0], sides[1])
        prod_a[:, part] = dy_low.astype(F32) * y - x_low.astype(F32) * dxdt
        prod_b[:, part] = dxdt * xc
        small_out[8 + TAPS + 1 : 8 + TAPS + 2, part] = jnp.sum(dy * xc, axis=0, keepdims=True)
        dpre = (skip * dy + dxdt * dt_pair) * xc_turn
        back, rows = conv_turn(dpre, sums[:, part], x_par[0:TAPS, part], valid)
        gx_out[:, part] = back.astype(BF16)
        small_out[0:8, part] = rows
    pick = jnp.where(iota((ch, LANES), 0) // HEAD == iota((ch, LANES), 1), 1.0, 0.0)
    dcum = fine(prod_a[...], pick)
    ddt = fine(prod_b[...], pick)
    after = fine(tri, dcum, ((0,), (0,)))
    ddt = ddt - rate * after
    ddt = ddt * jax.nn.sigmoid(dt_raw + head_par[0:1])
    gdt_out[...] = ddt.astype(BF16)
    small_out[8 + TAPS : 8 + TAPS + 1, 0:LANES] = jnp.sum(ddt, axis=0, keepdims=True)
    small_out[8 + TAPS : 8 + TAPS + 1, LANES : 2 * LANES] = jnp.sum(
        after * (-dt * rate), axis=0, keepdims=True
    )
    skip_sum = jnp.broadcast_to(small_out[8 + TAPS + 1 : 8 + TAPS + 2, :], (8, ch))
    small_out[8 + TAPS : 8 + TAPS + 1, 2 * LANES : 3 * LANES] = fine(skip_sum, pick)[0:1]
    dinner = turned[...]
    d_b = fine(dinner, c_in) * bcc_turn[:, :state]
    d_c = fine(dinner, b_in, ((0,), (0,))) * bcc_turn[:, state:]
    for b, grad in enumerate((d_b, d_c)):
        at = ch + b * LANES
        part = slice(b * LANES, (b + 1) * LANES)
        back, rows = conv_turn(grad, sums[:, at : at + LANES], bc_par[0:TAPS, part], valid)
        gbc_out[0:tokens, part] = back
        gbc_out[tokens : tokens + 8, part] = rows


def tall_far(fetch, start, size):
    return jnp.concatenate(
        [r[start : start + size] for r in fetch], axis=1
    )


def out_kernel(mixed, wm, wa, t0, t1, t2, t3, part_out):
    fetch = (t0, t1, t2, t3)
    half = wm.shape[1]
    ch = wm.shape[0]
    value = mixed[...]
    part_out[:, :half] = dot(value[:, :ch], wm[...]) + dot(value[:, ch:], wa[...])
    part_out[:, half:] = dot(value, tall_far(fetch, 0, value.shape[1]))


def norm_factor(value):
    return lax.rsqrt(jnp.mean(value * value, axis=1, keepdims=True) + NORM_EPS)


def act_grad_kernel(inner, dy_own, dy_far, wd, t0, t1, t2, t3, ga_out):
    fetch = (t0, t1, t2, t3)
    ff = wd.shape[0]
    ga_out[...] = dot_bt(dy_own[...], wd[...]) + dot_bt(
        dy_far[...], tall_far(fetch, inner, ff)
    )


def feed_kernel(
    place, own, far, part, came, gain, gu, gu0, gu1, gu2, gu3, grad_act, wd,
    h2_out, n2_out, act_out, ggu_out, n2p_out, keep_out, send_out,
):
    half = own.shape[1]
    quarter = half // 2
    h2_out[:, :half] = own[...].astype(F32) + (part[:, :half] + came[:, :half])
    h2_out[:, half:] = far[...].astype(F32) + (part[:, half:] + came[:, half:])
    h2 = h2_out[...]
    n2 = (h2 * norm_factor(h2) * gain[...]).astype(BF16)
    n2_out[...] = n2[:, :half]
    gu_far = jnp.concatenate([gu0[...], gu1[...], gu2[...], gu3[...]], axis=0)
    ff = wd.shape[0]
    gate_up = dot(n2[:, :half], gu[...]) + dot(n2[:, half:], gu_far)
    gate = gate_up[:, :ff]
    up = gate_up[:, ff:]
    silu, silu_grad = silu_turn(gate)
    act = (silu * up).astype(BF16)
    act_out[...] = act
    ga = grad_act[...]
    ggu_out[:, :ff] = (ga * up * silu_grad).astype(BF16)
    ggu_out[:, ff:] = (ga * silu).astype(BF16)
    ggu = ggu_out[...]
    n2p_out[:, :half] = dot_bt(ggu, gu[...])
    n2p_out[:, half:] = dot_bt(ggu, gu_far)
    down = dot(act, wd[...])
    first = place[0] == 0
    keep_out[...] = jnp.where(first, down[:, :quarter], down[:, quarter:])
    send_out[...] = jnp.where(first, down[:, quarter:], down[:, :quarter])


def permuted(left, source):
    width = left.shape[1]
    hot = jnp.where(iota((width, source.shape[1]), 0) == source, 1.0, 0.0).astype(BF16)
    return dot(left, hot).astype(BF16)


def feed_grad_kernel(
    n2, act, ggu, dy, order, order2, g_send, d_send, g_left, d_left
):
    rows = g_send.shape[0]
    width = dy.shape[1]
    left = permuted(n2[...], order[...])
    g_send[...] = dot_at(left[:, rows:], ggu[...]).astype(BF16)
    g_left[...] = left[:, :rows]
    left = permuted(act[...], order2[...])
    for s in (0, 1):
        cut = 2 * s * rows
        d_send[:, s * width : (s + 1) * width] = dot_at(
            left[:, cut + rows : cut + 2 * rows], dy[...]
        ).astype(BF16)
        d_left[:, s * rows : (s + 1) * rows] = left[:, cut : cut + rows]


def turn_kernel(
    ch, nq, place, dy_own, dy_far, h2, part, came, gain, wm, wa, t0, t1, t2, t3, d_keep, d_came,
    mixed, order_mix, seg_row, seg_col, sums, pre, ys, x_par, left1,
    dym_out, resid_out, low_out, gain_out, output_out, m_send, m_left, gtwo_out, two_send,
):
    fetch = (t0, t1, t2, t3)
    half = dy_own.shape[1]
    quarter = half // 2
    value = h2[...]
    output_out[...] = (
        jnp.where(place[0] == 0, value[:, :quarter], value[:, quarter:half])
        + (d_keep[...] + d_came[...])
    ).astype(BF16)
    factor = norm_factor(value)
    dn2 = part[...] + came[...]
    gained = dn2 * gain[...]
    inner_sum = jnp.sum(gained * value, axis=1, keepdims=True)
    gain_out[...] = jnp.broadcast_to(
        jnp.sum(dn2[:, :half] * value[:, :half] * factor, axis=0, keepdims=True), gain_out.shape
    )
    slope = factor * factor * factor * inner_sum / (2 * half)
    change = factor * gained - value * slope
    dh_own = dy_own[...].astype(F32) + change[:, :half]
    dh_far = dy_far[...].astype(F32) + change[:, half:]
    resid_out[...] = dh_own
    low_own = dh_own.astype(BF16)
    low_out[...] = low_own
    dym = dot_bt(dh_far.astype(BF16), tall_far(fetch, 0, dym_out.shape[1]))
    dym_out[:, :ch] = dym[:, :ch] + dot_bt(low_own, wm[...])
    dym_out[:, ch:] = dym[:, ch:] + dot_bt(low_own, wa[...])
    unmix_two_kernel(ch, nq, seg_row, seg_col, sums, pre, ys, dym_out, x_par, gtwo_out)
    rows = two_send.shape[0]
    two_send[...] = dot_at(left1[:, rows:], gtwo_out[...]).astype(BF16)
    left = permuted(mixed[...], order_mix[...])
    for s in (0, 1):
        cut = 2 * s * rows
        m_send[:, s * half : (s + 1) * half] = dot_at(
            left[:, cut + rows : cut + 2 * rows], low_own
        ).astype(BF16)
        m_left[:, s * rows : (s + 1) * rows] = left[:, cut : cut + rows]


def back_kernel(
    g_two, gx, gdt, gbc, gbc_came, wx, wb, wd, wg, wq, wk, left1,
    n1p_out, n1b_out, both_out, one_send,
):
    tokens = gx.shape[0]
    both = (gbc[0:tokens] + gbc_came[0:tokens]).astype(BF16)
    both_out[...] = both
    rows = one_send.shape[0]
    left = left1[:, rows:]
    at = 0
    for right in (gx[...], both, gdt[...]):
        size = right.shape[1]
        one_send[:, at : at + size] = dot_at(left, right).astype(BF16)
        at += size
    ch = wg.shape[1]
    nq = wq.shape[1]
    total = dot_bt(gx[...], wx[...]) + dot_bt(gdt[...], wd[...])
    total = total + dot_bt(g_two[:, :ch], wg[...]) + dot_bt(g_two[:, ch : ch + nq], wq[...])
    n1p_out[...] = total + dot_bt(g_two[:, ch + nq :], wk[...])
    n1b_out[...] = dot_bt(both, wb[...])


def store_halves(total, at, send_out, keep_out, skip=0):
    rows = keep_out.shape[0]
    size = total.shape[1]
    send_out[skip:, at : at + size] = total[rows:].astype(BF16)
    keep_out[:, at : at + size] = total[:rows]


def wide_kernel(left, right, came, send_out, keep_out):
    total = dot_at(left[:, : came.shape[0]], right[...]) + came[...].astype(F32)
    store_halves(total, 0, send_out, keep_out)


def tall_kernel(d_left, dy, d_came, m_left, low, m_came, send_out, keep_out):
    at = 0
    for left, right, came in ((d_left, dy, d_came), (m_left, low, m_came)):
        rows = came.shape[0]
        width = right.shape[1]
        for s in (0, 1):
            total = dot_at(left[:, s * rows : (s + 1) * rows], right[...])
            total = total + came[:, s * width : (s + 1) * width].astype(F32)
            store_halves(total, at, send_out, keep_out)
            at += width


def pack_vector(value, out):
    rows, width = value.shape
    high = value.astype(BF16)
    low = (value - high.astype(F32)).astype(BF16)
    out[0:rows, 0:width] = high
    out[rows : 2 * rows, 0:width] = low
    return high.astype(F32) + low.astype(F32)


def read_vector(came, shape):
    rows, width = shape
    return came[0:rows, 0:width].astype(F32) + came[rows : 2 * rows, 0:width].astype(F32)


def one_kernel(left1, gx, both, gdt, came, vector, vector_came, send_out, keep_out, vector_out):
    left = left1[:, : came.shape[0]]
    skip = 2 * vector.shape[0]
    at = 0
    for right in (gx[...], both[...], gdt[...]):
        size = right.shape[1]
        total = dot_at(left, right) + came[:, at : at + size].astype(F32)
        store_halves(total, at, send_out, keep_out, skip)
        at += size
    vector_out[...] = pack_vector(vector[...] + vector_came[...], send_out)


def one_stage_kernel(keep, came, vector, send_out, keep_out, vector_out):
    skip = 2 * vector.shape[0]
    total = keep[...] + came[skip:].astype(F32)
    store_halves(total, 0, send_out, keep_out, skip)
    vector_out[...] = pack_vector(vector[...] + read_vector(came, vector.shape), send_out)


def one_last_kernel(
    heads, place, keep, came, vector, x_out, bc_out, dt_out,
    n1_out, n2_out, xw_out, xb_out, bw_out, bb_out, dtb_out, alog_out, skip_out,
):
    skip = 2 * vector.shape[0]
    total = keep[...] + came[skip:].astype(F32)
    ch = x_out.shape[1]
    nbc = bc_out.shape[1]
    x_out[...] = total[:, :ch]
    bc_out[...] = total[:, ch : ch + nbc]
    dt_out[...] = total[:, ch + nbc : ch + nbc + LANES].T[:heads]
    value = vector[...] + read_vector(came, vector.shape)
    first = place[2] == 0
    half = n1_out.shape[1]
    cq = xb_out.shape[1]
    n1_out[...] = value[5:6, :half]
    n2_out[...] = value[5:6, half : 2 * half]
    mine = jnp.where(first, value[0:8, :cq], value[0:8, cq : 2 * cq])
    xw_out[...] = mine[0:TAPS]
    xb_out[...] = mine[TAPS : TAPS + 1]
    bw_out[...] = value[1 : TAPS + 1, ch : ch + nbc]
    bb_out[...] = value[6:7, :nbc]
    hq = dtb_out.shape[1]
    for i, out in enumerate((dtb_out, alog_out, skip_out)):
        at = ch + i * LANES
        out[...] = jnp.where(
            first, value[0:1, at : at + hq], value[0:1, at + hq : at + 2 * hq]
        )


def close_kernel(own, part, came, n1b, gain, gbc, gbc_came, dn1_out, rows_out):
    tokens = part.shape[0]
    dn1 = (part[...] + came[...]) + n1b[...]
    dn1_out[...] = dn1
    rows_out[0:8, :] = token_sums(dn1 * gain[...] * own[...].astype(F32))
    rows_out[8:16, :] = gbc[tokens:] + gbc_came[tokens:]


def end_kernel(
    place, own, factor1, resid, dn1, gain, rows, rows_far, small, gain2, hidden_out, vector_out
):
    half = dn1.shape[1]
    quarter = half // 2
    hid = own[...].astype(F32)
    factor = factor1[:, :1]
    inner_sum = column(rows[0:8] + rows_far[0:8])[:, :1]
    value = dn1[...]
    change = resid[...] + factor * (value * gain[...]) - hid * (
        factor * factor * factor * inner_sum / (2 * half)
    )
    hidden_out[...] = jnp.where(place[0] == 0, change[:, :quarter], change[:, quarter:])
    shared = jnp.where(place[2] == 0, rows[8:16], rows_far[8:16])
    nbc = rows.shape[1]
    ch = small.shape[1]
    heads = 3 * LANES
    vector_out[...] = jnp.zeros_like(vector_out)
    vector_out[0 : TAPS + 1, 0:ch] = small[0 : TAPS + 1]
    vector_out[0:1, ch : ch + heads] = small[8 + TAPS : 9 + TAPS, 0:heads]
    vector_out[1 : TAPS + 1, ch : ch + nbc] = shared[0:TAPS]
    vector_out[5:6, 0:half] = jnp.sum(value * hid * factor, axis=0, keepdims=True)
    vector_out[5:6, half : 2 * half] = gain2[0:1]
    vector_out[6:7, 0:nbc] = shared[TAPS : TAPS + 1]


def stage_kernel(keep, came, send_out, keep_out):
    rows = keep_out.shape[0]
    total = keep[...] + came[...].astype(F32)
    send_out[...] = total[rows:].astype(BF16)
    keep_out[...] = total[:rows]


def last_kernel(keep, came, *outs):
    total = keep[...] + came[...].astype(F32)
    at = 0
    for out in outs:
        out[...] = total[:, at : at + out.shape[1]]
        at += out.shape[1]


def last_tall_kernel(keep, came, *outs):
    total = keep[...] + came[...].astype(F32)
    width = outs[0].shape[1]
    outs[0][...] = jnp.concatenate([total[:, :width], total[:, width : 2 * width]], axis=0)
    tall = jnp.concatenate([total[:, 2 * width : 3 * width], total[:, 3 * width :]], axis=0)
    size = outs[1].shape[0]
    outs[1][...] = tall[:size]
    outs[2][...] = tall[size:]


def halving_order(steps):
    order = [0]
    for step in reversed(steps):
        order = order + [o | step for o in order]
    return order


def halve(run, steps, at, send, keep, last, outs):
    while True:
        came = swap(send, "dp", steps[at])
        yield None
        at += 1
        if at == len(steps):
            break
        rows, cols = keep.shape
        send, keep = run(
            stage_kernel, [((rows // 2, cols), BF16), ((rows // 2, cols), F32)], keep, came
        )
    yield run(last, outs, keep, came)


def finish(steps):
    result = None
    while result is None:
        result = next(steps)
    return result


def shards(
    hidden,
    segment_ids,
    norm1_gain,
    w_gate,
    w_xin,
    w_dt,
    w_bc,
    w_query,
    w_kv,
    convx_weight,
    convx_bias,
    convbc_weight,
    convbc_bias,
    dt_bias,
    a_log,
    d_skip,
    w_mixout,
    w_attnout,
    norm2_gain,
    w_gateup,
    w_down,
    cotangent,
):
    row = lax.axis_index("row")
    col = lax.axis_index("col")
    me = lax.axis_index("dp")
    count = lax.axis_size("dp")
    spot = me & 3
    place = jnp.stack([col, spot, row]).astype(jnp.int32)
    tokens, quarter = hidden.shape
    half = 2 * quarter
    full_width = 4 * quarter
    piece = half // 4
    ch = w_xin.shape[1]
    nq = w_query.shape[1]
    nkv = w_kv.shape[2]
    nbc = w_bc.shape[1]
    heads = w_dt.shape[1]
    ff = w_down.shape[0]
    cq = convx_bias.shape[0]
    hq = dt_bias.shape[0]

    run = Chain()
    cols = ch + nbc + LANES + ch + nq + nkv
    inner = ch + nq

    near = [1 << b for b in range(count.bit_length() - 1)]
    turned = [near[1], near[0]] + near[2:]
    size = half // count
    within = jnp.asarray(np.tile(np.arange(size), count), jnp.int32)
    both_within = jnp.concatenate([within, within + size])

    def block_order(steps):
        return jnp.asarray(np.repeat(np.array(halving_order(steps)), size), jnp.int32) ^ me

    near_block = block_order(near)
    turned_both = jnp.concatenate([block_order(turned)] * 2)
    order_near = (near_block * size + within)[None]
    order_down = (turned_both * (ff // count) + both_within)[None]
    m_rows = ch // count
    a_rows = nq // count
    order_mix = jnp.where(
        both_within < m_rows,
        turned_both * m_rows + both_within,
        ch + turned_both * a_rows + both_within - m_rows,
    )[None]

    def padded(value):
        return jnp.pad(value, (0, LANES - hq))

    small = jnp.concatenate(
        [convx_weight.T.reshape(-1), convx_bias, norm2_gain, padded(dt_bias), padded(a_log), padded(d_skip)]
    )
    small_rows = 16 * pl.cdiv(small.shape[0] // LANES + 8, 16)
    small = jnp.pad(small, (0, small_rows * LANES - small.shape[0])).reshape(small_rows, LANES)
    gu_mine = lax.dynamic_slice_in_dim(w_gateup, spot * piece, piece, 0).reshape(piece, 2 * ff)
    hid_came = swap(hidden, "col")
    mine = run(
        pieces_kernel,
        [((inner + 3 * ff + 4 * tokens + small_rows, piece), BF16)],
        place, w_mixout, w_attnout, w_down, gu_mine, cotangent, hidden, small,
        smem=(0,),
    )[0]
    got = swap(mine, "row")
    gu = w_gateup.reshape(half, 2 * ff)
    wk = w_kv.reshape(half, nkv)
    wd = jnp.pad(w_dt, ((0, 0), (0, LANES - heads)))
    gain_one = norm1_gain.astype(F32)[None]
    own, part, part_low = run(
        project_kernel,
        [((tokens, half), BF16), ((tokens, cols), F32), ((tokens, cols), BF16)],
        place, hidden, hid_came, gain_one, w_xin, w_bc, wd, w_gate, w_query, wk,
        smem=(0,),
    )
    part_came = swap(part_low, "row")
    bc_par = jnp.concatenate(
        [convbc_weight.T, convbc_bias[None], jnp.zeros((3, nbc), BF16)], 0
    ).astype(F32)
    seg_row = segment_ids.astype(F32)
    seg_col = jnp.broadcast_to(segment_ids[0].astype(F32)[:, None], (tokens, LANES))
    t_first, g_first, in_pair, x_par, head_par, gain_two = run(
        lambda *refs: split_kernel(heads, *refs),
        [
            ((inner + ff, piece), BF16),
            ((piece, 2 * ff), BF16),
            ((3 * tokens, quarter), BF16),
            ((8, ch), F32),
            ((8, LANES), F32),
            ((1, full_width), F32),
        ],
        place, got, cotangent, small,
        smem=(0,), after=(gu, seg_row, seg_col, bc_par, order_near, order_down, order_mix),
    )
    t_second = swap(t_first, "dp", 1)
    g_second = swap(g_first, "dp", 2)
    t_third = swap(t_first, "dp", 2)
    g_third = swap(g_first, "dp", 1)
    in_came = swap(in_pair, "col")
    far, dy_own, dy_far, factor1, n1, left1 = run(
        norm_kernel,
        [
            ((tokens, half), BF16),
            ((tokens, half), BF16),
            ((tokens, half), BF16),
            ((tokens, LANES), F32),
            ((tokens, half), BF16),
            ((tokens, half), BF16),
        ],
        place, in_pair, in_came, own, gain_one, order_near,
        smem=(0,), scratch=[((tokens, half), BF16)], after=(t_second, g_second),
    )
    t_fourth = swap(t_second, "dp", 2)
    g_fourth = swap(g_second, "dp", 1)
    tall_fetch = (t_first, t_second, t_third, t_fourth)

    mixed, raw, pre, ys = run(
        lambda *refs: mix_kernel(ch, nq, *refs),
        [
            ((tokens, inner), BF16),
            ((tokens, cols), F32),
            ((tokens, ch + nbc), F32),
            ((tokens, ch), F32),
        ],
        seg_row, seg_col, factor1, part, part_came, x_par, bc_par, head_par,
    )
    mix_part = run(
        out_kernel,
        [((tokens, full_width), F32)],
        mixed, w_mixout, w_attnout, *tall_fetch,
        after=(g_third, g_fourth),
    )[0]
    mix_came = swap(mix_part, "col")
    grad_act = run(
        lambda *refs: act_grad_kernel(inner, *refs),
        [((tokens, ff), F32)],
        dy_own, dy_far, w_down, *tall_fetch,
    )[0]
    h2, n2, act, ggu, n2_part, down_keep, down_send = run(
        feed_kernel,
        [
            ((tokens, full_width), F32),
            ((tokens, half), BF16),
            ((tokens, ff), BF16),
            ((tokens, 2 * ff), BF16),
            ((tokens, full_width), F32),
            ((tokens, quarter), F32),
            ((tokens, quarter), F32),
        ],
        place, own, far, mix_part, mix_came, gain_two,
        gu, g_first, g_third, g_second, g_fourth, grad_act, w_down,
        smem=(0,),
    )
    n2_came = swap(n2_part, "col")
    down_came = swap(down_send, "col")
    rows = half // 2

    g_send, d_send, g_left, d_left = run(
        feed_grad_kernel,
        [
            ((rows, 2 * ff), BF16),
            ((rows, 2 * half), BF16),
            ((tokens, rows), BF16),
            ((tokens, half), BF16),
        ],
        n2, act, ggu, dy_own, order_near, order_down,
    )
    g_came = swap(g_send, "dp", near[0])
    d_came = swap(d_send, "dp", turned[0])
    dym, resid, low, gain2_sum, output, m_send, m_left, g_two, two_send = run(
        lambda *refs: turn_kernel(ch, nq, *refs),
        [
            ((tokens, inner), F32),
            ((tokens, half), F32),
            ((tokens, half), BF16),
            ((8, half), F32),
            ((tokens, quarter), BF16),
            ((rows, 2 * half), BF16),
            ((tokens, half), BF16),
            ((tokens, ch + nq + nkv), BF16),
            ((rows, ch + nq + nkv), BF16),
        ],
        place, dy_own, dy_far, h2, n2_part, n2_came, gain_two,
        w_mixout, w_attnout, *tall_fetch, down_keep, down_came,
        mixed, order_mix, seg_row, seg_col, raw, pre, ys, x_par, left1,
        smem=(0,),
    )
    two_came = swap(two_send, "dp", near[0])
    m_came = swap(m_send, "dp", turned[0])
    gx, gdt, gbc, small_sum = run(
        lambda *refs: unmix_one_kernel(ch, nq, *refs),
        [
            ((tokens, ch), BF16),
            ((tokens, LANES), BF16),
            ((tokens + 8, nbc), F32),
            ((16, ch), F32),
        ],
        seg_row, seg_col, raw, pre, ys, dym, x_par, bc_par, head_par,
        scratch=[((tokens, ch), F32), ((tokens, ch), F32), ((tokens, tokens), F32)],
    )
    gbc_came = swap(gbc, "col")

    def quarters(width):
        return [((rows // 2, width), BF16), ((rows // 2, width), F32)]

    g_send, g_keep = run(wide_kernel, quarters(2 * ff), g_left, ggu, g_came)
    s_gu = halve(run, near, 1, g_send, g_keep, last_kernel, [((size, 2 * ff), F32)])
    next(s_gu)
    n1_part, n1_bc, gbc_both, one_send = run(
        back_kernel,
        [
            ((tokens, half), F32),
            ((tokens, half), F32),
            ((tokens, nbc), BF16),
            ((rows, ch + nbc + LANES), BF16),
        ],
        g_two, gx, gdt, gbc, gbc_came, w_xin, w_bc, wd, w_gate, w_query, wk, left1,
    )
    one_came = swap(one_send, "dp", near[0])
    n1_came = swap(n1_part, "col")
    def one_outs(keep):
        width = ch + nbc + LANES
        return [((keep + 16, width), BF16), ((keep, width), F32), ((8, ch + nbc + LANES), F32)]

    tall_send, tall_keep = run(
        tall_kernel, quarters(4 * half), d_left, dy_own, d_came, m_left, low, m_came
    )
    s_tall = halve(
        run, turned, 1, tall_send, tall_keep, last_tall_kernel,
        [((2 * size, half), F32), ((m_rows, half), F32), ((a_rows, half), F32)],
    )
    next(s_tall)
    two_send, two_keep = run(wide_kernel, quarters(ch + nq + nkv), left1, g_two, two_came)
    s_two = halve(
        run, near, 1, two_send, two_keep, last_kernel,
        [((size, ch), F32), ((size, nq), F32), ((size, nkv), F32)],
    )
    next(s_two)
    next(s_gu)
    dn1, sum_rows = run(
        close_kernel,
        [((tokens, half), F32), ((16, tokens), F32)],
        own, n1_part, n1_came, n1_bc, gain_one, gbc, gbc_came,
    )
    rows_far = swap(sum_rows, "row")
    next(s_two)
    grad_hidden, vector = run(
        end_kernel,
        [((tokens, quarter), F32), ((8, ch + nbc + LANES), F32)],
        place, own, factor1, resid, dn1, gain_one, sum_rows, rows_far, small_sum, gain2_sum,
        smem=(0,),
    )
    vector_came = swap(vector, "dp", near[0])
    r_gu = finish(s_gu)
    one_send, one_keep, vector = run(
        one_kernel, one_outs(rows // 2),
        left1, gx, gbc_both, gdt, one_came, vector, vector_came,
    )
    next(s_tall)
    r_two = finish(s_two)
    for step in near[1:-1]:
        one_came = swap(one_send, "dp", step)
        one_send, one_keep, vector = run(
            one_stage_kernel, one_outs(one_keep.shape[0] // 2), one_keep, one_came, vector
        )
    one_came = swap(one_send, "dp", near[-1])
    r_tall = finish(s_tall)
    (
        r_xin, r_bc, r_dt, o_norm1, o_norm2, o_cxw, o_cxb, o_cbw, o_cbb, o_dtb, o_alog, o_dsk
    ) = run(
        lambda *refs: one_last_kernel(heads, *refs),
        [
            ((size, ch), F32),
            ((size, nbc), F32),
            ((heads, size), F32),
            ((1, half), F32),
            ((1, half), F32),
            ((TAPS, cq), F32),
            ((1, cq), F32),
            ((TAPS, nbc), F32),
            ((1, nbc), F32),
            ((1, hq), F32),
            ((1, hq), F32),
            ((1, hq), F32),
        ],
        place, one_keep, one_came, vector,
        smem=(0,),
    )
    r_gate, r_query, r_kv = r_two
    r_down, r_mixout, r_attnout = r_tall
    return (
        output,
        grad_hidden,
        o_norm1[0],
        r_gate,
        r_xin,
        r_dt.T,
        r_bc,
        r_query,
        r_kv.reshape(size, 1, nkv),
        o_cxw.T,
        o_cxb[0],
        o_cbw.T,
        o_cbb[0],
        o_dtb[0],
        o_alog[0],
        o_dsk[0],
        r_mixout,
        r_attnout,
        o_norm2[0],
        r_gu[0].reshape(size, 2, ff),
        r_down,
    )


def solution(mesh):
    placed = (
        P("dp", ("row", "col")),
        P("dp", None),
        P("row"),
        P("row", "col"),
        P("row", "col"),
        P("row", "col"),
        P("row", None),
        P("row", "col"),
        P("row", "col", None),
        P(("col", "row"), None),
        P(("col", "row")),
        P(),
        P(),
        P(("col", "row")),
        P(("col", "row")),
        P(("col", "row")),
        P("col", "row"),
        P("col", "row"),
        P("row"),
        P("row", None, "col"),
        P("col", "row"),
        P("dp", ("row", "col")),
    )
    return jax.shard_map(
        shards,
        mesh=mesh,
        in_specs=placed,
        out_specs=(
            P("dp", ("row", "col")),
            P("dp", ("row", "col")),
            P("row"),
            P(("row", "dp"), "col"),
            P(("row", "dp"), "col"),
            P(("row", "dp"), "col"),
            P(("row", "dp"), None),
            P(("row", "dp"), "col"),
            P(("row", "dp"), "col", None),
            P(("col", "row"), None),
            P(("col", "row")),
            P(),
            P(),
            P(("col", "row")),
            P(("col", "row")),
            P(("col", "row")),
            P(("col", "dp"), "row"),
            P(("col", "dp"), "row"),
            P("row"),
            P(("row", "dp"), None, "col"),
            P(("col", "dp"), "row"),
        ),
        check_vma=False,
    )
```

```python
import jax
import jax.numpy as jnp
import numpy as np
from jax import lax
from jax.experimental import pallas as pl
from jax.experimental.pallas import tpu as pltpu
from jax.sharding import PartitionSpec as P

NORM_EPS = 1e-05
F32 = jnp.float32
BF16 = jnp.bfloat16
HEAD = 64
LANES = 128
TAPS = 4
FAR = -1e30


def swap(values, axis, step=1):
    count = lax.axis_size(axis)
    return lax.ppermute(values, axis, [(i, i ^ step) for i in range(count)])


def dot(left, right):
    return jnp.dot(left, right, preferred_element_type=F32)


def dot_bt(left, right):
    return lax.dot_general(left, right, (((1,), (1,)), ((), ())), preferred_element_type=F32)


def dot_at(left, right):
    return lax.dot_general(left, right, (((0,), (0,)), ((), ())), preferred_element_type=F32)


def fine(left, right, dims=((1,), (0,))):
    return lax.dot_general(
        left, right, (dims, ((), ())), precision=lax.Precision.HIGHEST, preferred_element_type=F32
    )


class Chain:
    def __init__(self):
        self.token = jnp.zeros((8, LANES), F32)

    def __call__(self, kernel, outs, *args, scratch=(), smem=(), after=()):
        plain = pltpu.VMEM
        specs = [
            pl.BlockSpec(memory_space=pltpu.SMEM if i in smem else plain)
            for i in range(len(args))
        ]
        extra = (self.token,) + tuple(after)
        count = len(args)
        held = count + len(extra)

        def body(*refs):
            refs[held][...] = jnp.zeros((8, LANES), F32)
            kernel(*refs[:count], *refs[held + 1 :])

        results = pl.pallas_call(
            body,
            out_shape=[jax.ShapeDtypeStruct((8, LANES), F32)]
            + [jax.ShapeDtypeStruct(s, d) for s, d in outs],
            in_specs=specs + [pl.BlockSpec(memory_space=pl.ANY)] * len(extra),
            out_specs=[pl.BlockSpec(memory_space=pltpu.VMEM)]
            + [pl.BlockSpec(memory_space=plain)] * len(outs),
            scratch_shapes=[pltpu.VMEM(s, d) if d is not None else s for s, d in scratch],
            compiler_params=pltpu.CompilerParams(vmem_limit_bytes=64 << 20),
            cost_estimate=pl.CostEstimate(flops=0, bytes_accessed=0, transcendentals=0),
        )(*args, *extra)
        self.token = results[0]
        return results[1:]


def two_parts(value):
    high = value.astype(BF16)
    return high, (value - high.astype(F32)).astype(BF16)


def dot_three(product, left, right):
    return product(left[0], right[0]) + (product(left[1], right[0]) + product(left[0], right[1]))


def iota(shape, dim):
    return lax.broadcasted_iota(jnp.int32, shape, dim)


def column(row_vector):
    ones = jnp.full((row_vector.shape[0], LANES), 1.0 / row_vector.shape[0], F32)
    return fine(row_vector, ones, ((0,), (0,)))


def token_sums(values):
    return fine(jnp.ones((8, values.shape[1]), F32), values, ((1,), (1,)))


def pieces_kernel(place, wm, wa, wd, gu, cot, hid, small, out):
    piece = out.shape[1]
    at = pl.multiple_of(place[1] * piece, piece)
    row = 0
    for w in (wm, wa, wd):
        out[row : row + w.shape[0]] = w[:, pl.ds(at, piece)]
        row += w.shape[0]
    for value in (gu, cot, hid):
        for j in range(value.shape[1] // piece):
            out[row : row + value.shape[0]] = value[:, j * piece : (j + 1) * piece]
            row += value.shape[0]
    out[row:] = small[...]


def join_small(place, heads, own, far, x_par_out, head_out, gain_out):
    first = place[2] == 0
    a = jnp.where(first, own, far)
    b = jnp.where(first, far, own)
    width = x_par_out.shape[1] // 2
    count = width // LANES
    x_par_out[...] = jnp.zeros_like(x_par_out)
    for k in range(TAPS + 1):
        for i in range(count):
            at = k * count + i
            x_par_out[k : k + 1, i * LANES : (i + 1) * LANES] = a[at : at + 1]
            x_par_out[k : k + 1, width + i * LANES : width + (i + 1) * LANES] = b[at : at + 1]
    row = (TAPS + 1) * count
    pieces = gain_out.shape[1] // (2 * LANES)
    for j in range(pieces):
        gain_out[:, j * LANES : (j + 1) * LANES] = own[row + j : row + j + 1]
        block = jnp.zeros((1, LANES), F32)
        for i in range(pieces):
            block = block + jnp.where((place[1] ^ j) == i, far[row + i : row + i + 1], 0.0)
        at = (pieces + j) * LANES
        gain_out[:, at : at + LANES] = block
    row += pieces
    joined = a[row : row + 8] + pltpu.roll(b[row : row + 8], heads // 2, 1)
    head_out[...] = joined
    pick = jnp.where(
        iota((LANES, 2 * width), 0) == iota((LANES, 2 * width), 1) // HEAD, 1.0, 0.0
    )
    x_par_out[TAPS + 1 : TAPS + 2] = fine(joined, pick)[2:3]


def split_kernel(
    heads, place, got, cot, small, t_out, g_out, pair_out, x_par_out, head_out, gain_out
):
    piece = got.shape[1]
    tokens = cot.shape[0]
    row = t_out.shape[0]
    t_out[...] = got[0:row]
    for j in range(g_out.shape[1] // piece):
        g_out[:, j * piece : (j + 1) * piece] = got[row : row + piece]
        row += piece
    pair_out[0:tokens] = cot[...]
    for i in (1, 2):
        for j in range(cot.shape[1] // piece):
            pair_out[i * tokens : (i + 1) * tokens, j * piece : (j + 1) * piece] = got[
                row : row + tokens
            ]
            row += tokens
    own = small[...].astype(F32)
    far = got[row:].astype(F32)
    join_small(place, heads, own, far, x_par_out, head_out, gain_out)


def far_order(place, value, out):
    piece = value.shape[1] // 4
    for j in range(4):
        at = pl.multiple_of((place[1] ^ j) * piece, piece)
        out[:, j * piece : (j + 1) * piece] = value[:, pl.ds(at, piece)]


def side_by_side(place, a, b, out):
    width = a.shape[1]
    first = place[0] == 0
    out[:, :width] = jnp.where(first, a, b)
    out[:, width:] = jnp.where(first, b, a)


def project_kernel(place, mine, came, gain, wx, wb, wd, wg, wq, wk, own_out, p_out, low_out):
    side_by_side(place, mine[...], came[...], own_out)
    high, low = two_parts(own_out[...].astype(F32) * gain[...])
    at = 0
    for w in (wx, wb, wd, wg, wq, wk):
        size = w.shape[1]
        part = dot(high, w[...]) + dot(low, w[...])
        p_out[:, at : at + size] = part
        low_out[:, at : at + size] = part.astype(BF16)
        at += size


def norm_kernel(
    place, pair, came, own, gain, order,
    far_out, dy_own, dy_far, factor_out, n1_out, left_out, far_tmp,
):
    tokens = own.shape[0]
    side_by_side(place, pair[0:tokens], came[0:tokens], dy_own)
    side_by_side(place, pair[tokens : 2 * tokens], came[tokens : 2 * tokens], far_tmp)
    far_order(place, far_tmp, dy_far)
    side_by_side(place, pair[2 * tokens :], came[2 * tokens :], far_tmp)
    far_order(place, far_tmp, far_out)
    hid = own[...].astype(F32)
    far = far_out[...].astype(F32)
    mean = jnp.sum(hid * hid + far * far, axis=1, keepdims=True) / (2 * hid.shape[1])
    factor = lax.rsqrt(mean + NORM_EPS)
    factor_out[...] = jnp.broadcast_to(factor, factor_out.shape)
    n1_out[...] = (hid * factor * gain[...]).astype(BF16)
    left_out[...] = permuted(n1_out[...], order[...])


def masks(seg_row, seg_col, turned):
    tokens = seg_row.shape[1]
    i = iota((tokens, tokens), 1 if turned else 0)
    j = iota((tokens, tokens), 0 if turned else 1)
    same = seg_col[:, :1] == seg_row[...]
    return jnp.where((i >= j) & same, 0.0, FAR)


def valids(seg_col):
    seg = seg_col[...]
    t = iota(seg.shape, 0)
    return [
        jnp.where((t >= k) & (pltpu.roll(seg, k, 0) == seg), 1.0, 0.0) for k in range(1, TAPS)
    ]


def conv(block, taps, bias, valid):
    total = block * taps[TAPS - 1 : TAPS] + bias
    for k in range(1, TAPS):
        total = total + (pltpu.roll(block, k, 0) * valid[k - 1]) * taps[TAPS - 1 - k : TAPS - k]
    return total


def conv_turn(grad, block, taps, valid):
    tokens = grad.shape[0]
    back = grad * taps[TAPS - 1 : TAPS]
    rows = [None] * TAPS
    rows[TAPS - 1] = jnp.sum(grad * block, axis=0, keepdims=True)
    for k in range(1, TAPS):
        kept = grad * valid[k - 1]
        back = back + pltpu.roll(kept, tokens - k, 0) * taps[TAPS - 1 - k : TAPS - k]
        rows[TAPS - 1 - k] = jnp.sum(kept * pltpu.roll(block, k, 0), axis=0, keepdims=True)
    rows.append(jnp.sum(grad, axis=0, keepdims=True))
    rows.append(jnp.zeros((8 - len(rows), grad.shape[1]), F32))
    return back, jnp.concatenate(rows, 0)


def silu_turn(value):
    sig = jax.nn.sigmoid(value)
    return value * sig, sig * (1.0 + value * (1.0 - sig))


def steps(dt_raw, head_par):
    shifted = dt_raw + head_par[0:1]
    return jnp.maximum(shifted, 0.0) + jnp.log1p(jnp.exp(-jnp.abs(shifted)))


def mix_kernel(
    ch, nq, seg_row, seg_col, factor, own, came, x_par, bc_par, head_par,
    mixed_out, sums_out, pre_out, y_out,
):
    tokens = own.shape[0]
    nbc = bc_par.shape[1]
    state = nbc // 2
    sums_out[...] = factor[:, :1] * (own[...] + came[...].astype(F32))
    lane = iota((tokens, LANES), 1)
    low = lane < HEAD
    mask = masks(seg_row, seg_col, False)
    valid = valids(seg_col)
    for b in range(nbc // LANES):
        at = ch + b * LANES
        part = slice(b * LANES, (b + 1) * LANES)
        pre_out[:, at : at + LANES] = conv(
            sums_out[:, at : at + LANES], bc_par[0:TAPS, part], bc_par[TAPS : TAPS + 1, part], valid
        )
    bcc = pre_out[:, ch : ch + nbc]
    bcc = bcc * jax.nn.sigmoid(bcc)
    inner = fine(bcc[:, state:], bcc[:, :state], ((1,), (1,)))
    dt = steps(sums_out[:, ch + nbc : ch + nbc + LANES], head_par)
    tri = jnp.where(iota((tokens, tokens), 0) >= iota((tokens, tokens), 1), 1.0, 0.0)
    cum = fine(tri, dt * -jnp.exp(head_par[1:2]))
    cum_row = cum.T
    base = ch + nbc + LANES
    for p in range(ch // LANES):
        part = slice(p * LANES, (p + 1) * LANES)
        pre = conv(sums_out[:, part], x_par[0:TAPS, part], x_par[TAPS : TAPS + 1, part], valid)
        pre_out[:, part] = pre
        xc = pre * jax.nn.sigmoid(pre)
        h = 2 * p
        xdt = (xc * jnp.where(low, dt[:, h : h + 1], dt[:, h + 1 : h + 2])).astype(BF16)
        ys = []
        for e in (h, h + 1):
            decay = jnp.exp((cum[:, e : e + 1] - cum_row[e : e + 1]) + mask)
            ys.append(dot((inner * decay).astype(BF16), xdt))
        y = jnp.where(low, ys[0], ys[1])
        y_out[:, part] = y
        y = y + x_par[TAPS + 1 : TAPS + 2, part] * xc
        z = sums_out[:, base + p * LANES : base + (p + 1) * LANES]
        mixed_out[:, part] = (y * (z * jax.nn.sigmoid(z))).astype(BF16)
    at = base + ch
    kv = sums_out[:, at + nq : at + nq + LANES]
    kv_turn = pltpu.roll(kv, HEAD, 1)
    keys = two_parts(jnp.where(low, kv, kv_turn))
    vals = two_parts(jnp.where(low, kv_turn, kv))
    for p in range(nq // LANES):
        query = sums_out[:, at + p * LANES : at + (p + 1) * LANES] * (HEAD ** -0.5)
        outs = []
        for side in (low, ~low):
            score = dot_three(dot_bt, two_parts(jnp.where(side, query, 0.0)), keys) + mask
            score = jnp.exp(score - jnp.max(score, axis=1, keepdims=True))
            total = jnp.sum(score, axis=1, keepdims=True)
            outs.append(dot_three(dot, two_parts(score), vals) / total)
        mixed_out[:, ch + p * LANES : ch + (p + 1) * LANES] = jnp.where(
            low, outs[0], outs[1]
        ).astype(BF16)


def unmix_two_kernel(ch, nq, seg_row, seg_col, sums, pre, ys, dym, x_par, gtwo_out):
    tokens = sums.shape[0]
    base = sums.shape[1] - (ch + nq + LANES)
    low = iota((tokens, LANES), 1) < HEAD
    mask = masks(seg_row, seg_col, True)
    for p in range(ch // LANES):
        part = slice(p * LANES, (p + 1) * LANES)
        value = pre[:, part]
        xc = value * jax.nn.sigmoid(value)
        _, gate_turn = silu_turn(sums[:, base + p * LANES : base + (p + 1) * LANES])
        y = ys[:, part] + x_par[TAPS + 1 : TAPS + 2, part] * xc
        gtwo_out[:, part] = (dym[:, part] * y * gate_turn).astype(BF16)
    at = base + ch
    kv = sums[:, at + nq : at + nq + LANES]
    kv_turn = pltpu.roll(kv, HEAD, 1)
    keys = jnp.where(low, kv, kv_turn).astype(BF16)
    vals = jnp.where(low, kv_turn, kv).astype(BF16)
    dk = jnp.zeros((tokens, LANES), F32)
    dv = jnp.zeros((tokens, LANES), F32)
    for p in range(nq // LANES):
        query = sums[:, at + p * LANES : at + (p + 1) * LANES] * (HEAD ** -0.5)
        grad = dym[:, ch + p * LANES : ch + (p + 1) * LANES]
        dqs = []
        for side in (low, ~low):
            q_low = jnp.where(side, query, 0.0).astype(BF16)
            g_low = jnp.where(side, grad, 0.0).astype(BF16)
            score = dot_bt(keys, q_low) + mask
            score = jnp.exp(score - jnp.max(score, axis=0, keepdims=True))
            prob = score * (1.0 / jnp.sum(score, axis=0, keepdims=True))
            dprob = dot_bt(vals, g_low)
            dv = dv + dot(prob.astype(BF16), g_low)
            inner_sum = jnp.sum(prob * dprob, axis=0, keepdims=True)
            dscore = (prob * (dprob - inner_sum)).astype(BF16)
            dk = dk + dot(dscore, q_low)
            dqs.append(dot_at(dscore, keys))
        gtwo_out[:, ch + p * LANES : ch + (p + 1) * LANES] = (
            jnp.where(low, dqs[0], dqs[1]) * (HEAD ** -0.5)
        ).astype(BF16)
    dk = dk + pltpu.roll(dk, HEAD, 1)
    dv = dv + pltpu.roll(dv, HEAD, 1)
    gtwo_out[:, ch + nq : ch + nq + LANES] = jnp.where(low, dk, dv).astype(BF16)

def unmix_one_kernel(
    ch, nq, seg_row, seg_col, sums, pre, ys, dym, x_par, bc_par, head_par,
    gx_out, gdt_out, gbc_out, small_out, prod_a, prod_b, turned,
):
    tokens = sums.shape[0]
    nbc = bc_par.shape[1]
    state = nbc // 2
    lane = iota((tokens, LANES), 1)
    low = lane < HEAD
    mask = masks(seg_row, seg_col, True)
    valid = valids(seg_col)
    bc_pre = pre[:, ch : ch + nbc]
    bcc, bcc_turn = silu_turn(bc_pre)
    b_in = bcc[:, :state]
    c_in = bcc[:, state:]
    inner = fine(b_in, c_in, ((1,), (1,)))
    dt_raw = sums[:, ch + nbc : ch + nbc + LANES]
    dt = steps(dt_raw, head_par)
    rate = jnp.exp(head_par[1:2])
    tri = jnp.where(iota((tokens, tokens), 0) >= iota((tokens, tokens), 1), 1.0, 0.0)
    cum = fine(tri, dt * -rate)
    cum_row = cum.T
    base = ch + nbc + LANES
    small_out[...] = jnp.zeros_like(small_out)
    turned[...] = jnp.zeros_like(turned)
    for p in range(ch // LANES):
        part = slice(p * LANES, (p + 1) * LANES)
        xc, xc_turn = silu_turn(pre[:, part])
        skip = x_par[TAPS + 1 : TAPS + 2, part]
        z = sums[:, base + p * LANES : base + (p + 1) * LANES]
        gate = z * jax.nn.sigmoid(z)
        dy_in = dym[:, part]
        y = ys[:, part]
        dy = dy_in * gate
        h = 2 * p
        dt_pair = jnp.where(low, dt[:, h : h + 1], dt[:, h + 1 : h + 2])
        xdt = xc * dt_pair
        dy_low = dy.astype(BF16)
        x_low = xdt.astype(BF16)
        sides = []
        for e, side in ((h, low), (h + 1, ~low)):
            decay = jnp.exp((cum_row[e : e + 1] - cum[:, e : e + 1]) + mask)
            turned[...] += dot_bt(jnp.where(side, xdt, 0.0).astype(BF16), dy_low) * decay
            sides.append(dot((inner * decay).astype(BF16), dy_low))
        dxdt = jnp.where(low, sides[0], sides[1])
        prod_a[:, part] = dy_low.astype(F32) * y - x_low.astype(F32) * dxdt
        prod_b[:, part] = dxdt * xc
        small_out[8 + TAPS + 1 : 8 + TAPS + 2, part] = jnp.sum(dy * xc, axis=0, keepdims=True)
        dpre = (skip * dy + dxdt * dt_pair) * xc_turn
        back, rows = conv_turn(dpre, sums[:, part], x_par[0:TAPS, part], valid)
        gx_out[:, part] = back.astype(BF16)
        small_out[0:8, part] = rows
    pick = jnp.where(iota((ch, LANES), 0) // HEAD == iota((ch, LANES), 1), 1.0, 0.0)
    dcum = fine(prod_a[...], pick)
    ddt = fine(prod_b[...], pick)
    after = fine(tri, dcum, ((0,), (0,)))
    ddt = ddt - rate * after
    ddt = ddt * jax.nn.sigmoid(dt_raw + head_par[0:1])
    gdt_out[...] = ddt.astype(BF16)
    small_out[8 + TAPS : 8 + TAPS + 1, 0:LANES] = jnp.sum(ddt, axis=0, keepdims=True)
    small_out[8 + TAPS : 8 + TAPS + 1, LANES : 2 * LANES] = jnp.sum(
        after * (-dt * rate), axis=0, keepdims=True
    )
    skip_sum = jnp.broadcast_to(small_out[8 + TAPS + 1 : 8 + TAPS + 2, :], (8, ch))
    small_out[8 + TAPS : 8 + TAPS + 1, 2 * LANES : 3 * LANES] = fine(skip_sum, pick)[0:1]
    dinner = turned[...]
    d_b = fine(dinner, c_in) * bcc_turn[:, :state]
    d_c = fine(dinner, b_in, ((0,), (0,))) * bcc_turn[:, state:]
    for b, grad in enumerate((d_b, d_c)):
        at = ch + b * LANES
        part = slice(b * LANES, (b + 1) * LANES)
        back, rows = conv_turn(grad, sums[:, at : at + LANES], bc_par[0:TAPS, part], valid)
        gbc_out[0:tokens, part] = back
        gbc_out[tokens : tokens + 8, part] = rows


def tall_far(fetch, start, size):
    return jnp.concatenate(
        [r[start : start + size] for r in fetch], axis=1
    )


def out_kernel(mixed, wm, wa, t0, t1, t2, t3, part_out):
    fetch = (t0, t1, t2, t3)
    half = wm.shape[1]
    ch = wm.shape[0]
    value = mixed[...]
    part_out[:, :half] = dot(value[:, :ch], wm[...]) + dot(value[:, ch:], wa[...])
    part_out[:, half:] = dot(value, tall_far(fetch, 0, value.shape[1]))


def norm_factor(value):
    return lax.rsqrt(jnp.mean(value * value, axis=1, keepdims=True) + NORM_EPS)


def act_grad_kernel(inner, dy_own, dy_far, wd, t0, t1, t2, t3, ga_out):
    fetch = (t0, t1, t2, t3)
    ff = wd.shape[0]
    ga_out[...] = dot_bt(dy_own[...], wd[...]) + dot_bt(
        dy_far[...], tall_far(fetch, inner, ff)
    )


def feed_kernel(
    place, own, far, part, came, gain, gu, gu0, gu1, gu2, gu3, grad_act, wd,
    h2_out, n2_out, act_out, ggu_out, n2p_out, keep_out, send_out,
):
    half = own.shape[1]
    quarter = half // 2
    h2_out[:, :half] = own[...].astype(F32) + (part[:, :half] + came[:, :half])
    h2_out[:, half:] = far[...].astype(F32) + (part[:, half:] + came[:, half:])
    h2 = h2_out[...]
    n2 = (h2 * norm_factor(h2) * gain[...]).astype(BF16)
    n2_out[...] = n2[:, :half]
    gu_far = jnp.concatenate([gu0[...], gu1[...], gu2[...], gu3[...]], axis=0)
    ff = wd.shape[0]
    gate_up = dot(n2[:, :half], gu[...]) + dot(n2[:, half:], gu_far)
    gate = gate_up[:, :ff]
    up = gate_up[:, ff:]
    silu, silu_grad = silu_turn(gate)
    act = (silu * up).astype(BF16)
    act_out[...] = act
    ga = grad_act[...]
    ggu_out[:, :ff] = (ga * up * silu_grad).astype(BF16)
    ggu_out[:, ff:] = (ga * silu).astype(BF16)
    ggu = ggu_out[...]
    n2p_out[:, :half] = dot_bt(ggu, gu[...])
    n2p_out[:, half:] = dot_bt(ggu, gu_far)
    down = dot(act, wd[...])
    first = place[0] == 0
    keep_out[...] = jnp.where(first, down[:, :quarter], down[:, quarter:])
    send_out[...] = jnp.where(first, down[:, quarter:], down[:, :quarter])


def permuted(left, source):
    width = left.shape[1]
    hot = jnp.where(iota((width, source.shape[1]), 0) == source, 1.0, 0.0).astype(BF16)
    return dot(left, hot).astype(BF16)


def feed_grad_kernel(
    n2, act, ggu, dy, order, order2, g_send, d_send, g_left, d_left
):
    rows = g_send.shape[0]
    width = dy.shape[1]
    left = permuted(n2[...], order[...])
    g_send[...] = dot_at(left[:, rows:], ggu[...]).astype(BF16)
    g_left[...] = left[:, :rows]
    left = permuted(act[...], order2[...])
    for s in (0, 1):
        cut = 2 * s * rows
        d_send[:, s * width : (s + 1) * width] = dot_at(
            left[:, cut + rows : cut + 2 * rows], dy[...]
        ).astype(BF16)
        d_left[:, s * rows : (s + 1) * rows] = left[:, cut : cut + rows]


def turn_kernel(
    ch, nq, place, dy_own, dy_far, h2, part, came, gain, wm, wa, t0, t1, t2, t3, d_keep, d_came,
    mixed, order_mix, seg_row, seg_col, sums, pre, ys, x_par, left1,
    dym_out, resid_out, low_out, gain_out, output_out, m_send, m_left, gtwo_out, two_send,
):
    fetch = (t0, t1, t2, t3)
    half = dy_own.shape[1]
    quarter = half // 2
    value = h2[...]
    output_out[...] = (
        jnp.where(place[0] == 0, value[:, :quarter], value[:, quarter:half])
        + (d_keep[...] + d_came[...])
    ).astype(BF16)
    factor = norm_factor(value)
    dn2 = part[...] + came[...]
    gained = dn2 * gain[...]
    inner_sum = jnp.sum(gained * value, axis=1, keepdims=True)
    gain_out[...] = jnp.broadcast_to(
        jnp.sum(dn2[:, :half] * value[:, :half] * factor, axis=0, keepdims=True), gain_out.shape
    )
    slope = factor * factor * factor * inner_sum / (2 * half)
    change = factor * gained - value * slope
    dh_own = dy_own[...].astype(F32) + change[:, :half]
    dh_far = dy_far[...].astype(F32) + change[:, half:]
    resid_out[...] = dh_own
    low_own = dh_own.astype(BF16)
    low_out[...] = low_own
    dym = dot_bt(dh_far.astype(BF16), tall_far(fetch, 0, dym_out.shape[1]))
    dym_out[:, :ch] = dym[:, :ch] + dot_bt(low_own, wm[...])
    dym_out[:, ch:] = dym[:, ch:] + dot_bt(low_own, wa[...])
    unmix_two_kernel(ch, nq, seg_row, seg_col, sums, pre, ys, dym_out, x_par, gtwo_out)
    rows = two_send.shape[0]
    two_send[...] = dot_at(left1[:, rows:], gtwo_out[...]).astype(BF16)
    left = permuted(mixed[...], order_mix[...])
    for s in (0, 1):
        cut = 2 * s * rows
        m_send[:, s * half : (s + 1) * half] = dot_at(
            left[:, cut + rows : cut + 2 * rows], low_own
        ).astype(BF16)
        m_left[:, s * rows : (s + 1) * rows] = left[:, cut : cut + rows]


def back_kernel(
    g_two, gx, gdt, gbc, gbc_came, wx, wb, wd, wg, wq, wk, left1,
    n1p_out, n1b_out, both_out, one_send,
):
    tokens = gx.shape[0]
    both = (gbc[0:tokens] + gbc_came[0:tokens]).astype(BF16)
    both_out[...] = both
    rows = one_send.shape[0]
    left = left1[:, rows:]
    at = 0
    for right in (gx[...], both, gdt[...]):
        size = right.shape[1]
        one_send[:, at : at + size] = dot_at(left, right).astype(BF16)
        at += size
    ch = wg.shape[1]
    nq = wq.shape[1]
    total = dot_bt(gx[...], wx[...]) + dot_bt(gdt[...], wd[...])
    total = total + dot_bt(g_two[:, :ch], wg[...]) + dot_bt(g_two[:, ch : ch + nq], wq[...])
    n1p_out[...] = total + dot_bt(g_two[:, ch + nq :], wk[...])
    n1b_out[...] = dot_bt(both, wb[...])


def store_halves(total, at, send_out, keep_out, skip=0):
    rows = keep_out.shape[0]
    size = total.shape[1]
    send_out[skip:, at : at + size] = total[rows:].astype(BF16)
    keep_out[:, at : at + size] = total[:rows]


def wide_kernel(left, right, came, send_out, keep_out):
    total = dot_at(left[:, : came.shape[0]], right[...]) + came[...].astype(F32)
    store_halves(total, 0, send_out, keep_out)


def tall_kernel(d_left, dy, d_came, m_left, low, m_came, send_out, keep_out):
    at = 0
    for left, right, came in ((d_left, dy, d_came), (m_left, low, m_came)):
        rows = came.shape[0]
        width = right.shape[1]
        for s in (0, 1):
            total = dot_at(left[:, s * rows : (s + 1) * rows], right[...])
            total = total + came[:, s * width : (s + 1) * width].astype(F32)
            store_halves(total, at, send_out, keep_out)
            at += width


def pack_vector(value, out):
    rows, width = value.shape
    high = value.astype(BF16)
    low = (value - high.astype(F32)).astype(BF16)
    out[0:rows, 0:width] = high
    out[rows : 2 * rows, 0:width] = low
    return high.astype(F32) + low.astype(F32)


def read_vector(came, shape):
    rows, width = shape
    return came[0:rows, 0:width].astype(F32) + came[rows : 2 * rows, 0:width].astype(F32)


def one_kernel(left1, gx, both, gdt, came, vector, vector_came, send_out, keep_out, vector_out):
    left = left1[:, : came.shape[0]]
    skip = 2 * vector.shape[0]
    at = 0
    for right in (gx[...], both[...], gdt[...]):
        size = right.shape[1]
        total = dot_at(left, right) + came[:, at : at + size].astype(F32)
        store_halves(total, at, send_out, keep_out, skip)
        at += size
    vector_out[...] = pack_vector(vector[...] + vector_came[...], send_out)


def one_stage_kernel(keep, came, vector, send_out, keep_out, vector_out):
    skip = 2 * vector.shape[0]
    total = keep[...] + came[skip:].astype(F32)
    store_halves(total, 0, send_out, keep_out, skip)
    vector_out[...] = pack_vector(vector[...] + read_vector(came, vector.shape), send_out)


def one_last_kernel(
    heads, place, keep, came, vector, x_out, bc_out, dt_out,
    n1_out, n2_out, xw_out, xb_out, bw_out, bb_out, dtb_out, alog_out, skip_out,
):
    skip = 2 * vector.shape[0]
    total = keep[...] + came[skip:].astype(F32)
    ch = x_out.shape[1]
    nbc = bc_out.shape[1]
    x_out[...] = total[:, :ch]
    bc_out[...] = total[:, ch : ch + nbc]
    dt_out[...] = total[:, ch + nbc : ch + nbc + LANES].T[:heads]
    value = vector[...] + read_vector(came, vector.shape)
    first = place[2] == 0
    half = n1_out.shape[1]
    cq = xb_out.shape[1]
    n1_out[...] = value[5:6, :half]
    n2_out[...] = value[5:6, half : 2 * half]
    mine = jnp.where(first, value[0:8, :cq], value[0:8, cq : 2 * cq])
    xw_out[...] = mine[0:TAPS]
    xb_out[...] = mine[TAPS : TAPS + 1]
    bw_out[...] = value[1 : TAPS + 1, ch : ch + nbc]
    bb_out[...] = value[6:7, :nbc]
    hq = dtb_out.shape[1]
    for i, out in enumerate((dtb_out, alog_out, skip_out)):
        at = ch + i * LANES
        out[...] = jnp.where(
            first, value[0:1, at : at + hq], value[0:1, at + hq : at + 2 * hq]
        )


def close_kernel(own, part, came, n1b, gain, gbc, gbc_came, dn1_out, rows_out):
    tokens = part.shape[0]
    dn1 = (part[...] + came[...]) + n1b[...]
    dn1_out[...] = dn1
    rows_out[0:8, :] = token_sums(dn1 * gain[...] * own[...].astype(F32))
    rows_out[8:16, :] = gbc[tokens:] + gbc_came[tokens:]


def end_kernel(
    place, own, factor1, resid, dn1, gain, rows, rows_far, small, gain2, hidden_out, vector_out
):
    half = dn1.shape[1]
    quarter = half // 2
    hid = own[...].astype(F32)
    factor = factor1[:, :1]
    inner_sum = column(rows[0:8] + rows_far[0:8])[:, :1]
    value = dn1[...]
    change = resid[...] + factor * (value * gain[...]) - hid * (
        factor * factor * factor * inner_sum / (2 * half)
    )
    hidden_out[...] = jnp.where(place[0] == 0, change[:, :quarter], change[:, quarter:])
    shared = jnp.where(place[2] == 0, rows[8:16], rows_far[8:16])
    nbc = rows.shape[1]
    ch = small.shape[1]
    heads = 3 * LANES
    vector_out[...] = jnp.zeros_like(vector_out)
    vector_out[0 : TAPS + 1, 0:ch] = small[0 : TAPS + 1]
    vector_out[0:1, ch : ch + heads] = small[8 + TAPS : 9 + TAPS, 0:heads]
    vector_out[1 : TAPS + 1, ch : ch + nbc] = shared[0:TAPS]
    vector_out[5:6, 0:half] = jnp.sum(value * hid * factor, axis=0, keepdims=True)
    vector_out[5:6, half : 2 * half] = gain2[0:1]
    vector_out[6:7, 0:nbc] = shared[TAPS : TAPS + 1]


def stage_kernel(keep, came, send_out, keep_out):
    rows = keep_out.shape[0]
    total = keep[...] + came[...].astype(F32)
    send_out[...] = total[rows:].astype(BF16)
    keep_out[...] = total[:rows]


def last_kernel(keep, came, *outs):
    total = keep[...] + came[...].astype(F32)
    at = 0
    for out in outs:
        out[...] = total[:, at : at + out.shape[1]]
        at += out.shape[1]


def last_tall_kernel(keep, came, *outs):
    total = keep[...] + came[...].astype(F32)
    width = outs[0].shape[1]
    outs[0][...] = jnp.concatenate([total[:, :width], total[:, width : 2 * width]], axis=0)
    tall = jnp.concatenate([total[:, 2 * width : 3 * width], total[:, 3 * width :]], axis=0)
    size = outs[1].shape[0]
    outs[1][...] = tall[:size]
    outs[2][...] = tall[size:]


def halving_order(steps):
    order = [0]
    for step in reversed(steps):
        order = order + [o | step for o in order]
    return order


def halve(run, steps, at, send, keep, last, outs):
    while True:
        came = swap(send, "dp", steps[at])
        yield None
        at += 1
        if at == len(steps):
            break
        rows, cols = keep.shape
        send, keep = run(
            stage_kernel, [((rows // 2, cols), BF16), ((rows // 2, cols), F32)], keep, came
        )
    yield run(last, outs, keep, came)


def finish(steps):
    result = None
    while result is None:
        result = next(steps)
    return result


def shards(
    hidden,
    segment_ids,
    norm1_gain,
    w_gate,
    w_xin,
    w_dt,
    w_bc,
    w_query,
    w_kv,
    convx_weight,
    convx_bias,
    convbc_weight,
    convbc_bias,
    dt_bias,
    a_log,
    d_skip,
    w_mixout,
    w_attnout,
    norm2_gain,
    w_gateup,
    w_down,
    cotangent,
):
    row = lax.axis_index("row")
    col = lax.axis_index("col")
    me = lax.axis_index("dp")
    count = lax.axis_size("dp")
    spot = me & 3
    place = jnp.stack([col, spot, row]).astype(jnp.int32)
    tokens, quarter = hidden.shape
    half = 2 * quarter
    full_width = 4 * quarter
    piece = half // 4
    ch = w_xin.shape[1]
    nq = w_query.shape[1]
    nkv = w_kv.shape[2]
    nbc = w_bc.shape[1]
    heads = w_dt.shape[1]
    ff = w_down.shape[0]
    cq = convx_bias.shape[0]
    hq = dt_bias.shape[0]

    run = Chain()
    cols = ch + nbc + LANES + ch + nq + nkv
    inner = ch + nq

    near = [1 << b for b in range(count.bit_length() - 1)]
    turned = [near[1], near[0]] + near[2:]
    size = half // count
    within = jnp.asarray(np.tile(np.arange(size), count), jnp.int32)
    both_within = jnp.concatenate([within, within + size])

    def block_order(steps):
        return jnp.asarray(np.repeat(np.array(halving_order(steps)), size), jnp.int32) ^ me

    near_block = block_order(near)
    turned_both = jnp.concatenate([block_order(turned)] * 2)
    order_near = (near_block * size + within)[None]
    order_down = (turned_both * (ff // count) + both_within)[None]
    m_rows = ch // count
    a_rows = nq // count
    order_mix = jnp.where(
        both_within < m_rows,
        turned_both * m_rows + both_within,
        ch + turned_both * a_rows + both_within - m_rows,
    )[None]

    def padded(value):
        return jnp.pad(value, (0, LANES - hq))

    small = jnp.concatenate(
        [convx_weight.T.reshape(-1), convx_bias, norm2_gain, padded(dt_bias), padded(a_log), padded(d_skip)]
    )
    small_rows = 16 * pl.cdiv(small.shape[0] // LANES + 8, 16)
    small = jnp.pad(small, (0, small_rows * LANES - small.shape[0])).reshape(small_rows, LANES)
    gu_mine = lax.dynamic_slice_in_dim(w_gateup, spot * piece, piece, 0).reshape(piece, 2 * ff)
    hid_came = swap(hidden, "col")
    mine = run(
        pieces_kernel,
        [((inner + 3 * ff + 4 * tokens + small_rows, piece), BF16)],
        place, w_mixout, w_attnout, w_down, gu_mine, cotangent, hidden, small,
        smem=(0,),
    )[0]
    got = swap(mine, "row")
    gu = w_gateup.reshape(half, 2 * ff)
    wk = w_kv.reshape(half, nkv)
    wd = jnp.pad(w_dt, ((0, 0), (0, LANES - heads)))
    gain_one = norm1_gain.astype(F32)[None]
    own, part, part_low = run(
        project_kernel,
        [((tokens, half), BF16), ((tokens, cols), F32), ((tokens, cols), BF16)],
        place, hidden, hid_came, gain_one, w_xin, w_bc, wd, w_gate, w_query, wk,
        smem=(0,),
    )
    part_came = swap(part_low, "row")
    t_first, g_first, in_pair, x_par, head_par, gain_two = run(
        lambda *refs: split_kernel(heads, *refs),
        [
            ((inner + ff, piece), BF16),
            ((piece, 2 * ff), BF16),
            ((3 * tokens, quarter), BF16),
            ((8, ch), F32),
            ((8, LANES), F32),
            ((1, full_width), F32),
        ],
        place, got, cotangent, small,
        smem=(0,), after=(gu,),
    )
    t_second = swap(t_first, "dp", 1)
    g_second = swap(g_first, "dp", 2)
    t_third = swap(t_first, "dp", 2)
    g_third = swap(g_first, "dp", 1)
    in_came = swap(in_pair, "col")
    far, dy_own, dy_far, factor1, n1, left1 = run(
        norm_kernel,
        [
            ((tokens, half), BF16),
            ((tokens, half), BF16),
            ((tokens, half), BF16),
            ((tokens, LANES), F32),
            ((tokens, half), BF16),
            ((tokens, half), BF16),
        ],
        place, in_pair, in_came, own, gain_one, order_near,
        smem=(0,), scratch=[((tokens, half), BF16)], after=(t_second, g_second),
    )
    t_fourth = swap(t_second, "dp", 2)
    g_fourth = swap(g_second, "dp", 1)
    tall_fetch = (t_first, t_second, t_third, t_fourth)

    bc_par = jnp.concatenate(
        [convbc_weight.T, convbc_bias[None], jnp.zeros((3, nbc), BF16)], 0
    ).astype(F32)
    seg_row = segment_ids.astype(F32)
    seg_col = jnp.broadcast_to(segment_ids[0].astype(F32)[:, None], (tokens, LANES))

    mixed, raw, pre, ys = run(
        lambda *refs: mix_kernel(ch, nq, *refs),
        [
            ((tokens, inner), BF16),
            ((tokens, cols), F32),
            ((tokens, ch + nbc), F32),
            ((tokens, ch), F32),
        ],
        seg_row, seg_col, factor1, part, part_came, x_par, bc_par, head_par,
    )
    mix_part = run(
        out_kernel,
        [((tokens, full_width), F32)],
        mixed, w_mixout, w_attnout, *tall_fetch,
        after=(g_third, g_fourth),
    )[0]
    mix_came = swap(mix_part, "col")
    grad_act = run(
        lambda *refs: act_grad_kernel(inner, *refs),
        [((tokens, ff), F32)],
        dy_own, dy_far, w_down, *tall_fetch,
    )[0]
    h2, n2, act, ggu, n2_part, down_keep, down_send = run(
        feed_kernel,
        [
            ((tokens, full_width), F32),
            ((tokens, half), BF16),
            ((tokens, ff), BF16),
            ((tokens, 2 * ff), BF16),
            ((tokens, full_width), F32),
            ((tokens, quarter), F32),
            ((tokens, quarter), F32),
        ],
        place, own, far, mix_part, mix_came, gain_two,
        gu, g_first, g_third, g_second, g_fourth, grad_act, w_down,
        smem=(0,),
    )
    n2_came = swap(n2_part, "col")
    down_came = swap(down_send, "col")
    rows = half // 2

    g_send, d_send, g_left, d_left = run(
        feed_grad_kernel,
        [
            ((rows, 2 * ff), BF16),
            ((rows, 2 * half), BF16),
            ((tokens, rows), BF16),
            ((tokens, half), BF16),
        ],
        n2, act, ggu, dy_own, order_near, order_down,
    )
    g_came = swap(g_send, "dp", near[0])
    d_came = swap(d_send, "dp", turned[0])
    dym, resid, low, gain2_sum, output, m_send, m_left, g_two, two_send = run(
        lambda *refs: turn_kernel(ch, nq, *refs),
        [
            ((tokens, inner), F32),
            ((tokens, half), F32),
            ((tokens, half), BF16),
            ((8, half), F32),
            ((tokens, quarter), BF16),
            ((rows, 2 * half), BF16),
            ((tokens, half), BF16),
            ((tokens, ch + nq + nkv), BF16),
            ((rows, ch + nq + nkv), BF16),
        ],
        place, dy_own, dy_far, h2, n2_part, n2_came, gain_two,
        w_mixout, w_attnout, *tall_fetch, down_keep, down_came,
        mixed, order_mix, seg_row, seg_col, raw, pre, ys, x_par, left1,
        smem=(0,),
    )
    two_came = swap(two_send, "dp", near[0])
    m_came = swap(m_send, "dp", turned[0])
    gx, gdt, gbc, small_sum = run(
        lambda *refs: unmix_one_kernel(ch, nq, *refs),
        [
            ((tokens, ch), BF16),
            ((tokens, LANES), BF16),
            ((tokens + 8, nbc), F32),
            ((16, ch), F32),
        ],
        seg_row, seg_col, raw, pre, ys, dym, x_par, bc_par, head_par,
        scratch=[((tokens, ch), F32), ((tokens, ch), F32), ((tokens, tokens), F32)],
    )
    gbc_came = swap(gbc, "col")

    def quarters(width):
        return [((rows // 2, width), BF16), ((rows // 2, width), F32)]

    g_send, g_keep = run(wide_kernel, quarters(2 * ff), g_left, ggu, g_came)
    s_gu = halve(run, near, 1, g_send, g_keep, last_kernel, [((size, 2 * ff), F32)])
    next(s_gu)
    n1_part, n1_bc, gbc_both, one_send = run(
        back_kernel,
        [
            ((tokens, half), F32),
            ((tokens, half), F32),
            ((tokens, nbc), BF16),
            ((rows, ch + nbc + LANES), BF16),
        ],
        g_two, gx, gdt, gbc, gbc_came, w_xin, w_bc, wd, w_gate, w_query, wk, left1,
    )
    one_came = swap(one_send, "dp", near[0])
    n1_came = swap(n1_part, "col")
    def one_outs(keep):
        width = ch + nbc + LANES
        return [((keep + 16, width), BF16), ((keep, width), F32), ((8, ch + nbc + LANES), F32)]

    tall_send, tall_keep = run(
        tall_kernel, quarters(4 * half), d_left, dy_own, d_came, m_left, low, m_came
    )
    s_tall = halve(
        run, turned, 1, tall_send, tall_keep, last_tall_kernel,
        [((2 * size, half), F32), ((m_rows, half), F32), ((a_rows, half), F32)],
    )
    next(s_tall)
    two_send, two_keep = run(wide_kernel, quarters(ch + nq + nkv), left1, g_two, two_came)
    s_two = halve(
        run, near, 1, two_send, two_keep, last_kernel,
        [((size, ch), F32), ((size, nq), F32), ((size, nkv), F32)],
    )
    next(s_two)
    next(s_gu)
    dn1, sum_rows = run(
        close_kernel,
        [((tokens, half), F32), ((16, tokens), F32)],
        own, n1_part, n1_came, n1_bc, gain_one, gbc, gbc_came,
    )
    rows_far = swap(sum_rows, "row")
    next(s_two)
    grad_hidden, vector = run(
        end_kernel,
        [((tokens, quarter), F32), ((8, ch + nbc + LANES), F32)],
        place, own, factor1, resid, dn1, gain_one, sum_rows, rows_far, small_sum, gain2_sum,
        smem=(0,),
    )
    vector_came = swap(vector, "dp", near[0])
    r_gu = finish(s_gu)
    one_send, one_keep, vector = run(
        one_kernel, one_outs(rows // 2),
        left1, gx, gbc_both, gdt, one_came, vector, vector_came,
    )
    next(s_tall)
    r_two = finish(s_two)
    for step in near[1:-1]:
        one_came = swap(one_send, "dp", step)
        one_send, one_keep, vector = run(
            one_stage_kernel, one_outs(one_keep.shape[0] // 2), one_keep, one_came, vector
        )
    one_came = swap(one_send, "dp", near[-1])
    r_tall = finish(s_tall)
    (
        r_xin, r_bc, r_dt, o_norm1, o_norm2, o_cxw, o_cxb, o_cbw, o_cbb, o_dtb, o_alog, o_dsk
    ) = run(
        lambda *refs: one_last_kernel(heads, *refs),
        [
            ((size, ch), F32),
            ((size, nbc), F32),
            ((heads, size), F32),
            ((1, half), F32),
            ((1, half), F32),
            ((TAPS, cq), F32),
            ((1, cq), F32),
            ((TAPS, nbc), F32),
            ((1, nbc), F32),
            ((1, hq), F32),
            ((1, hq), F32),
            ((1, hq), F32),
        ],
        place, one_keep, one_came, vector,
        smem=(0,),
    )
    r_gate, r_query, r_kv = r_two
    r_down, r_mixout, r_attnout = r_tall
    return (
        output,
        grad_hidden,
        o_norm1[0],
        r_gate,
        r_xin,
        r_dt.T,
        r_bc,
        r_query,
        r_kv.reshape(size, 1, nkv),
        o_cxw.T,
        o_cxb[0],
        o_cbw.T,
        o_cbb[0],
        o_dtb[0],
        o_alog[0],
        o_dsk[0],
        r_mixout,
        r_attnout,
        o_norm2[0],
        r_gu[0].reshape(size, 2, ff),
        r_down,
    )


def solution(mesh):
    placed = (
        P("dp", ("row", "col")),
        P("dp", None),
        P("row"),
        P("row", "col"),
        P("row", "col"),
        P("row", "col"),
        P("row", None),
        P("row", "col"),
        P("row", "col", None),
        P(("col", "row"), None),
        P(("col", "row")),
        P(),
        P(),
        P(("col", "row")),
        P(("col", "row")),
        P(("col", "row")),
        P("col", "row"),
        P("col", "row"),
        P("row"),
        P("row", None, "col"),
        P("col", "row"),
        P("dp", ("row", "col")),
    )
    return jax.shard_map(
        shards,
        mesh=mesh,
        in_specs=placed,
        out_specs=(
            P("dp", ("row", "col")),
            P("dp", ("row", "col")),
            P("row"),
            P(("row", "dp"), "col"),
            P(("row", "dp"), "col"),
            P(("row", "dp"), "col"),
            P(("row", "dp"), None),
            P(("row", "dp"), "col"),
            P(("row", "dp"), "col", None),
            P(("col", "row"), None),
            P(("col", "row")),
            P(),
            P(),
            P(("col", "row")),
            P(("col", "row")),
            P(("col", "row")),
            P(("col", "dp"), "row"),
            P(("col", "dp"), "row"),
            P("row"),
            P(("row", "dp"), None, "col"),
            P(("col", "dp"), "row"),
        ),
        check_vma=False,
    )
```
